128 devices in a mesh: seq: 16 (over y, x_hi, core), head: 8 (over x_lo, z).
Axes of the slice: x: 4 (x_hi: 2, x_lo: 2; x = x_hi * 2 + x_lo), y: 4, z: 4, core: 2. Of those that a mesh axis runs over, the one named last changes fastest.
Arguments:
- hidden: bfloat16 [2048, 8192], P('head', 'seq'), may hold values from -6 to 6
- cross_query: bfloat16 [2048, 8192], P('seq', 'head'), may hold values from -128 to 128
- image_cache: bfloat16 [16, 1600, 2048], P('seq', None, 'head'), may hold values from -48 to 48
- features: bfloat16 [16, 1600, 8192], P('seq', None, 'head'), may hold values from -6 to 6
- image_proj: bfloat16 [8192, 2048], P('head'), may hold values from -0.5 to 0.5
- key_gain: float32 [128], replicated, may hold values from 0.1 to 1.9
- out_weight: bfloat16 [8192, 8192], P('head', 'seq'), may hold values from -0.0625 to 0.0625
- cross_gate: float32 [1], replicated, may hold values from 0.5 to 1.5
- image_spans: int32 [2048, 2], replicated, may hold values from 0 to 16, as said below
- evicted: int32 [2], replicated, may hold values from 0 to 15, as said below
- placement: int32 [16], replicated, may hold values from 0 to 15, as said below
Outputs:
- layer_output: bfloat16 [2048, 8192], P('head', 'seq')
The draws below stay inside these ranges and needn't reach their ends.
Inputs may be any that keep to these rules, and one draw needn't show every extreme that they name: `image_spans`: row t holds the first image that token t sees and one past the last; the first is below the last, the last is at least 8, and the last never decreases as t grows. `evicted`: 2 distinct image ids. `placement`: each image id appears in exactly one slot.
All inputs are finite; a program needn't handle non-finite values.
Results may differ from the reference program's by a relative error of at most 0.038.
Values may be sent and summed in bfloat16 or wider, within the bound.
No kernel may reach another device: no remote copies, remote signals or barrier semaphores. Data moves between devices by JAX's collectives and lax.ppermute only.
A program may use at most 128 MiB of HBM per device.

```python
import jax
import jax.numpy as jnp
from jax import lax

D = 8192
HQ = 64
KVH = 8
HD = 128
PATCHES = 1600
EVICT = 2
TEXT_LEN = 2048
IMAGES = 16
N_HEAD = 8


def layout(key):
    placement = jax.random.permutation(jax.random.fold_in(key, 11), IMAGES).astype(jnp.int32)
    evicted = jax.random.permutation(jax.random.fold_in(key, 12), IMAGES)[:EVICT].astype(jnp.int32)
    cuts = jnp.sort(jax.random.randint(jax.random.fold_in(key, 13), (IMAGES - IMAGES // 2,), 0, TEXT_LEN))
    row_ids = jnp.arange(TEXT_LEN, dtype=jnp.int32)
    stop_image = (IMAGES // 2 + jnp.sum((cuts[None, :] <= row_ids[:, None]).astype(jnp.int32), axis=1)).astype(jnp.int32)
    first_image = jax.random.randint(jax.random.fold_in(key, 14), (TEXT_LEN,), 0, stop_image).astype(jnp.int32)
    return (placement, evicted, first_image, stop_image)


def kv_rows(key, count):
    key_cols = jax.random.truncated_normal(jax.random.fold_in(key, 1), -6.0, 6.0, (count, KVH, 1, HD), jnp.float32)
    value_cols = 8.0 * jax.random.truncated_normal(jax.random.fold_in(key, 2), -6.0, 6.0, (count, KVH, 1, HD), jnp.float32)
    return jnp.concatenate([key_cols, value_cols], axis=2)


def image_leading(key):
    leading = kv_rows(jax.random.fold_in(key, 51), IMAGES * 2).reshape(IMAGES, 2, KVH, 2, HD)
    return leading


def draw_image_cache(key, part):
    leading = image_leading(key)
    remaining = kv_rows(jax.random.fold_in(key, 52), IMAGES * (PATCHES - 2)).reshape(IMAGES, PATCHES - 2, KVH, 2, HD)
    return jnp.concatenate([leading, remaining], axis=1).reshape(IMAGES, PATCHES, 2 * KVH * HD).astype(jnp.bfloat16)


def draw_cross_query(key, part):
    baseline = 2.0 * jax.random.truncated_normal(jax.random.fold_in(key, 42), -6.0, 6.0, (TEXT_LEN, HQ * HD), jnp.float32)
    return baseline.astype(jnp.bfloat16)


def draw_image_spans(key, part):
    placement, evicted, first_image, stop_image = layout(key)
    return jnp.stack([first_image, stop_image], axis=1).astype(jnp.int32)


def draw_evicted(key, part):
    return layout(key)[1]


def draw_placement(key, part):
    return layout(key)[0]


def block_scale(rng, extent, shards, low, largest):
    loudness, own = 1.0, jax.random.fold_in(rng, 6)
    for axis_at, parts in shards:
        heights = jnp.exp(jax.random.uniform(jax.random.fold_in(own, axis_at), (parts,), jnp.float32, low / len(shards), largest / len(shards)))
        loudness = loudness * jnp.repeat(heights, extent[axis_at] // parts).reshape([-1 if axis == axis_at else 1 for axis in range(len(extent))])
    return loudness


def normal_values(stream_key, dims, deviation, most, cuts=(), kind=jnp.bfloat16):
    factor_of = block_scale(stream_key, dims, cuts, -0.22, 0.18) if cuts else 1.0
    result = jax.random.normal(stream_key, dims, jnp.float32) * deviation * factor_of
    return jnp.minimum(jnp.maximum(result, -most), most).astype(kind)


def setup_inputs(seed: int = 0) -> dict:
    seeds = jax.random.split(jax.random.key(seed), 12)
    hidden = normal_values(seeds[0], (TEXT_LEN, D), 1.0, 6.0, ((0, 8), (1, 16)))
    cross_query = draw_cross_query(jax.random.fold_in(seeds[11], 71), 0)
    image_cache = draw_image_cache(jax.random.fold_in(seeds[11], 71), 0)
    features = normal_values(seeds[3], (IMAGES, PATCHES, D), 1.0, 6.0, ((0, 16), (2, 8)))
    image_proj = normal_values(seeds[4], (D, 2 * KVH * HD), (D // 64) ** -0.5, 0.5, ((0, 8),))
    key_gain = jnp.clip(1.0 + 0.18 * jax.random.normal(seeds[5], (HD,), jnp.float32), 0.1, 1.9)
    out_weight = normal_values(seeds[6], (HQ * HD, D), (HQ * HD) ** -0.5, 0.0625, ((0, 8), (1, 16)))
    cross_gate = jnp.clip(jax.random.uniform(seeds[7], (1,), jnp.float32, 0.5, 1.5), 0.5, 1.5)
    image_spans = draw_image_spans(jax.random.fold_in(seeds[11], 71), 0)
    evicted = draw_evicted(jax.random.fold_in(seeds[11], 71), 0)
    placement = draw_placement(jax.random.fold_in(seeds[11], 71), 0)
    return {"hidden": hidden, "cross_query": cross_query, "image_cache": image_cache, "features": features, "image_proj": image_proj, "key_gain": key_gain, "out_weight": out_weight, "cross_gate": cross_gate, "image_spans": image_spans, "evicted": evicted, "placement": placement}


MASKED_SCORE = -1e+30

def attend_head(queries, key_cols, value_cols, allowed):
    scores = jnp.dot(queries, key_cols.T, preferred_element_type=jnp.float32) * HD ** (-0.5)
    scores = jnp.where(allowed, scores, MASKED_SCORE)
    highest = lax.optimization_barrier(jnp.max(scores, axis=-1, keepdims=True))
    weights = jnp.where(allowed, jnp.exp(scores - highest), 0.0)
    weight_sum = lax.optimization_barrier(jnp.sum(weights, axis=-1, keepdims=True))
    mixed_values = jnp.dot(weights.astype(jnp.bfloat16), value_cols, preferred_element_type=jnp.float32)
    return mixed_values / weight_sum

def attend_all(queries, key_values, allowed):
    per_group = HQ // KVH

    def one_head(head_index):
        group = head_index // per_group
        head_query = lax.dynamic_slice_in_dim(queries, (head_index * HD).astype(jnp.int32), HD, 1)
        key_cols = lax.dynamic_slice_in_dim(key_values, (group * 2 * HD).astype(jnp.int32), HD, 1)
        value_cols = lax.dynamic_slice_in_dim(key_values, (group * 2 * HD + HD).astype(jnp.int32), HD, 1)
        return attend_head(head_query, key_cols, value_cols, allowed)
    stacked = lax.map(one_head, jnp.arange(HQ, dtype=jnp.int32))
    return jnp.transpose(stacked, (1, 0, 2)).reshape(queries.shape[0], HQ * HD)

def normalize(raw_sums, key_gain):
    grouped = raw_sums.reshape(raw_sums.shape[0], KVH, 2, HD)
    key_cols = grouped[:, :, 0, :]
    inverse = lax.rsqrt(lax.optimization_barrier(jnp.mean(key_cols * key_cols, axis=-1, keepdims=True)) + 1e-05)
    key_cols = key_cols * inverse * key_gain
    return jnp.stack([key_cols, grouped[:, :, 1, :]], axis=2).reshape(raw_sums.shape[0], 2 * KVH * HD).astype(jnp.bfloat16)

def rebuild(features, image_proj, key_gain, holder):
    own_rows = lax.dynamic_index_in_dim(features, holder, 0, keepdims=False)
    block_cols = D // N_HEAD
    raw_sums = jnp.zeros((PATCHES, 2 * KVH * HD), jnp.float32)
    for block in range(N_HEAD):
        product = jnp.dot(own_rows[:, block * block_cols:(block + 1) * block_cols], image_proj[block * block_cols:(block + 1) * block_cols], preferred_element_type=jnp.float32)
        rounded = lax.optimization_barrier(product.astype(jnp.bfloat16))
        raw_sums = raw_sums + rounded.astype(jnp.float32)
    return normalize(raw_sums, key_gain)

def reference(hidden, cross_query, image_cache, features, image_proj, key_gain, out_weight, cross_gate, image_spans, evicted, placement):
    image_keys = image_cache
    for evict_index in range(EVICT):
        holder = jnp.argmax(placement == evicted[evict_index]).astype(jnp.int32)
        rebuilt = rebuild(features, image_proj, key_gain, holder)
        image_keys = lax.dynamic_update_slice_in_dim(image_keys, rebuilt[None], holder, 0)
    key_labels = jnp.repeat(placement, PATCHES)
    seen = (key_labels[None, :] >= image_spans[:, 0:1]) & (key_labels[None, :] < image_spans[:, 1:2])
    cross_context = attend_all(cross_query, image_keys.reshape(IMAGES * PATCHES, 2 * KVH * HD), seen).astype(jnp.bfloat16)
    projected = jnp.dot(cross_context, out_weight, preferred_element_type=jnp.float32)
    layer_output = (hidden.astype(jnp.float32) + jnp.tanh(cross_gate[0]) * projected).astype(jnp.bfloat16)
    return layer_output
```

```python
import functools
import math

import jax
import jax.numpy as jnp
from jax import lax
from jax.experimental import pallas as pl
from jax.experimental.pallas import tpu as pltpu
from jax.sharding import PartitionSpec as P

MASKED_SCORE = -1e30


def in_blocks(x, dim, peers):
    dims = x.shape
    blocks = x.reshape(*dims[:dim], peers, dims[dim] // peers, *dims[dim + 1 :])
    return jnp.moveaxis(blocks, dim, 0)


def sum_at_owner(x, axis, dim):
    blocks = in_blocks(x, dim, lax.axis_size(axis))
    arrived = lax.all_to_all(blocks, axis, split_axis=0, concat_axis=0, tiled=True)
    return arrived.astype(jnp.float32).sum(axis=0)


def attend_kernel(head_size, heads, ids_ref, q_ref, first_ref, stop_ref, kv_ref, out_ref, m_ref, l_ref, acc_ref):
    step = pl.program_id(0)
    tokens = q_ref.shape[0]
    factor = math.log2(math.e) * head_size ** (-0.5)

    @pl.when(step == 0)
    def _():
        m_ref[...] = jnp.full_like(m_ref, MASKED_SCORE)
        l_ref[...] = jnp.zeros_like(l_ref)
        acc_ref[...] = jnp.zeros_like(acc_ref)

    image = ids_ref[step]
    keys = kv_ref[0, :, :head_size]
    values = kv_ref[0, :, head_size:]
    seen = (first_ref[...] <= image) & (image < stop_ref[...])
    for pair in range(heads // 2):
        rows = pl.ds(pair * 2 * tokens, 2 * tokens)
        cols = pair * 2 * head_size
        queries = jnp.concatenate(
            [q_ref[:, cols : cols + head_size], q_ref[:, cols + head_size : cols + 2 * head_size]], axis=0
        )
        scores = lax.dot_general(queries, keys, (((1,), (1,)), ((), ())), preferred_element_type=jnp.float32)
        here = jnp.max(scores, axis=1, keepdims=True)
        weights = jnp.exp2((scores - here) * factor)
        total = jnp.sum(weights, axis=1, keepdims=True)
        mixed = jnp.dot(weights.astype(jnp.bfloat16), values, preferred_element_type=jnp.float32)
        before = m_ref[rows, :]
        after = jnp.where(seen, jnp.maximum(before, here), before)
        keep = jnp.exp2((before - after) * factor)
        add = jnp.where(seen, jnp.exp2((here - after) * factor), 0.0)
        m_ref[rows, :] = after
        l_ref[rows, :] = l_ref[rows, :] * keep + add * total
        acc_ref[rows, :] = acc_ref[rows, :] * keep + add * mixed

    @pl.when(step == pl.num_programs(0) - 1)
    def _():
        for head in range(heads):
            rows = pl.ds(head * tokens, tokens)
            out_ref[:, head * head_size : (head + 1) * head_size] = (acc_ref[rows, :] / l_ref[rows, :]).astype(
                out_ref.dtype
            )


def attend(queries, key_values, ids, first, stop, head_size):
    tokens, cols = queries.shape
    heads = cols // head_size
    slots, rows, kv_cols = key_values.shape
    pair = lambda x: jnp.concatenate([x, x])[:, None]
    whole = lambda shape: pl.BlockSpec(shape, lambda i, ids: (0,) * len(shape))
    return pl.pallas_call(
        functools.partial(attend_kernel, head_size, heads),
        grid_spec=pltpu.PrefetchScalarGridSpec(
            num_scalar_prefetch=1,
            grid=(slots,),
            in_specs=[
                whole((tokens, cols)),
                whole((2 * tokens, 1)),
                whole((2 * tokens, 1)),
                pl.BlockSpec((1, rows, kv_cols), lambda i, ids: (i, 0, 0)),
            ],
            out_specs=whole((tokens, cols)),
            scratch_shapes=[
                pltpu.VMEM((heads * tokens, 1), jnp.float32),
                pltpu.VMEM((heads * tokens, 1), jnp.float32),
                pltpu.VMEM((heads * tokens, head_size), jnp.float32),
            ],
        ),
        out_shape=jax.ShapeDtypeStruct((tokens, cols), jnp.bfloat16),
        compiler_params=pltpu.CompilerParams(vmem_limit_bytes=40 * 1024 * 1024),
        name="attend",
    )(ids, queries, pair(first), pair(stop), key_values)


def on_device(
    hidden,
    cross_query,
    image_cache,
    features,
    image_proj,
    key_gain,
    out_weight,
    cross_gate,
    image_spans,
    evicted,
    placement,
):
    head_size = key_gain.shape[0]
    tok_rows = cross_query.shape[0]
    seq_pos = lax.axis_index("seq")
    patches = features.shape[1]
    own_image = lax.dynamic_index_in_dim(placement, seq_pos, 0, keepdims=False)
    evicted_here = jnp.any(evicted == own_image)
    own_rows = features[0]
    partial_value = lax.cond(
        evicted_here,
        lambda: jnp.dot(own_rows, image_proj, preferred_element_type=jnp.float32).astype(jnp.bfloat16),
        lambda: jnp.zeros((patches, image_proj.shape[1]), jnp.bfloat16),
    )
    summed = lax.psum_scatter(partial_value, "head", scatter_dimension=1, tiled=True).astype(jnp.float32)
    key_cols = summed[:, :head_size]
    inverse = lax.rsqrt(jnp.mean(key_cols * key_cols, axis=-1, keepdims=True) + 1e-05)
    key_cols = key_cols * inverse * key_gain
    rebuilt = jnp.concatenate([key_cols, summed[:, head_size:]], axis=1).astype(jnp.bfloat16)
    slot_kv = jnp.where(evicted_here, rebuilt, image_cache[0])
    own_spans = lax.dynamic_slice_in_dim(image_spans, seq_pos * tok_rows, tok_rows)
    key_values = lax.all_gather(slot_kv, "seq", axis=0)
    cross_context = attend(cross_query, key_values, placement, own_spans[:, 0], own_spans[:, 1], head_size)
    partial_out = jnp.dot(
        lax.all_gather(cross_context, "seq", axis=0, tiled=True),
        out_weight,
        preferred_element_type=jnp.float32,
    )
    summed_out = sum_at_owner(partial_out.astype(jnp.bfloat16), "head", 0)
    layer_output = (hidden.astype(jnp.float32) + jnp.tanh(cross_gate[0]) * summed_out).astype(jnp.bfloat16)
    return layer_output


def solution(mesh):
    placed = (
        P("head", "seq"),
        P("seq", "head"),
        P("seq", None, "head"),
        P("seq", None, "head"),
        P("head", None),
        P(),
        P("head", "seq"),
        P(),
        P(),
        P(),
        P(),
    )
    return jax.shard_map(
        on_device, mesh=mesh, in_specs=placed, out_specs=P("head", "seq"), check_vma=False
    )
```

```python
import functools
import math

import jax
import jax.numpy as jnp
from jax import lax
from jax.experimental import pallas as pl
from jax.experimental.pallas import tpu as pltpu
from jax.sharding import PartitionSpec as P

MASKED_SCORE = -1e30
CHUNK = 32
LIST = 18
VMEM = pltpu.CompilerParams(vmem_limit_bytes=48 * 1024 * 1024)


def seq_at(y, x, core):
    return (y % 4) * 4 + (x % 2) * 2 + core % 2


def head_at(x, z):
    return (x % 2) * 4 + z % 4


def send_seq(array, y=0, x=0, core=0):
    pairs = [
        (seq_at(a, b, c), seq_at(a + y, b + x, c + core)) for a in range(4) for b in range(2) for c in range(2)
    ]
    return lax.ppermute(array, "seq", pairs)


def send_head(array, x=0, z=0):
    return lax.ppermute(array, "head", [(head_at(a, b), head_at(a + x, b + z)) for a in range(2) for b in range(4)])


def add(*terms):
    return sum(term.astype(jnp.float32) for term in terms).astype(jnp.bfloat16)


def sum_over_head(parts):
    p00, p01, p10, p11, p20, p21, p30, p31 = parts
    via_x = send_head(p21, x=1)
    down = send_head(p31, z=-1)
    across = send_head(p11, x=1)
    p20 = add(p20, via_x)
    last = send_head(p30, z=-1)
    up = send_head(p20, z=1)
    p01 = add(p01, down)
    p10 = add(p10, across, up)
    side = send_head(p01, x=1)
    ahead = send_head(p10, z=1)
    return sum(term.astype(jnp.float32) for term in (p00, last, side, ahead))


def gather_chips(block):
    r30 = send_seq(block, y=1)
    r01 = send_seq(block, x=1)
    r10 = send_seq(block, y=-1)
    r20 = send_seq(r30, y=1)
    r31 = send_seq(r30, x=1)
    r11 = send_seq(r01, y=-1)
    r21 = send_seq(r20, x=1)
    return block, r01, r10, r11, r20, r21, r30, r31


def rebuild_kernel(order_ref, rows_ref, proj_ref, *out_refs):
    product = jnp.dot(rows_ref[...], proj_ref[...], preferred_element_type=jnp.float32).astype(jnp.bfloat16)
    for at, out_ref in enumerate(out_refs):

        @pl.when(pl.program_id(0) == at)
        def _():
            out_ref[...] = product


def rebuild_parts(rows, proj, order):
    count, depth = rows.shape
    cols = proj.shape[1] // 8
    return pl.pallas_call(
        rebuild_kernel,
        grid_spec=pltpu.PrefetchScalarGridSpec(
            num_scalar_prefetch=1,
            grid=(8,),
            in_specs=[
                pl.BlockSpec((count, depth), lambda i, order: (0, 0)),
                pl.BlockSpec((depth, cols), lambda i, order: (0, order[i])),
            ],
            out_specs=[pl.BlockSpec((count, cols), lambda i, order: (0, 0))] * 8,
        ),
        out_shape=[jax.ShapeDtypeStruct((count, cols), jnp.bfloat16)] * 8,
        compiler_params=VMEM,
        name="rebuild_parts",
    )(order, rows, proj)


def project_kernel(order_ref, core_ref, own_ref, other_ref, weight_ref, *out_refs):
    tokens = own_ref.shape[1]
    core = core_ref[0]
    own = jnp.dot(own_ref[0], weight_ref[...], preferred_element_type=jnp.float32).astype(jnp.bfloat16)
    other = jnp.dot(other_ref[0], weight_ref[...], preferred_element_type=jnp.float32).astype(jnp.bfloat16)
    for at, out_ref in enumerate(out_refs):

        @pl.when(pl.program_id(0) == at)
        def _():
            out_ref[pl.ds(pl.multiple_of(core * tokens, tokens), tokens), :] = own
            out_ref[pl.ds(pl.multiple_of((1 - core) * tokens, tokens), tokens), :] = other


def project_parts(own, other, weight, order, core):
    _, tokens, depth = own.shape
    cols = weight.shape[1]
    block = pl.BlockSpec((1, tokens, depth), lambda i, order, core: (order[i], 0, 0))
    return pl.pallas_call(
        project_kernel,
        grid_spec=pltpu.PrefetchScalarGridSpec(
            num_scalar_prefetch=2,
            grid=(8,),
            in_specs=[block, block, pl.BlockSpec((depth, cols), lambda i, order, core: (0, 0))],
            out_specs=[pl.BlockSpec((2 * tokens, cols), lambda i, order, core: (0, 0))] * 8,
        ),
        out_shape=[jax.ShapeDtypeStruct((2 * tokens, cols), jnp.bfloat16)] * 8,
        compiler_params=VMEM,
        name="project_parts",
    )(order, core, own, other, weight)


def sweep(head_size, ids_ref, count_ref, list_ref, q_ref, first_ref, stop_ref, kv_parts, m_ref, l_ref, acc_ref, even, odd):
    factor = math.log2(math.e) * head_size ** (-0.5)
    heads = q_ref.shape[1] // CHUNK

    for slot, (keys_of, values_of) in enumerate(kv_parts):
        count = count_ref[slot]

        def score(place, into):
            into[...] = lax.dot_general(
                q_ref[list_ref[slot * LIST + place]],
                keys_of(),
                (((1,), (1,)), ((), ())),
                preferred_element_type=jnp.float32,
            )

        def take(place, scores_ref):
            chunk = list_ref[slot * LIST + place]
            image = jnp.where(place < count, ids_ref[slot], -1)
            scores = scores_ref[...]
            here = jnp.max(scores, axis=1, keepdims=True)
            weights = jnp.exp2((scores - here) * factor)
            total = jnp.sum(weights, axis=1, keepdims=True)
            mixed = jnp.dot(weights.astype(jnp.bfloat16), values_of(), preferred_element_type=jnp.float32)
            tokens = pl.ds(pl.multiple_of(chunk * CHUNK, CHUNK), CHUNK)
            seen = (first_ref[tokens, :] <= image) & (image < stop_ref[tokens, :])
            seen = jnp.concatenate([seen.astype(jnp.int32)] * heads, axis=0) > 0
            before = m_ref[chunk]
            after = jnp.where(seen, jnp.maximum(before, here), before)
            keep = jnp.exp2((before - after) * factor)
            gain = jnp.where(seen, jnp.exp2((here - after) * factor), 0.0)
            m_ref[chunk] = after
            l_ref[chunk] = l_ref[chunk] * keep + gain * total
            acc_ref[chunk] = acc_ref[chunk] * keep + gain * mixed

        @pl.when(count > 0)
        def _():
            score(0, even)

            def body(at, carry):
                place = 2 * at
                score(place + 1, odd)
                take(place, even)
                score(place + 2, even)
                take(place + 1, odd)
                return carry

            lax.fori_loop(0, (count + 1) // 2, body, 0)


def held_kernel(head_size, ids, count, lists, q0, q1, q2, q3, order, first, stop, a, b, c, d, qs, m, l, acc, even, odd):
    heads = q0.shape[1] // head_size
    per_block = q0.shape[0] // CHUNK
    for block, q_ref in enumerate((q0, q1, q2, q3)):
        ordered = jnp.dot(order[block], q_ref[...], preferred_element_type=jnp.float32).astype(jnp.bfloat16)
        for part in range(per_block):
            for head in range(heads):
                qs[block * per_block + part, head * CHUNK : (head + 1) * CHUNK, :] = ordered[
                    part * CHUNK : (part + 1) * CHUNK, head * head_size : (head + 1) * head_size
                ]
    m[...] = jnp.full_like(m, MASKED_SCORE)
    l[...] = jnp.zeros_like(l)
    acc[...] = jnp.zeros_like(acc)
    kv_parts = [(lambda r=r: r[:, :head_size], lambda r=r: r[:, head_size:]) for r in (a, b, c, d)]
    sweep(head_size, ids, count, lists, qs, first, stop, kv_parts, m, l, acc, even, odd)


def rebuilt_kernel(
    head_size, ids, count, lists, qs, order, first, stop, m_in, l_in, acc_in, a, b, c, d, o0, o1, o2, o3, m, l, acc, even, odd
):
    factor = math.log2(math.e) * head_size ** (-0.5)
    tokens = o0.shape[0]
    heads = qs.shape[1] // CHUNK
    per_block = tokens // CHUNK
    m[...] = m_in[...]
    l[...] = l_in[...]
    acc[...] = acc_in[...]
    kv_parts = [
        (lambda r=r, i=i: r[i, :, :head_size], lambda r=r, i=i: r[i, :, head_size:])
        for r in (a, b, c, d)
        for i in range(2)
    ]
    sweep(head_size, ids, count, lists, qs, first, stop, kv_parts, m, l, acc, even, odd)
    lanes = lax.broadcasted_iota(jnp.int32, (tokens, 128), 1)
    for block, out in enumerate((o0, o1, o2, o3)):
        extra = jnp.zeros((tokens, 128), jnp.float32)
        for head in range(heads):
            rows = slice(head * CHUNK, (head + 1) * CHUNK)
            chunks = range(block * per_block, (block + 1) * per_block)
            high = jnp.concatenate([m[chunk, rows, :] for chunk in chunks], axis=0)
            total = jnp.concatenate([l[chunk, rows, :] for chunk in chunks], axis=0)
            mixed = jnp.concatenate([acc[chunk, rows, :] for chunk in chunks], axis=0)
            some = total > 0.0
            safe = jnp.where(some, total, 1.0)
            level = jnp.where(some, high * factor + jnp.log2(safe), MASKED_SCORE)
            ordered = (mixed / safe).astype(jnp.bfloat16)
            out[:, head * head_size : (head + 1) * head_size] = lax.dot_general(
                order[block], ordered, (((0,), (0,)), ((), ())), preferred_element_type=jnp.float32
            ).astype(jnp.bfloat16)
            for piece in range(3):
                rounded = level.astype(jnp.bfloat16).astype(jnp.float32)
                extra = jnp.where(lanes == piece * heads + head, rounded, extra)
                level = level - rounded
        out[:, heads * head_size :] = lax.dot_general(
            order[block], extra.astype(jnp.bfloat16), (((0,), (0,)), ((), ())), preferred_element_type=jnp.float32
        ).astype(jnp.bfloat16)


def merge_kernel(head_size, a, b, c, d, out):
    heads = out.shape[1] // head_size
    parts = (a, b, c, d)
    extras = [part[:, heads * head_size :].astype(jnp.float32) for part in parts]
    for head in range(heads):
        cols = slice(head * head_size, (head + 1) * head_size)
        levels = [sum(e[:, p * heads + head : p * heads + head + 1] for p in range(3)) for e in extras]
        top = functools.reduce(jnp.maximum, levels)
        shares = [jnp.exp2(level - top) for level in levels]
        mixed = sum(share * part[:, cols].astype(jnp.float32) for share, part in zip(shares, parts))
        out[:, cols] = (mixed / sum(shares)).astype(jnp.bfloat16)


def normalize(summed, key_gain):
    head_size = key_gain.shape[0]
    key_cols = summed[:, :head_size]
    inverse = lax.rsqrt(jnp.mean(key_cols * key_cols, axis=-1, keepdims=True) + 1e-05)
    return jnp.concatenate([key_cols * inverse * key_gain, summed[:, head_size:]], axis=1).astype(jnp.bfloat16)


def on_device(
    hidden,
    cross_query,
    image_cache,
    features,
    image_proj,
    key_gain,
    out_weight,
    cross_gate,
    image_spans,
    evicted,
    placement,
):
    head_size = key_gain.shape[0]
    tokens, cols = cross_query.shape
    heads = cols // head_size
    patches = features.shape[1]
    half = patches // 2
    seq_pos = lax.axis_index("seq")
    head_pos = lax.axis_index("head")
    y, x, core = seq_pos // 4, (seq_pos // 2) % 2, seq_pos % 2
    head_x, head_z = head_pos // 4, head_pos % 4
    chunks = 4 * tokens // CHUNK
    rows = heads * CHUNK

    own_part = lax.dynamic_slice_in_dim(features[0], core * half, half)
    sent_part = lax.dynamic_slice_in_dim(features[0], (1 - core) * half, half)
    peer_part = send_seq(sent_part, core=1)
    slots = placement.reshape(8, 2)
    stale = jnp.any(slots[:, :, None] == evicted, axis=-1)
    both = stale[:, 0] & stale[:, 1]
    chip = seq_pos // 2
    first_stale = stale[chip, 0]
    use_own = first_stale == (core == 0)
    home = jnp.stack([head_at(head_x + r % 2, head_z + r // 2) for r in range(8)]).astype(jnp.int32)

    def rebuild(part_rows):
        summed = sum_over_head(rebuild_parts(part_rows, image_proj, home))
        mine = normalize(summed, key_gain)
        pair = jnp.stack([mine, send_seq(mine, x=1)])
        return pair, send_seq(pair, core=1)

    held = image_cache[0]
    q_blocks = [cross_query] + [send_seq(cross_query, y=-dy) for dy in (1, 2, 3)]
    held_x = send_seq(held, x=1)
    held_core = send_seq(held, core=1)
    held_both = send_seq(held_x, core=1)

    spans = image_spans.reshape(16, tokens, 2)
    mine = jnp.stack(
        [lax.dynamic_index_in_dim(spans, seq_at(y + dy, x, core), 0, keepdims=False) for dy in range(4)]
    )
    first, stop = mine[:, :, 0], mine[:, :, 1]
    index = jnp.arange(tokens, dtype=jnp.int32)
    earlier = (first[:, None, :] < first[:, :, None]) | (
        (first[:, None, :] == first[:, :, None]) & (index[None, :] < index[:, None])[None]
    )
    rank = jnp.sum(earlier.astype(jnp.int32), axis=2)
    order = rank[:, None, :] == index[None, :, None]
    first = jnp.sum(jnp.where(order, first[:, None, :], 0), axis=2)
    stop = jnp.sum(jnp.where(order, stop[:, None, :], 0), axis=2)
    order = order.astype(jnp.bfloat16)
    chips = (chip, seq_at(y, x + 1, 0) // 2)
    held_ids = [slots[chips[0], core], slots[chips[0], 1 - core], slots[chips[1], core], slots[chips[1], 1 - core]]
    held_live = [
        ~stale[chips[0], core],
        ~stale[chips[0], 1 - core],
        ~stale[chips[1], core],
        ~stale[chips[1], 1 - core],
    ]
    once_ids = [jnp.where(stale[at, 0], slots[at, 0], slots[at, 1]) for at in chips]
    once_live = [stale[at, 0] | stale[at, 1] for at in chips]
    twice_ids = [slots[at, 1] for at in chips]
    twice_live = [both[at] for at in chips]
    ids = jnp.stack(held_ids + once_ids * 2 + twice_ids * 2).astype(jnp.int32)
    live = jnp.stack(held_live + once_live * 2 + twice_live * 2)
    seen = (first.reshape(1, chunks, CHUNK) <= ids[:, None, None]) & (
        ids[:, None, None] < stop.reshape(1, chunks, CHUNK)
    )
    wanted = jnp.any(seen, axis=2) & live[:, None]
    chunk_index = jnp.arange(chunks, dtype=jnp.int32)
    place = jnp.sum((wanted[:, None, :] & (chunk_index[None, :] < chunk_index[:, None])[None]).astype(jnp.int32), axis=2)
    lists = jnp.sum(
        jnp.where(
            wanted[:, None, :] & (place[:, None, :] == jnp.arange(LIST, dtype=jnp.int32)[None, :, None]),
            chunk_index[None, None, :],
            0,
        ),
        axis=2,
    )
    counts = jnp.sum(wanted.astype(jnp.int32), axis=1)
    first_col = first.reshape(4 * tokens, 1)
    stop_col = stop.reshape(4 * tokens, 1)

    state_shapes = [
        jax.ShapeDtypeStruct((chunks, rows, 1), jnp.float32),
        jax.ShapeDtypeStruct((chunks, rows, 1), jnp.float32),
        jax.ShapeDtypeStruct((chunks, rows, head_size), jnp.float32),
    ]
    smem = pl.BlockSpec(memory_space=pltpu.SMEM)
    vmem = pl.BlockSpec(memory_space=pltpu.VMEM)
    qs, high, total, mixed = pl.pallas_call(
        functools.partial(held_kernel, head_size),
        in_specs=[smem] * 3 + [vmem] * 11,
        out_specs=[vmem] * 4,
        out_shape=[jax.ShapeDtypeStruct((chunks, rows, head_size), jnp.bfloat16)] + state_shapes,
        scratch_shapes=[pltpu.VMEM((rows, patches), jnp.float32)] * 2,
        compiler_params=VMEM,
        name="attend_held",
    )(
        ids[:4], counts[:4], lists[:4].reshape(-1), *q_blocks, order, first_col, stop_col, held, held_core, held_x, held_both
    )

    once, once_core = rebuild(jnp.where(use_own, own_part, peer_part))
    nothing = jnp.zeros((2, half, 2 * head_size), jnp.bfloat16)
    twice, twice_core = lax.cond(
        jnp.any(both),
        lambda: rebuild(jnp.where(use_own, peer_part, own_part)),
        lambda: (nothing, nothing),
    )
    partial_out = pl.pallas_call(
        functools.partial(rebuilt_kernel, head_size),
        in_specs=[smem] * 3 + [vmem] * 11,
        out_specs=[vmem] * 4,
        out_shape=[jax.ShapeDtypeStruct((tokens, cols + 128), jnp.bfloat16)] * 4,
        scratch_shapes=[pltpu.VMEM(s.shape, s.dtype) for s in state_shapes]
        + [pltpu.VMEM((rows, half), jnp.float32)] * 2,
        compiler_params=VMEM,
        name="attend_rebuilt",
    )(
        ids[4:], counts[4:], lists[4:].reshape(-1), qs, order, first_col, stop_col, high, total, mixed,
        once, once_core, twice, twice_core,
    )
    arrived = [partial_out[0]] + [send_seq(partial_out[dy], y=dy) for dy in (1, 2, 3)]
    context = pl.pallas_call(
        functools.partial(merge_kernel, head_size),
        in_specs=[vmem] * 4,
        out_specs=vmem,
        out_shape=jax.ShapeDtypeStruct((tokens, cols), jnp.bfloat16),
        compiler_params=VMEM,
        name="merge",
    )(*arrived)

    own_context = jnp.stack(gather_chips(context))
    other_context = send_seq(own_context, core=1)
    source = []
    for r in range(8):
        target = head_at(head_x + r % 2, head_z + r // 2)
        source.append(2 * ((target // 2 - y) % 4) + (target % 2 - x) % 2)
    parts = project_parts(
        own_context, other_context, out_weight, jnp.stack(source).astype(jnp.int32), core.reshape(1).astype(jnp.int32)
    )
    summed_out = sum_over_head(parts)
    return (hidden.astype(jnp.float32) + jnp.tanh(cross_gate[0]) * summed_out).astype(jnp.bfloat16)


def solution(mesh):
    placed = (
        P("head", "seq"),
        P("seq", "head"),
        P("seq", None, "head"),
        P("seq", None, "head"),
        P("head", None),
        P(),
        P("head", "seq"),
        P(),
        P(),
        P(),
        P(),
    )
    return jax.shard_map(
        on_device, mesh=mesh, in_specs=placed, out_specs=P("head", "seq"), check_vma=False
    )
```

```python
import functools
import math

import jax
import jax.numpy as jnp
from jax import lax
from jax.experimental import pallas as pl
from jax.experimental.pallas import tpu as pltpu
from jax.sharding import PartitionSpec as P

MASKED_SCORE = -1e30
CHUNK = 32
LIST = 18
VMEM = pltpu.CompilerParams(vmem_limit_bytes=40 * 1024 * 1024)


def seq_at(y, x, core):
    return (y % 4) * 4 + (x % 2) * 2 + core % 2


def head_at(x, z):
    return (x % 2) * 4 + z % 4


def send_seq(array, y=0, x=0, core=0):
    pairs = [
        (seq_at(a, b, c), seq_at(a + y, b + x, c + core)) for a in range(4) for b in range(2) for c in range(2)
    ]
    return lax.ppermute(array, "seq", pairs)


def send_head(array, x=0, z=0):
    return lax.ppermute(array, "head", [(head_at(a, b), head_at(a + x, b + z)) for a in range(2) for b in range(4)])


def add(*terms):
    return sum(term.astype(jnp.float32) for term in terms).astype(jnp.bfloat16)


def add_kernel(a_ref, b_ref, after_ref, out_ref):
    out_ref[...] = (a_ref[...].astype(jnp.float32) + b_ref[...].astype(jnp.float32)).astype(out_ref.dtype)


def add_after(a, b, after):
    vmem = pl.BlockSpec(memory_space=pltpu.VMEM)
    return pl.pallas_call(
        add_kernel,
        in_specs=[vmem, vmem, pl.BlockSpec(memory_space=pl.ANY)],
        out_specs=vmem,
        out_shape=jax.ShapeDtypeStruct(a.shape, a.dtype),
        compiler_params=VMEM,
        name="add_after",
    )(a, b, after)


def sum_over_head(parts, work=None):
    p00, p01, p10, p11, p20, p21, p30, p31 = parts
    via_x = send_head(p21, x=1)
    down = send_head(p31, z=-1)
    across = send_head(p11, x=1)
    last = send_head(p30, z=-1)
    if work is None:
        p20 = add(p20, via_x)
        p01 = add(p01, down)
    else:
        state = work[0]()
        p20 = add_after(p20, via_x, state[-1])
        p01 = add_after(p01, down, state[-1])
    up = send_head(p20, z=1)
    side = send_head(p01, x=1)
    p10 = add(p10, across)
    if work is None:
        p10 = add(p10, up)
    else:
        state = work[1](state)
        p10 = add_after(p10, up, state[-1])
    ahead = send_head(p10, z=1)
    total = sum(term.astype(jnp.float32) for term in (p00, last, side))
    if work is None:
        return total + ahead.astype(jnp.float32)
    return total + ahead.astype(jnp.float32), state


def gather_chips(block):
    r30 = send_seq(block, y=1)
    r01 = send_seq(block, x=1)
    r10 = send_seq(block, y=-1)
    r20 = send_seq(r30, y=1)
    r31 = send_seq(r30, x=1)
    r11 = send_seq(r01, y=-1)
    r21 = send_seq(r20, x=1)
    return block, r01, r10, r11, r20, r21, r30, r31


def rebuild_kernel(order_ref, rows_ref, proj_ref, *out_refs):
    product = jnp.dot(rows_ref[...], proj_ref[...], preferred_element_type=jnp.float32).astype(jnp.bfloat16)
    for at, out_ref in enumerate(out_refs):

        @pl.when(pl.program_id(0) == at)
        def _():
            out_ref[...] = product


def rebuild_parts(rows, proj, order):
    count, depth = rows.shape
    cols = proj.shape[1] // 8
    return pl.pallas_call(
        rebuild_kernel,
        grid_spec=pltpu.PrefetchScalarGridSpec(
            num_scalar_prefetch=1,
            grid=(8,),
            in_specs=[
                pl.BlockSpec((count, depth), lambda i, order: (0, 0)),
                pl.BlockSpec((depth, cols), lambda i, order: (0, order[i])),
            ],
            out_specs=[pl.BlockSpec((count, cols), lambda i, order: (0, 0))] * 8,
        ),
        out_shape=[jax.ShapeDtypeStruct((count, cols), jnp.bfloat16)] * 8,
        compiler_params=VMEM,
        name="rebuild_parts",
    )(order, rows, proj)


def project_kernel(order_ref, core_ref, own_ref, other_ref, weight_ref, *out_refs):
    own, other = own_ref[0], other_ref[0]
    even = core_ref[0] == 0
    both = jnp.concatenate([jnp.where(even, own, other), jnp.where(even, other, own)], axis=0)
    product = jnp.dot(both, weight_ref[...], preferred_element_type=jnp.float32).astype(jnp.bfloat16)
    for at, out_ref in enumerate(out_refs):

        @pl.when(pl.program_id(0) == at)
        def _():
            out_ref[...] = product


def project_parts(own, other, weight, order, core):
    _, tokens, depth = own.shape
    cols = weight.shape[1]
    block = pl.BlockSpec((1, tokens, depth), lambda i, order, core: (order[i], 0, 0))
    return pl.pallas_call(
        project_kernel,
        grid_spec=pltpu.PrefetchScalarGridSpec(
            num_scalar_prefetch=2,
            grid=(8,),
            in_specs=[block, block, pl.BlockSpec((depth, cols), lambda i, order, core: (0, 0))],
            out_specs=[pl.BlockSpec((2 * tokens, cols), lambda i, order, core: (0, 0))] * 8,
        ),
        out_shape=[jax.ShapeDtypeStruct((2 * tokens, cols), jnp.bfloat16)] * 8,
        compiler_params=VMEM,
        name="project_parts",
    )(order, core, own, other, weight)


def sweep(head_size, ids_ref, count_ref, list_ref, q_ref, first_ref, stop_ref, kv_parts, state, even, odd, wide):
    factor = math.log2(math.e) * head_size ** (-0.5)
    heads = q_ref.shape[1] // CHUNK
    m_ref, l_ref, acc_ref = state

    for slot, part in enumerate(kv_parts):
        count = count_ref[slot]

        def score(place, into):
            into[...] = lax.dot_general(
                q_ref[list_ref[slot * LIST + place]],
                part()[:, :head_size],
                (((1,), (1,)), ((), ())),
                preferred_element_type=jnp.float32,
            )

        def take(place, scores_ref):
            chunk = list_ref[slot * LIST + place]
            image = jnp.where(place < count, ids_ref[slot], -1)
            scores = scores_ref[...]
            here = jnp.broadcast_to(jnp.max(scores, axis=1, keepdims=True), (scores.shape[0], head_size))
            weights = jnp.exp2((scores - here[:, :1]) * factor)
            both = jnp.dot(weights.astype(jnp.bfloat16), wide[...], preferred_element_type=jnp.float32)
            mixed, total = both[:, :head_size], both[:, head_size:]
            tokens = pl.ds(pl.multiple_of(chunk * CHUNK, CHUNK), CHUNK)
            seen = (first_ref[tokens, :] <= image) & (image < stop_ref[tokens, :])
            seen = jnp.concatenate([seen.astype(jnp.int32)] * heads, axis=0) > 0
            before = m_ref[chunk]
            after = jnp.where(seen, jnp.maximum(before, here), before)
            keep = jnp.exp2((before - after) * factor)
            gain = jnp.where(seen, jnp.exp2((here - after) * factor), 0.0)
            m_ref[chunk] = after
            l_ref[chunk] = l_ref[chunk] * keep + gain * total
            acc_ref[chunk] = acc_ref[chunk] * keep + gain * mixed

        @pl.when(count > 0)
        def _():
            wide[:, :head_size] = part()[:, head_size:]
            wide[:, head_size:] = jnp.ones_like(wide[:, head_size:])
            score(0, even)

            def body(at, carry):
                place = 2 * at
                score(place + 1, odd)
                take(place, even)
                score(place + 2, even)
                take(place + 1, odd)
                return carry

            lax.fori_loop(0, (count + 1) // 2, body, 0)


def begin_kernel(head_size, ids, count, lists, q0, q1, q2, q3, order, first, stop, a, qs, m, l, acc, even, odd, wide):
    heads = q0.shape[1] // head_size
    per_block = q0.shape[0] // CHUNK
    for block, q_ref in enumerate((q0, q1, q2, q3)):
        ordered = jnp.dot(order[block], q_ref[...], preferred_element_type=jnp.float32).astype(jnp.bfloat16)
        for part in range(per_block):
            for head in range(heads):
                qs[block * per_block + part, head * CHUNK : (head + 1) * CHUNK, :] = ordered[
                    part * CHUNK : (part + 1) * CHUNK, head * head_size : (head + 1) * head_size
                ]
    m[...] = jnp.full_like(m, MASKED_SCORE)
    l[...] = jnp.zeros_like(l)
    acc[...] = jnp.zeros_like(acc)
    sweep(head_size, ids, count, lists, qs, first, stop, [lambda: a[...]], (m, l, acc), even, odd, wide)


def go_on_kernel(head_size, parts, ids, count, lists, qs, first, stop, m_in, l_in, acc_in, *refs):
    kv, (m, l, acc, even, odd, wide) = refs[:parts], refs[parts:]
    m[...] = m_in[...]
    l[...] = l_in[...]
    acc[...] = acc_in[...]
    sweep(
        head_size, ids, count, lists, qs, first, stop, [lambda r=r: r[...] for r in kv], (m, l, acc), even, odd, wide
    )


def rebuilt_kernel(
    head_size, ids, count, lists, qs, first, stop, m_in, l_in, acc_in, order, a, b, c, d, o0, o1, o2, o3, m, l, acc, even, odd, wide
):
    factor = math.log2(math.e) * head_size ** (-0.5)
    tokens = o0.shape[0]
    heads = qs.shape[1] // CHUNK
    per_block = tokens // CHUNK
    m[...] = m_in[...]
    l[...] = l_in[...]
    acc[...] = acc_in[...]
    kv_parts = [lambda r=r, i=i: r[i] for r in (a, b, c, d) for i in range(2)]
    sweep(head_size, ids, count, lists, qs, first, stop, kv_parts, (m, l, acc), even, odd, wide)
    lanes = lax.broadcasted_iota(jnp.int32, (tokens, 128), 1)
    for block, out in enumerate((o0, o1, o2, o3)):
        extra = jnp.zeros((tokens, 128), jnp.float32)
        for head in range(heads):
            rows = slice(head * CHUNK, (head + 1) * CHUNK)
            chunks = range(block * per_block, (block + 1) * per_block)
            high = jnp.concatenate([m[chunk, rows, :] for chunk in chunks], axis=0)
            total = jnp.concatenate([l[chunk, rows, :] for chunk in chunks], axis=0)
            mixed = jnp.concatenate([acc[chunk, rows, :] for chunk in chunks], axis=0)
            some = total > 0.0
            safe = jnp.where(some, total, 1.0)
            level = jnp.where(some, high * factor + jnp.log2(safe), MASKED_SCORE)
            ordered = (mixed / safe).astype(jnp.bfloat16)
            out[:, head * head_size : (head + 1) * head_size] = lax.dot_general(
                order[block], ordered, (((0,), (0,)), ((), ())), preferred_element_type=jnp.float32
            ).astype(jnp.bfloat16)
            for piece in range(3):
                rounded = level.astype(jnp.bfloat16).astype(jnp.float32)
                extra = jnp.where(lanes == piece * heads + head, rounded, extra)
                level = level - rounded
        out[:, heads * head_size :] = lax.dot_general(
            order[block], extra.astype(jnp.bfloat16), (((0,), (0,)), ((), ())), preferred_element_type=jnp.float32
        ).astype(jnp.bfloat16)


def merge_kernel(head_size, a, b, c, d, out):
    heads = out.shape[1] // head_size
    parts = (a, b, c, d)
    extras = [part[:, heads * head_size :].astype(jnp.float32) for part in parts]
    for head in range(heads):
        cols = slice(head * head_size, (head + 1) * head_size)
        levels = [sum(e[:, p * heads + head : p * heads + head + 1] for p in range(3)) for e in extras]
        top = functools.reduce(jnp.maximum, levels)
        shares = [jnp.exp2(level - top) for level in levels]
        mixed = sum(share * part[:, cols].astype(jnp.float32) for share, part in zip(shares, parts))
        out[:, cols] = (mixed / sum(shares)).astype(jnp.bfloat16)


def normalize(summed, key_gain):
    head_size = key_gain.shape[0]
    key_cols = summed[:, :head_size]
    inverse = lax.rsqrt(jnp.mean(key_cols * key_cols, axis=-1, keepdims=True) + 1e-05)
    return jnp.concatenate([key_cols * inverse * key_gain, summed[:, head_size:]], axis=1).astype(jnp.bfloat16)


def on_device(
    hidden,
    cross_query,
    image_cache,
    features,
    image_proj,
    key_gain,
    out_weight,
    cross_gate,
    image_spans,
    evicted,
    placement,
):
    head_size = key_gain.shape[0]
    tokens, cols = cross_query.shape
    heads = cols // head_size
    patches = features.shape[1]
    half = patches // 2
    seq_pos = lax.axis_index("seq")
    head_pos = lax.axis_index("head")
    y, x, core = seq_pos // 4, (seq_pos // 2) % 2, seq_pos % 2
    head_x, head_z = head_pos // 4, head_pos % 4
    chunks = 4 * tokens // CHUNK
    rows = heads * CHUNK

    own_part = lax.dynamic_slice_in_dim(features[0], core * half, half)
    sent_part = lax.dynamic_slice_in_dim(features[0], (1 - core) * half, half)
    peer_part = send_seq(sent_part, core=1)
    slots = placement.reshape(8, 2)
    stale = jnp.any(slots[:, :, None] == evicted, axis=-1)
    both = stale[:, 0] & stale[:, 1]
    chip = seq_pos // 2
    first_stale = stale[chip, 0]
    use_own = first_stale == (core == 0)
    home = jnp.stack([head_at(head_x + r % 2, head_z + r // 2) for r in range(8)]).astype(jnp.int32)

    def rebuild(part_rows, work=None):
        summed = sum_over_head(rebuild_parts(part_rows, image_proj, home), work)
        summed, rest = (summed, ()) if work is None else (summed[0], (summed[1],))
        mine = normalize(summed, key_gain)
        pair = jnp.stack([mine, send_seq(mine, x=1)])
        return (pair, send_seq(pair, core=1)) + rest

    held = image_cache[0]
    q_blocks = [cross_query] + [send_seq(cross_query, y=-dy) for dy in (1, 2, 3)]
    held_x = send_seq(held, x=1)
    held_core = send_seq(held, core=1)
    held_both = send_seq(held_x, core=1)

    spans = image_spans.reshape(16, tokens, 2)
    mine = jnp.stack(
        [lax.dynamic_index_in_dim(spans, seq_at(y + dy, x, core), 0, keepdims=False) for dy in range(4)]
    )
    first, stop = mine[:, :, 0], mine[:, :, 1]
    index = jnp.arange(tokens, dtype=jnp.int32)
    earlier = (first[:, None, :] < first[:, :, None]) | (
        (first[:, None, :] == first[:, :, None]) & (index[None, :] < index[:, None])[None]
    )
    rank = jnp.sum(earlier.astype(jnp.int32), axis=2)
    order = rank[:, None, :] == index[None, :, None]
    first = jnp.sum(jnp.where(order, first[:, None, :], 0), axis=2)
    stop = jnp.sum(jnp.where(order, stop[:, None, :], 0), axis=2)
    order = order.astype(jnp.bfloat16)
    chips = (chip, seq_at(y, x + 1, 0) // 2)
    held_ids = [slots[chips[0], core], slots[chips[0], 1 - core], slots[chips[1], core], slots[chips[1], 1 - core]]
    held_live = [
        ~stale[chips[0], core],
        ~stale[chips[0], 1 - core],
        ~stale[chips[1], core],
        ~stale[chips[1], 1 - core],
    ]
    once_ids = [jnp.where(stale[at, 0], slots[at, 0], slots[at, 1]) for at in chips]
    once_live = [stale[at, 0] | stale[at, 1] for at in chips]
    twice_ids = [slots[at, 1] for at in chips]
    twice_live = [both[at] for at in chips]
    ids = jnp.stack(held_ids + once_ids * 2 + twice_ids * 2).astype(jnp.int32)
    live = jnp.stack(held_live + once_live * 2 + twice_live * 2)
    seen = (first.reshape(1, chunks, CHUNK) <= ids[:, None, None]) & (
        ids[:, None, None] < stop.reshape(1, chunks, CHUNK)
    )
    wanted = jnp.any(seen, axis=2) & live[:, None]
    chunk_index = jnp.arange(chunks, dtype=jnp.int32)
    place = jnp.sum((wanted[:, None, :] & (chunk_index[None, :] < chunk_index[:, None])[None]).astype(jnp.int32), axis=2)
    lists = jnp.sum(
        jnp.where(
            wanted[:, None, :] & (place[:, None, :] == jnp.arange(LIST, dtype=jnp.int32)[None, :, None]),
            chunk_index[None, None, :],
            0,
        ),
        axis=2,
    )
    counts = jnp.sum(wanted.astype(jnp.int32), axis=1)
    first_all = jnp.broadcast_to(first.reshape(4 * tokens, 1), (4 * tokens, head_size))
    stop_all = jnp.broadcast_to(stop.reshape(4 * tokens, 1), (4 * tokens, head_size))
    state_shapes = [jax.ShapeDtypeStruct((chunks, rows, head_size), jnp.float32)] * 3
    smem = pl.BlockSpec(memory_space=pltpu.SMEM)
    vmem = pl.BlockSpec(memory_space=pltpu.VMEM)

    def scratch(keys):
        return [pltpu.VMEM((rows, keys), jnp.float32)] * 2 + [pltpu.VMEM((keys, 2 * head_size), jnp.bfloat16)]

    def listed(low, high):
        return ids[low:high], counts[low:high], lists[low:high].reshape(-1)

    def attend_first():
        return pl.pallas_call(
            functools.partial(begin_kernel, head_size),
            in_specs=[smem] * 3 + [vmem] * 8,
            out_specs=[vmem] * 4,
            out_shape=[jax.ShapeDtypeStruct((chunks, rows, head_size), jnp.bfloat16)] + state_shapes,
            scratch_shapes=scratch(patches),
            compiler_params=VMEM,
            name="attend_first",
        )(*listed(0, 1), *q_blocks, order, first_all, stop_all, held)

    def attend_more(state, low, *kv):
        return state[:1] + pl.pallas_call(
            functools.partial(go_on_kernel, head_size, len(kv)),
            in_specs=[smem] * 3 + [vmem] * (6 + len(kv)),
            out_specs=[vmem] * 3,
            out_shape=state_shapes,
            scratch_shapes=scratch(patches),
            compiler_params=VMEM,
            name="attend_more",
        )(*listed(low, low + len(kv)), state[0], first_all, stop_all, *state[1:], *kv)

    work = (attend_first, lambda state: attend_more(state, 1, held_core, held_x))
    once, once_core, state = rebuild(jnp.where(use_own, own_part, peer_part), work)
    state = attend_more(state, 3, held_both)
    nothing = jnp.zeros((2, half, 2 * head_size), jnp.bfloat16)
    twice, twice_core = lax.cond(
        jnp.any(both),
        lambda: rebuild(jnp.where(use_own, peer_part, own_part)),
        lambda: (nothing, nothing),
    )
    partial_out = pl.pallas_call(
        functools.partial(rebuilt_kernel, head_size),
        in_specs=[smem] * 3 + [vmem] * 11,
        out_specs=[vmem] * 4,
        out_shape=[jax.ShapeDtypeStruct((tokens, cols + 128), jnp.bfloat16)] * 4,
        scratch_shapes=[pltpu.VMEM(s.shape, s.dtype) for s in state_shapes] + scratch(half),
        compiler_params=VMEM,
        name="attend_rebuilt",
    )(*listed(4, 12), state[0], first_all, stop_all, *state[1:], order, once, once_core, twice, twice_core)
    arrived = [partial_out[0]] + [send_seq(partial_out[dy], y=dy) for dy in (1, 2, 3)]
    context = pl.pallas_call(
        functools.partial(merge_kernel, head_size),
        in_specs=[vmem] * 4,
        out_specs=vmem,
        out_shape=jax.ShapeDtypeStruct((tokens, cols), jnp.bfloat16),
        compiler_params=VMEM,
        name="merge",
    )(*arrived)

    own_context = jnp.stack(gather_chips(context))
    other_context = send_seq(own_context, core=1)
    source = []
    for r in range(8):
        target = head_at(head_x + r % 2, head_z + r // 2)
        source.append(2 * ((target // 2 - y) % 4) + (target % 2 - x) % 2)
    parts = project_parts(
        own_context, other_context, out_weight, jnp.stack(source).astype(jnp.int32), core.reshape(1).astype(jnp.int32)
    )
    summed_out = sum_over_head(parts)
    return (hidden.astype(jnp.float32) + jnp.tanh(cross_gate[0]) * summed_out).astype(jnp.bfloat16)


def solution(mesh):
    placed = (
        P("head", "seq"),
        P("seq", "head"),
        P("seq", None, "head"),
        P("seq", None, "head"),
        P("head", None),
        P(),
        P("head", "seq"),
        P(),
        P(),
        P(),
        P(),
    )
    return jax.shard_map(
        on_device, mesh=mesh, in_specs=placed, out_specs=P("head", "seq"), check_vma=False
    )
```

```python
import functools
import math

import jax
import jax.numpy as jnp
from jax import lax
from jax.experimental import pallas as pl
from jax.experimental.pallas import tpu as pltpu
from jax.sharding import PartitionSpec as P

MASKED_SCORE = -1e30
CHUNK = 32
COUNT_ROW = 18
ID_ROW = 19
PLAN_ROWS = 24
VMEM = pltpu.CompilerParams(vmem_limit_bytes=20 * 1024 * 1024)


def seq_at(y, x, core):
    return (y % 4) * 4 + (x % 2) * 2 + core % 2


def head_at(x, z):
    return (x % 2) * 4 + z % 4


def send_seq(array, y=0, x=0, core=0):
    pairs = [
        (seq_at(a, b, c), seq_at(a + y, b + x, c + core)) for a in range(4) for b in range(2) for c in range(2)
    ]
    return lax.ppermute(array, "seq", pairs)


def send_head(array, x=0, z=0):
    return lax.ppermute(array, "head", [(head_at(a, b), head_at(a + x, b + z)) for a in range(2) for b in range(4)])


def add(*terms):
    return sum(term.astype(jnp.float32) for term in terms).astype(jnp.bfloat16)


def add_kernel(a_ref, b_ref, after_ref, out_ref):
    out_ref[...] = (a_ref[...].astype(jnp.float32) + b_ref[...].astype(jnp.float32)).astype(out_ref.dtype)


def add_after(a, b, after):
    vmem = pl.BlockSpec(memory_space=pltpu.VMEM)
    return pl.pallas_call(
        add_kernel,
        in_specs=[vmem, vmem, pl.BlockSpec(memory_space=pl.ANY)],
        out_specs=vmem,
        out_shape=jax.ShapeDtypeStruct(a.shape, a.dtype),
        compiler_params=VMEM,
        name="add_after",
    )(a, b, after)


def sum_over_head(parts, work=None):
    p00, p01, p10, p11, p20, p21, p30, p31 = parts
    via_x = send_head(p21, x=1)
    down = send_head(p31, z=-1)
    across = send_head(p11, x=1)
    last = send_head(p30, z=-1)
    if work is None:
        p20 = add(p20, via_x)
        p01 = add(p01, down)
    else:
        state = work[0]()
        p20 = add_after(p20, via_x, state[-1])
        p01 = add_after(p01, down, state[-1])
    up = send_head(p20, z=1)
    side = send_head(p01, x=1)
    p10 = add(p10, across)
    if work is None:
        p10 = add(p10, up)
    else:
        state = work[1](state)
        p10 = add_after(p10, up, state[-1])
    ahead = send_head(p10, z=1)
    terms = (p00, last, side, ahead)
    return terms if work is None else (terms, state)


def gather_chips(block):
    r30 = send_seq(block, y=1)
    r01 = send_seq(block, x=1)
    r10 = send_seq(block, y=-1)
    r20 = send_seq(r30, y=1)
    r31 = send_seq(r30, x=1)
    r11 = send_seq(r01, y=-1)
    r21 = send_seq(r20, x=1)
    return jnp.stack([block, r01, r10, r30]), jnp.stack([r20, r31, r11, r21])


def rebuild_kernel(order_ref, pick_ref, own_ref, peer_ref, proj0_ref, proj1_ref, *refs):
    out_refs, rows_ref = refs[:8], refs[8]
    step = pl.program_id(0)

    @pl.when(step == 0)
    def _():
        rows_ref[...] = jnp.where(pick_ref[0] > 0, own_ref[0], peer_ref[...])

    products = [
        jnp.dot(rows_ref[...], proj_ref[...], preferred_element_type=jnp.float32).astype(jnp.bfloat16)
        for proj_ref in (proj0_ref, proj1_ref)
    ]
    for at in range(4):

        @pl.when(step == at)
        def _():
            out_refs[2 * at][...] = products[0]
            out_refs[2 * at + 1][...] = products[1]


def rebuild_parts(features, peer_part, proj, order, pick):
    count, depth = peer_part.shape
    cols = proj.shape[1] // 8
    return pl.pallas_call(
        rebuild_kernel,
        grid_spec=pltpu.PrefetchScalarGridSpec(
            num_scalar_prefetch=2,
            grid=(4,),
            in_specs=[
                pl.BlockSpec((1, count, depth), lambda i, order, pick: (0, pick[1], 0)),
                pl.BlockSpec((count, depth), lambda i, order, pick: (0, 0)),
                pl.BlockSpec((depth, cols), lambda i, order, pick: (0, order[2 * i])),
                pl.BlockSpec((depth, cols), lambda i, order, pick: (0, order[2 * i + 1])),
            ],
            out_specs=[pl.BlockSpec((count, cols), lambda i, order, pick: (0, 0))] * 8,
            scratch_shapes=[pltpu.VMEM((count, depth), jnp.bfloat16)],
        ),
        out_shape=[jax.ShapeDtypeStruct((count, cols), jnp.bfloat16)] * 8,
        compiler_params=VMEM,
        name="rebuild_parts",
    )(order, pick, features, peer_part, proj, proj)


def project_kernel(order_ref, core_ref, own0_ref, own1_ref, other0_ref, other1_ref, weight_ref, *out_refs):
    step = pl.program_id(0)
    even = core_ref[0] == 0
    tokens = own0_ref.shape[1]

    def block(first_ref, second_ref, at):
        return jnp.where(at < 4, first_ref[jnp.minimum(at, 3)], second_ref[jnp.maximum(at - 4, 0)])

    rows = []
    for part in range(2):
        at = order_ref[2 * step + part]
        own, other = block(own0_ref, own1_ref, at), block(other0_ref, other1_ref, at)
        rows += [jnp.where(even, own, other), jnp.where(even, other, own)]
    product = jnp.dot(
        jnp.concatenate(rows, axis=0), weight_ref[...], preferred_element_type=jnp.float32
    ).astype(jnp.bfloat16)
    for at in range(4):

        @pl.when(step == at)
        def _():
            out_refs[2 * at][...] = product[: 2 * tokens]
            out_refs[2 * at + 1][...] = product[2 * tokens :]


def project_parts(blocks, weight, order, core):
    _, tokens, depth = blocks[0].shape
    cols = weight.shape[1]
    return pl.pallas_call(
        project_kernel,
        grid_spec=pltpu.PrefetchScalarGridSpec(
            num_scalar_prefetch=2,
            grid=(4,),
            in_specs=[pl.BlockSpec((4, tokens, depth), lambda i, order, core: (0, 0, 0))] * 4
            + [pl.BlockSpec((depth, cols), lambda i, order, core: (0, 0))],
            out_specs=[pl.BlockSpec((2 * tokens, cols), lambda i, order, core: (0, 0))] * 8,
        ),
        out_shape=[jax.ShapeDtypeStruct((2 * tokens, cols), jnp.bfloat16)] * 8,
        compiler_params=VMEM,
        name="project_parts",
    )(order, core, *blocks, weight)


def plan_kernel(pos_ref, placement_ref, evicted_ref, spans_ref, order_ref, first_ref, stop_ref, plan_ref):
    seq_pos = pos_ref[0]
    y, x, core = seq_pos // 4, (seq_pos // 2) % 2, seq_pos % 2
    tokens = spans_ref.shape[2]
    chips = (seq_pos // 2, seq_at(y, x + 1, 0) // 2)

    def stale(slot):
        image = placement_ref[slot]
        return (image == evicted_ref[0]) | (image == evicted_ref[1])

    entries = []
    for chip in chips:
        for slot in (2 * chip + core, 2 * chip + 1 - core):
            entries.append((placement_ref[slot], ~stale(slot)))
    once, twice = [], []
    for chip in chips:
        low, high = stale(2 * chip), stale(2 * chip + 1)
        once.append((jnp.where(low, placement_ref[2 * chip], placement_ref[2 * chip + 1]), low | high))
        twice.append((placement_ref[2 * chip + 1], low & high))
    entries += once * 2 + twice * 2
    slot_lane = lax.broadcasted_iota(jnp.int32, (CHUNK, 128), 1)
    ids = jnp.full((CHUNK, 128), -1, jnp.int32)
    for at, (image, live) in enumerate(entries):
        ids = jnp.where(slot_lane == at, jnp.where(live, image, -1), ids)

    up = lax.broadcasted_iota(jnp.int32, (tokens, tokens), 0)
    along = lax.broadcasted_iota(jnp.int32, (tokens, tokens), 1)
    wanted = []
    for dy in range(4):
        block = seq_at(y + dy, x, core)
        first = jnp.broadcast_to(spans_ref[0, pl.ds(block, 1), :].astype(jnp.float32), (tokens, tokens))
        stop = jnp.broadcast_to(spans_ref[1, pl.ds(block, 1), :].astype(jnp.float32), (tokens, tokens))
        down = jnp.sum(jnp.where(up == along, first, 0.0), axis=1, keepdims=True)
        earlier = (down < first) | ((down == first) & (up < along))
        rank = jnp.sum(jnp.where(earlier, 1.0, 0.0), axis=0, keepdims=True).astype(jnp.int32)
        order = jnp.where(up == rank, 1.0, 0.0)
        order_ref[dy] = order.astype(jnp.bfloat16)
        first = jnp.broadcast_to(jnp.sum(order * first, axis=1, keepdims=True), (tokens, 128)).astype(jnp.int32)
        stop = jnp.broadcast_to(jnp.sum(order * stop, axis=1, keepdims=True), (tokens, 128)).astype(jnp.int32)
        first_ref[dy * tokens : (dy + 1) * tokens, :] = first
        stop_ref[dy * tokens : (dy + 1) * tokens, :] = stop
        for part in range(tokens // CHUNK):
            rows = slice(part * CHUNK, (part + 1) * CHUNK)
            seen = (first[rows] <= ids) & (ids < stop[rows])
            wanted.append(jnp.max(jnp.where(seen, 1, 0), axis=0, keepdims=True))
    places, total = [], jnp.zeros((1, 128), jnp.int32)
    for want in wanted:
        places.append(total)
        total = total + want
    for place in range(COUNT_ROW):
        row = jnp.zeros((1, 128), jnp.int32)
        for chunk, (want, at) in enumerate(zip(wanted, places)):
            row = jnp.where((want > 0) & (at == place), chunk, row)
        plan_ref[place : place + 1, :] = row
    plan_ref[COUNT_ROW : COUNT_ROW + 1, :] = total
    plan_ref[ID_ROW : ID_ROW + 1, :] = ids[:1]
    plan_ref[ID_ROW + 1 :, :] = jnp.zeros((PLAN_ROWS - ID_ROW - 1, 128), jnp.int32)


def sweep(head_size, plan_ref, low, q_ref, first_ref, stop_ref, kv_parts, state, even, odd, wide):
    factor = math.log2(math.e) * head_size ** (-0.5)
    heads = q_ref.shape[1] // CHUNK
    m_ref, l_ref, acc_ref = state

    for slot, part in enumerate(kv_parts, low):
        count = plan_ref[COUNT_ROW, slot]

        def score(place, into):
            into[...] = lax.dot_general(
                q_ref[plan_ref[place, slot]],
                part()[:, :head_size],
                (((1,), (1,)), ((), ())),
                preferred_element_type=jnp.float32,
            )

        def take(place, scores_ref):
            chunk = plan_ref[place, slot]
            image = jnp.where(place < count, plan_ref[ID_ROW, slot], -1)
            scores = scores_ref[...]
            here = jnp.broadcast_to(jnp.max(scores, axis=1, keepdims=True), (scores.shape[0], head_size))
            weights = jnp.exp2((scores - here[:, :1]) * factor)
            both = jnp.dot(weights.astype(jnp.bfloat16), wide[...], preferred_element_type=jnp.float32)
            mixed, total = both[:, :head_size], both[:, head_size:]
            tokens = pl.ds(pl.multiple_of(chunk * CHUNK, CHUNK), CHUNK)
            seen = (first_ref[tokens, :] <= image) & (image < stop_ref[tokens, :])
            seen = jnp.concatenate([seen.astype(jnp.int32)] * heads, axis=0) > 0
            before = m_ref[chunk]
            after = jnp.where(seen, jnp.maximum(before, here), before)
            keep = jnp.exp2((before - after) * factor)
            gain = jnp.where(seen, jnp.exp2((here - after) * factor), 0.0)
            m_ref[chunk] = after
            l_ref[chunk] = l_ref[chunk] * keep + gain * total
            acc_ref[chunk] = acc_ref[chunk] * keep + gain * mixed

        @pl.when(count > 0)
        def _():
            wide[:, :head_size] = part()[:, head_size:]
            wide[:, head_size:] = jnp.ones_like(wide[:, head_size:])
            score(0, even)

            def body(at, carry):
                place = 2 * at
                score(place + 1, odd)
                take(place, even)
                score(place + 2, even)
                take(place + 1, odd)
                return carry

            lax.fori_loop(0, (count + 1) // 2, body, 0)


def begin_kernel(head_size, plan, q0, q1, q2, q3, order, first, stop, a, qs, m, l, acc, even, odd, wide):
    heads = q0.shape[1] // head_size
    per_block = q0.shape[0] // CHUNK
    for block, q_ref in enumerate((q0, q1, q2, q3)):
        ordered = jnp.dot(order[block], q_ref[...], preferred_element_type=jnp.float32).astype(jnp.bfloat16)
        for part in range(per_block):
            for head in range(heads):
                qs[block * per_block + part, head * CHUNK : (head + 1) * CHUNK, :] = ordered[
                    part * CHUNK : (part + 1) * CHUNK, head * head_size : (head + 1) * head_size
                ]
    m[...] = jnp.full_like(m, MASKED_SCORE)
    l[...] = jnp.zeros_like(l)
    acc[...] = jnp.zeros_like(acc)
    sweep(head_size, plan, 0, qs, first, stop, [lambda: a[...]], (m, l, acc), even, odd, wide)


def go_on_kernel(head_size, parts, low, plan, qs, first, stop, m_in, l_in, acc_in, *refs):
    kv, (m, l, acc, even, odd, wide) = refs[:parts], refs[parts:]
    m[...] = m_in[...]
    l[...] = l_in[...]
    acc[...] = acc_in[...]
    sweep(head_size, plan, low, qs, first, stop, [lambda r=r: r[...] for r in kv], (m, l, acc), even, odd, wide)


def rebuilt_kernel(head_size, plan, qs, first, stop, m_in, l_in, acc_in, order, *refs):
    kv, (o0, o1, o2, o3, m, l, acc, even, odd, wide) = refs[:8], refs[8:]
    factor = math.log2(math.e) * head_size ** (-0.5)
    tokens = o0.shape[0]
    heads = qs.shape[1] // CHUNK
    per_block = tokens // CHUNK
    m[...] = m_in[...]
    l[...] = l_in[...]
    acc[...] = acc_in[...]
    kv_parts = [lambda r=r: r[...] for r in kv]
    sweep(head_size, plan, 4, qs, first, stop, kv_parts, (m, l, acc), even, odd, wide)
    lanes = lax.broadcasted_iota(jnp.int32, (tokens, 128), 1)
    for block, out in enumerate((o0, o1, o2, o3)):
        extra = jnp.zeros((tokens, 128), jnp.float32)
        for head in range(heads):
            rows = slice(head * CHUNK, (head + 1) * CHUNK)
            chunks = range(block * per_block, (block + 1) * per_block)
            high = jnp.concatenate([m[chunk, rows, :] for chunk in chunks], axis=0)
            total = jnp.concatenate([l[chunk, rows, :] for chunk in chunks], axis=0)
            mixed = jnp.concatenate([acc[chunk, rows, :] for chunk in chunks], axis=0)
            some = total > 0.0
            safe = jnp.where(some, total, 1.0)
            level = jnp.where(some, high * factor + jnp.log2(safe), MASKED_SCORE)
            ordered = (mixed / safe).astype(jnp.bfloat16)
            out[:, head * head_size : (head + 1) * head_size] = lax.dot_general(
                order[block], ordered, (((0,), (0,)), ((), ())), preferred_element_type=jnp.float32
            ).astype(jnp.bfloat16)
            for piece in range(3):
                rounded = level.astype(jnp.bfloat16).astype(jnp.float32)
                extra = jnp.where(lanes == piece * heads + head, rounded, extra)
                level = level - rounded
        out[:, heads * head_size :] = lax.dot_general(
            order[block], extra.astype(jnp.bfloat16), (((0,), (0,)), ((), ())), preferred_element_type=jnp.float32
        ).astype(jnp.bfloat16)


def merge_kernel(head_size, a, b, c, d, out):
    heads = out.shape[1] // head_size
    parts = (a, b, c, d)
    extras = [part[:, heads * head_size :].astype(jnp.float32) for part in parts]
    for head in range(heads):
        cols = slice(head * head_size, (head + 1) * head_size)
        levels = [sum(e[:, p * heads + head : p * heads + head + 1] for p in range(3)) for e in extras]
        top = functools.reduce(jnp.maximum, levels)
        shares = [jnp.exp2(level - top) for level in levels]
        mixed = sum(share * part[:, cols].astype(jnp.float32) for share, part in zip(shares, parts))
        out[:, cols] = (mixed / sum(shares)).astype(jnp.bfloat16)


def normalize_kernel(gain_ref, a, b, c, d, out):
    head_size = gain_ref.shape[1]
    keys, values = (
        sum(part[:, low : low + head_size].astype(jnp.float32) for part in (a, b, c, d)) for low in (0, head_size)
    )
    inverse = lax.rsqrt(jnp.mean(keys * keys, axis=-1, keepdims=True) + 1e-05)
    out[:, :head_size] = (keys * inverse * gain_ref[...]).astype(out.dtype)
    out[:, head_size:] = values.astype(out.dtype)


def normalize(terms, key_gain):
    vmem = pl.BlockSpec(memory_space=pltpu.VMEM)
    return pl.pallas_call(
        normalize_kernel,
        in_specs=[vmem] * 5,
        out_specs=vmem,
        out_shape=jax.ShapeDtypeStruct(terms[0].shape, jnp.bfloat16),
        compiler_params=VMEM,
        name="normalize",
    )(key_gain[None], *terms)


def on_device(
    hidden,
    cross_query,
    image_cache,
    features,
    image_proj,
    key_gain,
    out_weight,
    cross_gate,
    image_spans,
    evicted,
    placement,
):
    head_size = key_gain.shape[0]
    tokens, cols = cross_query.shape
    heads = cols // head_size
    patches = features.shape[1]
    half = patches // 2
    seq_pos = lax.axis_index("seq")
    head_pos = lax.axis_index("head")
    y, x, core = seq_pos // 4, (seq_pos // 2) % 2, seq_pos % 2
    head_x, head_z = head_pos // 4, head_pos % 4
    chunks = 4 * tokens // CHUNK
    rows = heads * CHUNK

    sent_part = lax.dynamic_slice_in_dim(features[0], (1 - core) * half, half)
    peer_part = send_seq(sent_part, core=1)
    stale = jnp.any(placement[:, None] == evicted, axis=1).reshape(8, 2)
    both = jnp.any(stale[:, 0] & stale[:, 1])
    use_own = lax.dynamic_index_in_dim(stale, seq_pos // 2, 0, keepdims=False)[0] == (core == 0)
    part_index = jnp.arange(8, dtype=jnp.int32)
    home = head_at(head_x + part_index % 2, head_z + part_index // 2).astype(jnp.int32)

    def rebuild(own_first, work=None):
        pick = jnp.where(jnp.arange(2) == 0, own_first.astype(jnp.int32), core).astype(jnp.int32)
        summed = sum_over_head(rebuild_parts(features, peer_part, image_proj, home, pick), work)
        summed, rest = (summed, ()) if work is None else (summed[0], (summed[1],))
        mine = normalize(summed, key_gain)
        other = send_seq(mine, x=1)
        return (mine, other, send_seq(mine, core=1), send_seq(other, core=1)) + rest

    held = image_cache[0]
    q_blocks = [cross_query] + [send_seq(cross_query, y=-dy) for dy in (1, 2, 3)]
    held_x = send_seq(held, x=1)
    held_core = send_seq(held, core=1)
    held_both = send_seq(held_x, core=1)

    smem = pl.BlockSpec(memory_space=pltpu.SMEM)
    vmem = pl.BlockSpec(memory_space=pltpu.VMEM)
    order, first_all, stop_all, plan = pl.pallas_call(
        plan_kernel,
        in_specs=[smem] * 3 + [vmem],
        out_specs=[vmem] * 4,
        out_shape=[
            jax.ShapeDtypeStruct((4, tokens, tokens), jnp.bfloat16),
            jax.ShapeDtypeStruct((4 * tokens, head_size), jnp.int32),
            jax.ShapeDtypeStruct((4 * tokens, head_size), jnp.int32),
            jax.ShapeDtypeStruct((PLAN_ROWS, 128), jnp.int32),
        ],
        compiler_params=VMEM,
        name="plan",
    )(seq_pos.reshape(1).astype(jnp.int32), placement, evicted, image_spans.T.reshape(2, 16, tokens))
    state_shapes = [jax.ShapeDtypeStruct((chunks, rows, head_size), jnp.float32)] * 3

    def scratch(keys):
        return [pltpu.VMEM((rows, keys), jnp.float32)] * 2 + [pltpu.VMEM((keys, 2 * head_size), jnp.bfloat16)]

    def attend_first():
        return pl.pallas_call(
            functools.partial(begin_kernel, head_size),
            in_specs=[smem] + [vmem] * 8,
            out_specs=[vmem] * 4,
            out_shape=[jax.ShapeDtypeStruct((chunks, rows, head_size), jnp.bfloat16)] + state_shapes,
            scratch_shapes=scratch(patches),
            compiler_params=VMEM,
            name="attend_first",
        )(plan, *q_blocks, order, first_all, stop_all, held)

    def attend_more(state, low, *kv):
        return state[:1] + pl.pallas_call(
            functools.partial(go_on_kernel, head_size, len(kv), low),
            in_specs=[smem] + [vmem] * (6 + len(kv)),
            out_specs=[vmem] * 3,
            out_shape=state_shapes,
            scratch_shapes=scratch(patches),
            compiler_params=VMEM,
            name="attend_more",
        )(plan, state[0], first_all, stop_all, *state[1:], *kv)

    work = (attend_first, lambda state: attend_more(state, 1, held_core, held_x))
    *once, state = rebuild(use_own, work)
    state = attend_more(state, 3, held_both)
    nothing = jnp.zeros((half, 2 * head_size), jnp.bfloat16)
    twice = lax.cond(
        both,
        lambda: rebuild(~use_own),
        lambda: (nothing,) * 4,
    )
    partial_out = pl.pallas_call(
        functools.partial(rebuilt_kernel, head_size),
        in_specs=[smem] + [vmem] * 15,
        out_specs=[vmem] * 4,
        out_shape=[jax.ShapeDtypeStruct((tokens, cols + 128), jnp.bfloat16)] * 4,
        scratch_shapes=[pltpu.VMEM(s.shape, s.dtype) for s in state_shapes] + scratch(half),
        compiler_params=VMEM,
        name="attend_rebuilt",
    )(plan, state[0], first_all, stop_all, *state[1:], order, *once, *twice)
    arrived = [partial_out[0]] + [send_seq(partial_out[dy], y=dy) for dy in (1, 2, 3)]
    context = pl.pallas_call(
        functools.partial(merge_kernel, head_size),
        in_specs=[vmem] * 4,
        out_specs=vmem,
        out_shape=jax.ShapeDtypeStruct((tokens, cols), jnp.bfloat16),
        compiler_params=VMEM,
        name="merge",
    )(*arrived)

    near, far = gather_chips(context)
    target = head_at(head_x + part_index % 2, head_z + part_index // 2)
    offset = 2 * ((target // 2 - y) % 4) + (target % 2 - x) % 2
    source = jnp.zeros(8, jnp.int32)
    for at, place in enumerate((0, 1, 2, 6, 4, 7, 3, 5)):
        source = jnp.where(offset == place, at, source)
    parts = project_parts(
        (near, far, send_seq(near, core=1), send_seq(far, core=1)),
        out_weight,
        source.astype(jnp.int32),
        core.reshape(1).astype(jnp.int32),
    )
    summed_out = sum(term.astype(jnp.float32) for term in sum_over_head(parts))
    return (hidden.astype(jnp.float32) + jnp.tanh(cross_gate[0]) * summed_out).astype(jnp.bfloat16)


def solution(mesh):
    placed = (
        P("head", "seq"),
        P("seq", "head"),
        P("seq", None, "head"),
        P("seq", None, "head"),
        P("head", None),
        P(),
        P("head", "seq"),
        P(),
        P(),
        P(),
        P(),
    )
    return jax.shard_map(
        on_device, mesh=mesh, in_specs=placed, out_specs=P("head", "seq"), check_vma=False
    )
```

```python
import functools
import math

import jax
import jax.numpy as jnp
from jax import lax
from jax.experimental import pallas as pl
from jax.experimental.pallas import tpu as pltpu
from jax.sharding import PartitionSpec as P

MASKED_SCORE = -1e30
CHUNK = 32
COUNT_ROW = 18
ID_ROW = 19
PLAN_ROWS = 24
VMEM = pltpu.CompilerParams(vmem_limit_bytes=20 * 1024 * 1024)


def seq_at(y, x, core):
    return (y % 4) * 4 + (x % 2) * 2 + core % 2


def head_at(x, z):
    return (x % 2) * 4 + z % 4


def send_seq(array, y=0, x=0, core=0):
    pairs = [
        (seq_at(a, b, c), seq_at(a + y, b + x, c + core)) for a in range(4) for b in range(2) for c in range(2)
    ]
    return lax.ppermute(array, "seq", pairs)


def send_head(array, x=0, z=0):
    return lax.ppermute(array, "head", [(head_at(a, b), head_at(a + x, b + z)) for a in range(2) for b in range(4)])


def add(*terms):
    return sum(term.astype(jnp.float32) for term in terms).astype(jnp.bfloat16)


def add_kernel(a_ref, b_ref, after_ref, out_ref):
    out_ref[...] = (a_ref[...].astype(jnp.float32) + b_ref[...].astype(jnp.float32)).astype(out_ref.dtype)


def add_after(a, b, after):
    vmem = pl.BlockSpec(memory_space=pltpu.VMEM)
    return pl.pallas_call(
        add_kernel,
        in_specs=[vmem, vmem, pl.BlockSpec(memory_space=pl.ANY)],
        out_specs=vmem,
        out_shape=jax.ShapeDtypeStruct(a.shape, a.dtype),
        compiler_params=VMEM,
        name="add_after",
    )(a, b, after)


def sum_over_head(parts, work=None):
    p00, p01, p10, p11, p20, p21, p30, p31 = parts
    via_x = send_head(p21, x=1)
    down = send_head(p31, z=-1)
    across = send_head(p11, x=1)
    last = send_head(p30, z=-1)
    if work is None:
        p20 = add(p20, via_x)
        p01 = add(p01, down)
    else:
        state = work[0]()
        p20 = add_after(p20, via_x, state[-1])
        p01 = add_after(p01, down, state[-1])
    up = send_head(p20, z=1)
    side = send_head(p01, x=1)
    p10 = add(p10, across)
    if work is None:
        p10 = add(p10, up)
    else:
        state = work[1](state)
        p10 = add_after(p10, up, state[-1])
    ahead = send_head(p10, z=1)
    terms = (p00, last, side, ahead)
    return terms if work is None else (terms, work[2](state))


def gather_chips(block):
    r30 = send_seq(block, y=1)
    r01 = send_seq(block, x=1)
    r10 = send_seq(block, y=-1)
    r20 = send_seq(r30, y=1)
    r31 = send_seq(r30, x=1)
    r11 = send_seq(r01, y=-1)
    r21 = send_seq(r20, x=1)
    return jnp.stack([block, r01, r10, r30]), jnp.stack([r20, r31, r11, r21])


def rebuild_kernel(order_ref, pick_ref, own_ref, peer_ref, proj0_ref, proj1_ref, *refs):
    out_refs, rows_ref = refs[:8], refs[8]
    step = pl.program_id(0)

    @pl.when(step == 0)
    def _():
        rows_ref[...] = jnp.where(pick_ref[0] > 0, own_ref[0], peer_ref[...])

    products = [
        jnp.dot(rows_ref[...], proj_ref[...], preferred_element_type=jnp.float32).astype(jnp.bfloat16)
        for proj_ref in (proj0_ref, proj1_ref)
    ]
    for at in range(4):

        @pl.when(step == at)
        def _():
            out_refs[2 * at][...] = products[0]
            out_refs[2 * at + 1][...] = products[1]


def rebuild_parts(features, peer_part, proj, order, pick):
    count, depth = peer_part.shape
    cols = proj.shape[1] // 8
    return pl.pallas_call(
        rebuild_kernel,
        grid_spec=pltpu.PrefetchScalarGridSpec(
            num_scalar_prefetch=2,
            grid=(4,),
            in_specs=[
                pl.BlockSpec((1, count, depth), lambda i, order, pick: (0, pick[1], 0)),
                pl.BlockSpec((count, depth), lambda i, order, pick: (0, 0)),
                pl.BlockSpec((depth, cols), lambda i, order, pick: (0, order[2 * i])),
                pl.BlockSpec((depth, cols), lambda i, order, pick: (0, order[2 * i + 1])),
            ],
            out_specs=[pl.BlockSpec((count, cols), lambda i, order, pick: (0, 0))] * 8,
            scratch_shapes=[pltpu.VMEM((count, depth), jnp.bfloat16)],
        ),
        out_shape=[jax.ShapeDtypeStruct((count, cols), jnp.bfloat16)] * 8,
        compiler_params=VMEM,
        name="rebuild_parts",
    )(order, pick, features, peer_part, proj, proj)


def project_kernel(order_ref, core_ref, own0_ref, own1_ref, other0_ref, other1_ref, weight_ref, *out_refs):
    step = pl.program_id(0)
    even = core_ref[0] == 0
    tokens = own0_ref.shape[1]

    def block(first_ref, second_ref, at):
        return jnp.where(at < 4, first_ref[jnp.minimum(at, 3)], second_ref[jnp.maximum(at - 4, 0)])

    rows = []
    for part in range(2):
        at = order_ref[2 * step + part]
        own, other = block(own0_ref, own1_ref, at), block(other0_ref, other1_ref, at)
        rows += [jnp.where(even, own, other), jnp.where(even, other, own)]
    product = jnp.dot(
        jnp.concatenate(rows, axis=0), weight_ref[...], preferred_element_type=jnp.float32
    ).astype(jnp.bfloat16)
    for at in range(4):

        @pl.when(step == at)
        def _():
            out_refs[2 * at][...] = product[: 2 * tokens]
            out_refs[2 * at + 1][...] = product[2 * tokens :]


def project_parts(blocks, weight, order, core):
    _, tokens, depth = blocks[0].shape
    cols = weight.shape[1]
    return pl.pallas_call(
        project_kernel,
        grid_spec=pltpu.PrefetchScalarGridSpec(
            num_scalar_prefetch=2,
            grid=(4,),
            in_specs=[pl.BlockSpec((4, tokens, depth), lambda i, order, core: (0, 0, 0))] * 4
            + [pl.BlockSpec((depth, cols), lambda i, order, core: (0, 0))],
            out_specs=[pl.BlockSpec((2 * tokens, cols), lambda i, order, core: (0, 0))] * 8,
        ),
        out_shape=[jax.ShapeDtypeStruct((2 * tokens, cols), jnp.bfloat16)] * 8,
        compiler_params=VMEM,
        name="project_parts",
    )(order, core, *blocks, weight)


def plan_kernel(pos_ref, placement_ref, evicted_ref, spans_ref, order_ref, first_ref, stop_ref, plan_ref):
    seq_pos = pos_ref[0]
    y, x, core = seq_pos // 4, (seq_pos // 2) % 2, seq_pos % 2
    tokens = spans_ref.shape[2]
    chips = (seq_pos // 2, seq_at(y, x + 1, 0) // 2)

    def stale(slot):
        image = placement_ref[slot]
        return (image == evicted_ref[0]) | (image == evicted_ref[1])

    entries = []
    for chip in chips:
        for slot in (2 * chip + core, 2 * chip + 1 - core):
            entries.append((placement_ref[slot], ~stale(slot)))
    once, twice = [], []
    for chip in chips:
        low, high = stale(2 * chip), stale(2 * chip + 1)
        once.append((jnp.where(low, placement_ref[2 * chip], placement_ref[2 * chip + 1]), low | high))
        twice.append((placement_ref[2 * chip + 1], low & high))
    entries += once * 2 + twice * 2
    slot_lane = lax.broadcasted_iota(jnp.int32, (CHUNK, 128), 1)
    ids = jnp.full((CHUNK, 128), -1, jnp.int32)
    for at, (image, live) in enumerate(entries):
        ids = jnp.where(slot_lane == at, jnp.where(live, image, -1), ids)

    up = lax.broadcasted_iota(jnp.int32, (tokens, tokens), 0)
    along = lax.broadcasted_iota(jnp.int32, (tokens, tokens), 1)
    wanted = []
    for dy in range(4):
        block = seq_at(y + dy, x, core)
        first = jnp.broadcast_to(spans_ref[0, pl.ds(block, 1), :].astype(jnp.float32), (tokens, tokens))
        stop = jnp.broadcast_to(spans_ref[1, pl.ds(block, 1), :].astype(jnp.float32), (tokens, tokens))
        down = jnp.sum(jnp.where(up == along, first, 0.0), axis=1, keepdims=True)
        earlier = (down < first) | ((down == first) & (up < along))
        rank = jnp.sum(jnp.where(earlier, 1.0, 0.0), axis=0, keepdims=True).astype(jnp.int32)
        order = jnp.where(up == rank, 1.0, 0.0)
        order_ref[dy] = order.astype(jnp.bfloat16)
        first = jnp.broadcast_to(jnp.sum(order * first, axis=1, keepdims=True), (tokens, 128)).astype(jnp.int32)
        stop = jnp.broadcast_to(jnp.sum(order * stop, axis=1, keepdims=True), (tokens, 128)).astype(jnp.int32)
        first_ref[dy * tokens : (dy + 1) * tokens, :] = first
        stop_ref[dy * tokens : (dy + 1) * tokens, :] = stop
        for part in range(tokens // CHUNK):
            rows = slice(part * CHUNK, (part + 1) * CHUNK)
            seen = (first[rows] <= ids) & (ids < stop[rows])
            wanted.append(jnp.max(jnp.where(seen, 1, 0), axis=0, keepdims=True))
    places, total = [], jnp.zeros((1, 128), jnp.int32)
    for want in wanted:
        places.append(total)
        total = total + want
    for place in range(COUNT_ROW):
        row = jnp.zeros((1, 128), jnp.int32)
        for chunk, (want, at) in enumerate(zip(wanted, places)):
            row = jnp.where((want > 0) & (at == place), chunk, row)
        plan_ref[place : place + 1, :] = row
    plan_ref[COUNT_ROW : COUNT_ROW + 1, :] = total
    plan_ref[ID_ROW : ID_ROW + 1, :] = ids[:1]
    plan_ref[ID_ROW + 1 :, :] = jnp.zeros((PLAN_ROWS - ID_ROW - 1, 128), jnp.int32)


def sweep(head_size, plan_ref, low, q_ref, first_ref, stop_ref, kv_parts, state, even, odd, wide):
    factor = math.log2(math.e) * head_size ** (-0.5)
    heads = q_ref.shape[1] // CHUNK
    m_ref, l_ref, acc_ref = state

    for slot, part in enumerate(kv_parts, low):
        count = plan_ref[COUNT_ROW, slot]

        def score(place, into):
            into[...] = lax.dot_general(
                q_ref[plan_ref[place, slot]],
                part()[:, :head_size],
                (((1,), (1,)), ((), ())),
                preferred_element_type=jnp.float32,
            )

        def take(place, scores_ref):
            chunk = plan_ref[place, slot]
            image = jnp.where(place < count, plan_ref[ID_ROW, slot], -1)
            scores = scores_ref[...]
            here = jnp.broadcast_to(jnp.max(scores, axis=1, keepdims=True), (scores.shape[0], head_size))
            weights = jnp.exp2((scores - here[:, :1]) * factor)
            both = jnp.dot(weights.astype(jnp.bfloat16), wide[...], preferred_element_type=jnp.float32)
            mixed, total = both[:, :head_size], both[:, head_size:]
            tokens = pl.ds(pl.multiple_of(chunk * CHUNK, CHUNK), CHUNK)
            seen = (first_ref[tokens, :] <= image) & (image < stop_ref[tokens, :])
            seen = jnp.concatenate([seen.astype(jnp.int32)] * heads, axis=0) > 0
            before = m_ref[chunk]
            after = jnp.where(seen, jnp.maximum(before, here), before)
            keep = jnp.exp2((before - after) * factor)
            gain = jnp.where(seen, jnp.exp2((here - after) * factor), 0.0)
            m_ref[chunk] = after
            l_ref[chunk] = l_ref[chunk] * keep + gain * total
            acc_ref[chunk] = acc_ref[chunk] * keep + gain * mixed

        @pl.when(count > 0)
        def _():
            wide[:, :head_size] = part()[:, head_size:]
            wide[:, head_size:] = jnp.ones_like(wide[:, head_size:])
            score(0, even)

            def body(at, carry):
                place = 2 * at
                score(place + 1, odd)
                take(place, even)
                score(place + 2, even)
                take(place + 1, odd)
                return carry

            lax.fori_loop(0, (count + 1) // 2, body, 0)


def begin_kernel(head_size, plan, q0, q1, q2, q3, order, first, stop, a, qs, m, l, acc, even, odd, wide):
    heads = q0.shape[1] // head_size
    per_block = q0.shape[0] // CHUNK
    for block, q_ref in enumerate((q0, q1, q2, q3)):
        ordered = jnp.dot(order[block], q_ref[...], preferred_element_type=jnp.float32).astype(jnp.bfloat16)
        for part in range(per_block):
            for head in range(heads):
                qs[block * per_block + part, head * CHUNK : (head + 1) * CHUNK, :] = ordered[
                    part * CHUNK : (part + 1) * CHUNK, head * head_size : (head + 1) * head_size
                ]
    m[...] = jnp.full_like(m, MASKED_SCORE)
    l[...] = jnp.zeros_like(l)
    acc[...] = jnp.zeros_like(acc)
    sweep(head_size, plan, 0, qs, first, stop, [lambda: a[...]], (m, l, acc), even, odd, wide)


def go_on_kernel(head_size, parts, low, plan, qs, first, stop, m_in, l_in, acc_in, *refs):
    kv, (m, l, acc, even, odd, wide) = refs[:parts], refs[parts:]
    m[...] = m_in[...]
    l[...] = l_in[...]
    acc[...] = acc_in[...]
    sweep(head_size, plan, low, qs, first, stop, [lambda r=r: r[...] for r in kv], (m, l, acc), even, odd, wide)


def rebuilt_kernel(head_size, parts, plan, qs, first, stop, m_in, l_in, acc_in, order, *refs):
    kv, (o0, o1, o2, o3, m, l, acc, even, odd, wide) = refs[:parts], refs[parts:]
    factor = math.log2(math.e) * head_size ** (-0.5)
    tokens = o0.shape[0]
    heads = qs.shape[1] // CHUNK
    per_block = tokens // CHUNK
    m[...] = m_in[...]
    l[...] = l_in[...]
    acc[...] = acc_in[...]
    kv_parts = [lambda r=r: r[...] for r in kv]
    sweep(head_size, plan, 4, qs, first, stop, kv_parts, (m, l, acc), even, odd, wide)
    lanes = lax.broadcasted_iota(jnp.int32, (tokens, 128), 1)
    for block, out in enumerate((o0, o1, o2, o3)):
        extra = jnp.zeros((tokens, 128), jnp.float32)
        for head in range(heads):
            rows = slice(head * CHUNK, (head + 1) * CHUNK)
            chunks = range(block * per_block, (block + 1) * per_block)
            high = jnp.concatenate([m[chunk, rows, :] for chunk in chunks], axis=0)
            total = jnp.concatenate([l[chunk, rows, :] for chunk in chunks], axis=0)
            mixed = jnp.concatenate([acc[chunk, rows, :] for chunk in chunks], axis=0)
            some = total > 0.0
            safe = jnp.where(some, total, 1.0)
            level = jnp.where(some, high * factor + jnp.log2(safe), MASKED_SCORE)
            ordered = (mixed / safe).astype(jnp.bfloat16)
            out[:, head * head_size : (head + 1) * head_size] = lax.dot_general(
                order[block], ordered, (((0,), (0,)), ((), ())), preferred_element_type=jnp.float32
            ).astype(jnp.bfloat16)
            for piece in range(3):
                rounded = level.astype(jnp.bfloat16).astype(jnp.float32)
                extra = jnp.where(lanes == piece * heads + head, rounded, extra)
                level = level - rounded
        out[:, heads * head_size :] = lax.dot_general(
            order[block], extra.astype(jnp.bfloat16), (((0,), (0,)), ((), ())), preferred_element_type=jnp.float32
        ).astype(jnp.bfloat16)


def merge_kernel(head_size, a, b, c, d, out):
    heads = out.shape[1] // head_size
    parts = (a, b, c, d)
    extras = [part[:, heads * head_size :].astype(jnp.float32) for part in parts]
    for head in range(heads):
        cols = slice(head * head_size, (head + 1) * head_size)
        levels = [sum(e[:, p * heads + head : p * heads + head + 1] for p in range(3)) for e in extras]
        top = functools.reduce(jnp.maximum, levels)
        shares = [jnp.exp2(level - top) for level in levels]
        mixed = sum(share * part[:, cols].astype(jnp.float32) for share, part in zip(shares, parts))
        out[:, cols] = (mixed / sum(shares)).astype(jnp.bfloat16)


def normalize_kernel(gain_ref, after_ref, a, b, c, d, out):
    head_size = gain_ref.shape[1]
    keys, values = (
        sum(part[:, low : low + head_size].astype(jnp.float32) for part in (a, b, c, d)) for low in (0, head_size)
    )
    inverse = lax.rsqrt(jnp.mean(keys * keys, axis=-1, keepdims=True) + 1e-05)
    out[:, :head_size] = (keys * inverse * gain_ref[...]).astype(out.dtype)
    out[:, head_size:] = values.astype(out.dtype)


def normalize(terms, key_gain, after):
    vmem = pl.BlockSpec(memory_space=pltpu.VMEM)
    return pl.pallas_call(
        normalize_kernel,
        in_specs=[vmem, pl.BlockSpec(memory_space=pl.ANY)] + [vmem] * 4,
        out_specs=vmem,
        out_shape=jax.ShapeDtypeStruct(terms[0].shape, jnp.bfloat16),
        compiler_params=VMEM,
        name="normalize",
    )(key_gain[None], after, *terms)


def on_device(
    hidden,
    cross_query,
    image_cache,
    features,
    image_proj,
    key_gain,
    out_weight,
    cross_gate,
    image_spans,
    evicted,
    placement,
):
    head_size = key_gain.shape[0]
    tokens, cols = cross_query.shape
    heads = cols // head_size
    patches = features.shape[1]
    half = patches // 2
    seq_pos = lax.axis_index("seq")
    head_pos = lax.axis_index("head")
    y, x, core = seq_pos // 4, (seq_pos // 2) % 2, seq_pos % 2
    head_x, head_z = head_pos // 4, head_pos % 4
    chunks = 4 * tokens // CHUNK
    rows = heads * CHUNK

    sent_part = lax.dynamic_slice_in_dim(features[0], (1 - core) * half, half)
    peer_part = send_seq(sent_part, core=1)
    stale = jnp.any(placement[:, None] == evicted, axis=1).reshape(8, 2)
    both = jnp.any(stale[:, 0] & stale[:, 1])
    use_own = lax.dynamic_index_in_dim(stale, seq_pos // 2, 0, keepdims=False)[0] == (core == 0)
    part_index = jnp.arange(8, dtype=jnp.int32)
    home = head_at(head_x + part_index % 2, head_z + part_index // 2).astype(jnp.int32)

    def rebuild(own_first, work=None):
        pick = jnp.where(jnp.arange(2) == 0, own_first.astype(jnp.int32), core).astype(jnp.int32)
        summed = sum_over_head(rebuild_parts(features, peer_part, image_proj, home, pick), work)
        summed, rest = (summed, ()) if work is None else (summed[0], (summed[1],))
        mine = normalize(summed, key_gain, rest[0][-1] if rest else peer_part)
        other = send_seq(mine, x=1)
        return (mine, other, send_seq(mine, core=1), send_seq(other, core=1)) + rest

    smem = pl.BlockSpec(memory_space=pltpu.SMEM)
    vmem = pl.BlockSpec(memory_space=pltpu.VMEM)
    order, first_all, stop_all, plan = pl.pallas_call(
        plan_kernel,
        in_specs=[smem] * 3 + [vmem],
        out_specs=[vmem] * 4,
        out_shape=[
            jax.ShapeDtypeStruct((4, tokens, tokens), jnp.bfloat16),
            jax.ShapeDtypeStruct((4 * tokens, head_size), jnp.int32),
            jax.ShapeDtypeStruct((4 * tokens, head_size), jnp.int32),
            jax.ShapeDtypeStruct((PLAN_ROWS, 128), jnp.int32),
        ],
        compiler_params=VMEM,
        name="plan",
    )(seq_pos.reshape(1).astype(jnp.int32), placement, evicted, image_spans.T.reshape(2, 16, tokens))
    state_shapes = [jax.ShapeDtypeStruct((chunks, rows, head_size), jnp.float32)] * 3

    def scratch(keys):
        return [pltpu.VMEM((rows, keys), jnp.float32)] * 2 + [pltpu.VMEM((keys, 2 * head_size), jnp.bfloat16)]

    def attend_all(rounds):
        held = image_cache[0]
        q_blocks = [cross_query] + [send_seq(cross_query, y=-dy) for dy in (1, 2, 3)]
        held_x = send_seq(held, x=1)
        held_core = send_seq(held, core=1)
        held_both = send_seq(held_x, core=1)

        def attend_first():
            return pl.pallas_call(
                functools.partial(begin_kernel, head_size),
                in_specs=[smem] + [vmem] * 8,
                out_specs=[vmem] * 4,
                out_shape=[jax.ShapeDtypeStruct((chunks, rows, head_size), jnp.bfloat16)] + state_shapes,
                scratch_shapes=scratch(patches),
                compiler_params=VMEM,
                name="attend_first",
            )(plan, *q_blocks, order, first_all, stop_all, held)

        def attend_more(state, low, *kv):
            return state[:1] + pl.pallas_call(
                functools.partial(go_on_kernel, head_size, len(kv), low),
                in_specs=[smem] + [vmem] * (6 + len(kv)),
                out_specs=[vmem] * 3,
                out_shape=state_shapes,
                scratch_shapes=scratch(patches),
                compiler_params=VMEM,
                name="attend_more",
            )(plan, state[0], first_all, stop_all, *state[1:], *kv)

        work = (
            attend_first,
            lambda state: attend_more(state, 1, held_core, held_x),
            lambda state: attend_more(state, 3, held_both),
        )
        *rebuilt, state = rebuild(use_own, work)
        if rounds == 2:
            rebuilt += rebuild(~use_own)
        return pl.pallas_call(
            functools.partial(rebuilt_kernel, head_size, len(rebuilt)),
            in_specs=[smem] + [vmem] * (7 + len(rebuilt)),
            out_specs=[vmem] * 4,
            out_shape=[jax.ShapeDtypeStruct((tokens, cols + 128), jnp.bfloat16)] * 4,
            scratch_shapes=[pltpu.VMEM(s.shape, s.dtype) for s in state_shapes] + scratch(half),
            compiler_params=VMEM,
            name="attend_rebuilt",
        )(plan, state[0], first_all, stop_all, *state[1:], order, *rebuilt)

    partial_out = lax.cond(both, lambda: attend_all(2), lambda: attend_all(1))
    arrived = [partial_out[0]] + [send_seq(partial_out[dy], y=dy) for dy in (1, 2, 3)]
    context = pl.pallas_call(
        functools.partial(merge_kernel, head_size),
        in_specs=[vmem] * 4,
        out_specs=vmem,
        out_shape=jax.ShapeDtypeStruct((tokens, cols), jnp.bfloat16),
        compiler_params=VMEM,
        name="merge",
    )(*arrived)

    near, far = gather_chips(context)
    target = head_at(head_x + part_index % 2, head_z + part_index // 2)
    offset = 2 * ((target // 2 - y) % 4) + (target % 2 - x) % 2
    source = jnp.zeros(8, jnp.int32)
    for at, place in enumerate((0, 1, 2, 6, 4, 7, 3, 5)):
        source = jnp.where(offset == place, at, source)
    parts = project_parts(
        (near, far, send_seq(near, core=1), send_seq(far, core=1)),
        out_weight,
        source.astype(jnp.int32),
        core.reshape(1).astype(jnp.int32),
    )
    summed_out = sum(term.astype(jnp.float32) for term in sum_over_head(parts))
    return (hidden.astype(jnp.float32) + jnp.tanh(cross_gate[0]) * summed_out).astype(jnp.bfloat16)


def solution(mesh):
    placed = (
        P("head", "seq"),
        P("seq", "head"),
        P("seq", None, "head"),
        P("seq", None, "head"),
        P("head", None),
        P(),
        P("head", "seq"),
        P(),
        P(),
        P(),
        P(),
    )
    return jax.shard_map(
        on_device, mesh=mesh, in_specs=placed, out_specs=P("head", "seq"), check_vma=False
    )
```

```python
import functools
import math

import jax
import jax.numpy as jnp
from jax import lax
from jax.experimental import pallas as pl
from jax.experimental.pallas import tpu as pltpu
from jax.sharding import PartitionSpec as P

MASKED_SCORE = -1e30
CHUNK = 32
COUNT_ROW = 18
ID_ROW = 19
PLAN_ROWS = 24
VMEM = pltpu.CompilerParams(vmem_limit_bytes=20 * 1024 * 1024)


def seq_at(y, x, core):
    return (y % 4) * 4 + (x % 2) * 2 + core % 2


def head_at(x, z):
    return (x % 2) * 4 + z % 4


def send_seq(array, y=0, x=0, core=0):
    pairs = [
        (seq_at(a, b, c), seq_at(a + y, b + x, c + core)) for a in range(4) for b in range(2) for c in range(2)
    ]
    return lax.ppermute(array, "seq", pairs)


def send_head(array, x=0, z=0):
    return lax.ppermute(array, "head", [(head_at(a, b), head_at(a + x, b + z)) for a in range(2) for b in range(4)])


def add(*terms):
    return sum(term.astype(jnp.float32) for term in terms).astype(jnp.bfloat16)


def add_kernel(*refs):
    *terms, _, out_ref = refs
    out_ref[...] = sum(term[...].astype(jnp.float32) for term in terms).astype(out_ref.dtype)


def add_after(after, *terms):
    vmem = pl.BlockSpec(memory_space=pltpu.VMEM)
    return pl.pallas_call(
        add_kernel,
        in_specs=[vmem] * len(terms) + [pl.BlockSpec(memory_space=pl.ANY)],
        out_specs=vmem,
        out_shape=jax.ShapeDtypeStruct(terms[0].shape, terms[0].dtype),
        compiler_params=VMEM,
        name="add_after",
    )(*terms, after)


def sum_over_head(parts):
    p00, p01, p10, p11, p20, p21, p30, p31 = parts
    via_x = send_head(p21, x=1)
    down = send_head(p31, z=-1)
    across = send_head(p11, x=1)
    last = send_head(p30, z=-1)
    p20 = add(p20, via_x)
    p01 = add(p01, down)
    up = send_head(p20, z=1)
    side = send_head(p01, x=1)
    p10 = add(p10, across, up)
    ahead = send_head(p10, z=1)
    return p00, last, side, ahead


def sum_beside(parts, work):
    p00, p01, p10, p11, p20, p21, p30, p31 = parts
    up = send_head(p20, z=1)
    down = send_head(p21, z=-1)
    across = send_head(p11, z=1)
    last = send_head(p30, z=-1)
    state = work[0]()
    p10 = add_after(state[-1], p10, up)
    p31 = add_after(state[-1], p31, down)
    ahead = send_head(p10, z=1)
    behind = send_head(p31, z=-1)
    state = work[1](state)
    p01 = add_after(state[-1], p01, across, behind)
    side = send_head(p01, x=1)
    state = work[2](state)
    return (p00, last, ahead, side), state


def gather_chips(block):
    r30 = send_seq(block, y=1)
    r01 = send_seq(block, x=1)
    r10 = send_seq(block, y=-1)
    r20 = send_seq(r30, y=1)
    r31 = send_seq(r30, x=1)
    r11 = send_seq(r01, y=-1)
    r21 = send_seq(r20, x=1)
    return jnp.stack([block, r01, r10, r30]), jnp.stack([r20, r31, r11, r21])


def rebuild_kernel(order_ref, pick_ref, own_ref, peer_ref, proj0_ref, proj1_ref, *refs):
    *out_refs, rows_ref = refs[-9:]
    step = pl.program_id(0)

    @pl.when(step == 0)
    def _():
        rows_ref[...] = jnp.where(pick_ref[0] > 0, own_ref[0], peer_ref[...])

    products = [
        jnp.dot(rows_ref[...], proj_ref[...], preferred_element_type=jnp.float32).astype(jnp.bfloat16)
        for proj_ref in (proj0_ref, proj1_ref)
    ]
    for at in range(4):

        @pl.when(step == at)
        def _():
            out_refs[2 * at][...] = products[0]
            out_refs[2 * at + 1][...] = products[1]


def rebuild_parts(features, peer_part, proj, order, pick, after):
    count, depth = peer_part.shape
    cols = proj.shape[1] // 8
    return pl.pallas_call(
        rebuild_kernel,
        grid_spec=pltpu.PrefetchScalarGridSpec(
            num_scalar_prefetch=2,
            grid=(4,),
            in_specs=[
                pl.BlockSpec((1, count, depth), lambda i, order, pick: (0, pick[1], 0)),
                pl.BlockSpec((count, depth), lambda i, order, pick: (0, 0)),
                pl.BlockSpec((depth, cols), lambda i, order, pick: (0, order[2 * i])),
                pl.BlockSpec((depth, cols), lambda i, order, pick: (0, order[2 * i + 1])),
            ]
            + [pl.BlockSpec(memory_space=pl.ANY)] * len(after),
            out_specs=[pl.BlockSpec((count, cols), lambda i, order, pick: (0, 0))] * 8,
            scratch_shapes=[pltpu.VMEM((count, depth), jnp.bfloat16)],
        ),
        out_shape=[jax.ShapeDtypeStruct((count, cols), jnp.bfloat16)] * 8,
        compiler_params=VMEM,
        name="rebuild_parts",
    )(order, pick, features, peer_part, proj, proj, *after)


def project_kernel(order_ref, core_ref, own0_ref, own1_ref, other0_ref, other1_ref, weight_ref, *out_refs):
    step = pl.program_id(0)
    even = core_ref[0] == 0
    tokens = own0_ref.shape[1]

    def block(first_ref, second_ref, at):
        return jnp.where(at < 4, first_ref[jnp.minimum(at, 3)], second_ref[jnp.maximum(at - 4, 0)])

    rows = []
    for part in range(2):
        at = order_ref[2 * step + part]
        own, other = block(own0_ref, own1_ref, at), block(other0_ref, other1_ref, at)
        rows += [jnp.where(even, own, other), jnp.where(even, other, own)]
    product = jnp.dot(
        jnp.concatenate(rows, axis=0), weight_ref[...], preferred_element_type=jnp.float32
    ).astype(jnp.bfloat16)
    for at in range(4):

        @pl.when(step == at)
        def _():
            out_refs[2 * at][...] = product[: 2 * tokens]
            out_refs[2 * at + 1][...] = product[2 * tokens :]


def project_parts(blocks, weight, order, core):
    _, tokens, depth = blocks[0].shape
    cols = weight.shape[1]
    return pl.pallas_call(
        project_kernel,
        grid_spec=pltpu.PrefetchScalarGridSpec(
            num_scalar_prefetch=2,
            grid=(4,),
            in_specs=[pl.BlockSpec((4, tokens, depth), lambda i, order, core: (0, 0, 0))] * 4
            + [pl.BlockSpec((depth, cols), lambda i, order, core: (0, 0))],
            out_specs=[pl.BlockSpec((2 * tokens, cols), lambda i, order, core: (0, 0))] * 8,
        ),
        out_shape=[jax.ShapeDtypeStruct((2 * tokens, cols), jnp.bfloat16)] * 8,
        compiler_params=VMEM,
        name="project_parts",
    )(order, core, *blocks, weight)


def plan_kernel(pos_ref, placement_ref, evicted_ref, spans_ref, order_ref, first_ref, stop_ref, plan_ref):
    seq_pos = pos_ref[0]
    y, x, core = seq_pos // 4, (seq_pos // 2) % 2, seq_pos % 2
    tokens = spans_ref.shape[2]
    chips = (seq_pos // 2, seq_at(y, x + 1, 0) // 2)

    def stale(slot):
        image = placement_ref[slot]
        return (image == evicted_ref[0]) | (image == evicted_ref[1])

    entries = []
    for chip in chips:
        for slot in (2 * chip + core, 2 * chip + 1 - core):
            entries.append((placement_ref[slot], ~stale(slot)))
    once, twice = [], []
    for chip in chips:
        low, high = stale(2 * chip), stale(2 * chip + 1)
        once.append((jnp.where(low, placement_ref[2 * chip], placement_ref[2 * chip + 1]), low | high))
        twice.append((placement_ref[2 * chip + 1], low & high))
    entries += once * 2 + twice * 2
    slot_lane = lax.broadcasted_iota(jnp.int32, (CHUNK, 128), 1)
    ids = jnp.full((CHUNK, 128), -1, jnp.int32)
    for at, (image, live) in enumerate(entries):
        ids = jnp.where(slot_lane == at, jnp.where(live, image, -1), ids)

    up = lax.broadcasted_iota(jnp.int32, (tokens, tokens), 0)
    along = lax.broadcasted_iota(jnp.int32, (tokens, tokens), 1)
    wanted = []
    for dy in range(4):
        block = seq_at(y + dy, x, core)
        first = jnp.broadcast_to(spans_ref[0, pl.ds(block, 1), :].astype(jnp.float32), (tokens, tokens))
        stop = jnp.broadcast_to(spans_ref[1, pl.ds(block, 1), :].astype(jnp.float32), (tokens, tokens))
        down = jnp.sum(jnp.where(up == along, first, 0.0), axis=1, keepdims=True)
        earlier = (down < first) | ((down == first) & (up < along))
        rank = jnp.sum(jnp.where(earlier, 1.0, 0.0), axis=0, keepdims=True).astype(jnp.int32)
        order = jnp.where(up == rank, 1.0, 0.0)
        order_ref[dy] = order.astype(jnp.bfloat16)
        first = jnp.broadcast_to(jnp.sum(order * first, axis=1, keepdims=True), (tokens, 128)).astype(jnp.int32)
        stop = jnp.broadcast_to(jnp.sum(order * stop, axis=1, keepdims=True), (tokens, 128)).astype(jnp.int32)
        first_ref[dy * tokens : (dy + 1) * tokens, :] = first
        stop_ref[dy * tokens : (dy + 1) * tokens, :] = stop
        for part in range(tokens // CHUNK):
            rows = slice(part * CHUNK, (part + 1) * CHUNK)
            seen = (first[rows] <= ids) & (ids < stop[rows])
            wanted.append(jnp.max(jnp.where(seen, 1, 0), axis=0, keepdims=True))
    places, total = [], jnp.zeros((1, 128), jnp.int32)
    for want in wanted:
        places.append(total)
        total = total + want
    for place in range(COUNT_ROW):
        row = jnp.zeros((1, 128), jnp.int32)
        for chunk, (want, at) in enumerate(zip(wanted, places)):
            row = jnp.where((want > 0) & (at == place), chunk, row)
        plan_ref[place : place + 1, :] = row
    plan_ref[COUNT_ROW : COUNT_ROW + 1, :] = total
    plan_ref[ID_ROW : ID_ROW + 1, :] = ids[:1]
    plan_ref[ID_ROW + 1 :, :] = jnp.zeros((PLAN_ROWS - ID_ROW - 1, 128), jnp.int32)


def sweep(head_size, plan_ref, low, q_ref, first_ref, stop_ref, kv_parts, state, even, odd, wide):
    factor = math.log2(math.e) * head_size ** (-0.5)
    heads = q_ref.shape[1] // CHUNK
    m_ref, l_ref, acc_ref = state

    for slot, part in enumerate(kv_parts, low):
        count = plan_ref[COUNT_ROW, slot]

        def score(place, into):
            into[...] = lax.dot_general(
                q_ref[plan_ref[place, slot]],
                part()[:, :head_size],
                (((1,), (1,)), ((), ())),
                preferred_element_type=jnp.float32,
            )

        def take(place, scores_ref):
            chunk = plan_ref[place, slot]
            image = jnp.where(place < count, plan_ref[ID_ROW, slot], -1)
            scores = scores_ref[...]
            here = jnp.broadcast_to(jnp.max(scores, axis=1, keepdims=True), (scores.shape[0], head_size))
            weights = jnp.exp2((scores - here[:, :1]) * factor)
            both = jnp.dot(weights.astype(jnp.bfloat16), wide[...], preferred_element_type=jnp.float32)
            mixed, total = both[:, :head_size], both[:, head_size:]
            tokens = pl.ds(pl.multiple_of(chunk * CHUNK, CHUNK), CHUNK)
            seen = (first_ref[tokens, :] <= image) & (image < stop_ref[tokens, :])
            seen = jnp.concatenate([seen.astype(jnp.int32)] * heads, axis=0) > 0
            before = m_ref[chunk]
            after = jnp.where(seen, jnp.maximum(before, here), before)
            keep = jnp.exp2((before - after) * factor)
            gain = jnp.where(seen, jnp.exp2((here - after) * factor), 0.0)
            m_ref[chunk] = after
            l_ref[chunk] = l_ref[chunk] * keep + gain * total
            acc_ref[chunk] = acc_ref[chunk] * keep + gain * mixed

        @pl.when(count > 0)
        def _():
            wide[:, :head_size] = part()[:, head_size:]
            wide[:, head_size:] = jnp.ones_like(wide[:, head_size:])
            score(0, even)

            def body(at, carry):
                place = 2 * at
                score(place + 1, odd)
                take(place, even)
                score(place + 2, even)
                take(place + 1, odd)
                return carry

            lax.fori_loop(0, (count + 1) // 2, body, 0)


def begin_kernel(head_size, plan, q0, q1, q2, q3, order, first, stop, a, qs, m, l, acc, even, odd, wide):
    heads = q0.shape[1] // head_size
    per_block = q0.shape[0] // CHUNK
    for block, q_ref in enumerate((q0, q1, q2, q3)):
        ordered = jnp.dot(order[block], q_ref[...], preferred_element_type=jnp.float32).astype(jnp.bfloat16)
        for part in range(per_block):
            for head in range(heads):
                qs[block * per_block + part, head * CHUNK : (head + 1) * CHUNK, :] = ordered[
                    part * CHUNK : (part + 1) * CHUNK, head * head_size : (head + 1) * head_size
                ]
    m[...] = jnp.full_like(m, MASKED_SCORE)
    l[...] = jnp.zeros_like(l)
    acc[...] = jnp.zeros_like(acc)
    sweep(head_size, plan, 0, qs, first, stop, [lambda: a[...]], (m, l, acc), even, odd, wide)


def go_on_kernel(head_size, parts, low, plan, qs, first, stop, m_in, l_in, acc_in, *refs):
    kv, (m, l, acc, even, odd, wide) = refs[:parts], refs[parts:]
    m[...] = m_in[...]
    l[...] = l_in[...]
    acc[...] = acc_in[...]
    sweep(head_size, plan, low, qs, first, stop, [lambda r=r: r[...] for r in kv], (m, l, acc), even, odd, wide)


def rebuilt_kernel(head_size, parts, plan, qs, first, stop, m_in, l_in, acc_in, order, *refs):
    kv, (o0, o1, o2, o3, m, l, acc, even, odd, wide) = refs[:parts], refs[parts:]
    factor = math.log2(math.e) * head_size ** (-0.5)
    tokens = o0.shape[0]
    heads = qs.shape[1] // CHUNK
    per_block = tokens // CHUNK
    m[...] = m_in[...]
    l[...] = l_in[...]
    acc[...] = acc_in[...]
    kv_parts = [lambda r=r: r[...] for r in kv]
    sweep(head_size, plan, 4, qs, first, stop, kv_parts, (m, l, acc), even, odd, wide)
    lanes = lax.broadcasted_iota(jnp.int32, (tokens, 128), 1)
    for block, out in enumerate((o0, o1, o2, o3)):
        extra = jnp.zeros((tokens, 128), jnp.float32)
        for head in range(heads):
            rows = slice(head * CHUNK, (head + 1) * CHUNK)
            chunks = range(block * per_block, (block + 1) * per_block)
            high = jnp.concatenate([m[chunk, rows, :] for chunk in chunks], axis=0)
            total = jnp.concatenate([l[chunk, rows, :] for chunk in chunks], axis=0)
            mixed = jnp.concatenate([acc[chunk, rows, :] for chunk in chunks], axis=0)
            some = total > 0.0
            safe = jnp.where(some, total, 1.0)
            level = jnp.where(some, high * factor + jnp.log2(safe), MASKED_SCORE)
            ordered = (mixed / safe).astype(jnp.bfloat16)
            out[:, head * head_size : (head + 1) * head_size] = lax.dot_general(
                order[block], ordered, (((0,), (0,)), ((), ())), preferred_element_type=jnp.float32
            ).astype(jnp.bfloat16)
            for piece in range(3):
                rounded = level.astype(jnp.bfloat16).astype(jnp.float32)
                extra = jnp.where(lanes == piece * heads + head, rounded, extra)
                level = level - rounded
        out[:, heads * head_size :] = lax.dot_general(
            order[block], extra.astype(jnp.bfloat16), (((0,), (0,)), ((), ())), preferred_element_type=jnp.float32
        ).astype(jnp.bfloat16)


def merge_kernel(head_size, a, b, c, d, out):
    heads = out.shape[1] // head_size
    parts = (a, b, c, d)
    extras = [part[:, heads * head_size :].astype(jnp.float32) for part in parts]
    for head in range(heads):
        cols = slice(head * head_size, (head + 1) * head_size)
        levels = [sum(e[:, p * heads + head : p * heads + head + 1] for p in range(3)) for e in extras]
        top = functools.reduce(jnp.maximum, levels)
        shares = [jnp.exp2(level - top) for level in levels]
        mixed = sum(share * part[:, cols].astype(jnp.float32) for share, part in zip(shares, parts))
        out[:, cols] = (mixed / sum(shares)).astype(jnp.bfloat16)


def normalize_kernel(gain_ref, after_ref, a, b, c, d, out):
    head_size = gain_ref.shape[1]
    keys, values = (
        sum(part[:, low : low + head_size].astype(jnp.float32) for part in (a, b, c, d)) for low in (0, head_size)
    )
    inverse = lax.rsqrt(jnp.mean(keys * keys, axis=-1, keepdims=True) + 1e-05)
    out[:, :head_size] = (keys * inverse * gain_ref[...]).astype(out.dtype)
    out[:, head_size:] = values.astype(out.dtype)


def normalize(terms, key_gain, after):
    vmem = pl.BlockSpec(memory_space=pltpu.VMEM)
    return pl.pallas_call(
        normalize_kernel,
        in_specs=[vmem, pl.BlockSpec(memory_space=pl.ANY)] + [vmem] * 4,
        out_specs=vmem,
        out_shape=jax.ShapeDtypeStruct(terms[0].shape, jnp.bfloat16),
        compiler_params=VMEM,
        name="normalize",
    )(key_gain[None], after, *terms)


def on_device(
    hidden,
    cross_query,
    image_cache,
    features,
    image_proj,
    key_gain,
    out_weight,
    cross_gate,
    image_spans,
    evicted,
    placement,
):
    head_size = key_gain.shape[0]
    tokens, cols = cross_query.shape
    heads = cols // head_size
    patches = features.shape[1]
    half = patches // 2
    seq_pos = lax.axis_index("seq")
    head_pos = lax.axis_index("head")
    y, x, core = seq_pos // 4, (seq_pos // 2) % 2, seq_pos % 2
    head_x, head_z = head_pos // 4, head_pos % 4
    chunks = 4 * tokens // CHUNK
    rows = heads * CHUNK

    sent_part = lax.dynamic_slice_in_dim(features[0], (1 - core) * half, half)
    peer_part = send_seq(sent_part, core=1)
    stale = jnp.any(placement[:, None] == evicted, axis=1).reshape(8, 2)
    both = jnp.any(stale[:, 0] & stale[:, 1])
    use_own = lax.dynamic_index_in_dim(stale, seq_pos // 2, 0, keepdims=False)[0] == (core == 0)
    part_index = jnp.arange(8, dtype=jnp.int32)
    home = head_at(head_x + part_index % 2, head_z + part_index // 2).astype(jnp.int32)

    held = image_cache[0]
    q_blocks = [cross_query] + [send_seq(cross_query, y=-dy) for dy in (1, 2, 3)]
    held_x = send_seq(held, x=1)
    held_core = send_seq(held, core=1)
    held_both = send_seq(held_x, core=1)

    def rebuild(own_first, work=None):
        pick = jnp.where(jnp.arange(2) == 0, own_first.astype(jnp.int32), core).astype(jnp.int32)
        parts = rebuild_parts(features, peer_part, image_proj, home, pick, q_blocks[1:])
        if work is None:
            terms, state = sum_over_head(parts), (peer_part,)
        else:
            terms, state = sum_beside(parts, work)
        mine = normalize(terms, key_gain, state[-1])
        other = send_seq(mine, x=1)
        pieces = (mine, other, send_seq(mine, core=1), send_seq(other, core=1))
        return pieces if work is None else (pieces, state)

    smem = pl.BlockSpec(memory_space=pltpu.SMEM)
    vmem = pl.BlockSpec(memory_space=pltpu.VMEM)
    order, first_all, stop_all, plan = pl.pallas_call(
        plan_kernel,
        in_specs=[smem] * 3 + [vmem],
        out_specs=[vmem] * 4,
        out_shape=[
            jax.ShapeDtypeStruct((4, tokens, tokens), jnp.bfloat16),
            jax.ShapeDtypeStruct((4 * tokens, head_size), jnp.int32),
            jax.ShapeDtypeStruct((4 * tokens, head_size), jnp.int32),
            jax.ShapeDtypeStruct((PLAN_ROWS, 128), jnp.int32),
        ],
        compiler_params=VMEM,
        name="plan",
    )(seq_pos.reshape(1).astype(jnp.int32), placement, evicted, image_spans.T.reshape(2, 16, tokens))
    state_shapes = [jax.ShapeDtypeStruct((chunks, rows, head_size), jnp.float32)] * 3

    def scratch(keys):
        return [pltpu.VMEM((rows, keys), jnp.float32)] * 2 + [pltpu.VMEM((keys, 2 * head_size), jnp.bfloat16)]

    def attend_first():
        return pl.pallas_call(
            functools.partial(begin_kernel, head_size),
            in_specs=[smem] + [vmem] * 8,
            out_specs=[vmem] * 4,
            out_shape=[jax.ShapeDtypeStruct((chunks, rows, head_size), jnp.bfloat16)] + state_shapes,
            scratch_shapes=scratch(patches),
            compiler_params=VMEM,
            name="attend_first",
        )(plan, *q_blocks, order, first_all, stop_all, held)

    def attend_more(state, low, *kv):
        return state[:1] + pl.pallas_call(
            functools.partial(go_on_kernel, head_size, len(kv), low),
            in_specs=[smem] + [vmem] * (6 + len(kv)),
            out_specs=[vmem] * 3,
            out_shape=state_shapes,
            scratch_shapes=scratch(patches),
            compiler_params=VMEM,
            name="attend_more",
        )(plan, state[0], first_all, stop_all, *state[1:], *kv)

    work = (
        attend_first,
        lambda state: attend_more(state, 1, held_core, held_x),
        lambda state: attend_more(state, 3, held_both),
    )
    once, state = rebuild(use_own, work)
    nothing = jnp.zeros((half, 2 * head_size), jnp.bfloat16)
    twice = lax.cond(both, lambda: rebuild(~use_own), lambda: (nothing,) * 4)
    rebuilt = once + twice
    partial_out = pl.pallas_call(
        functools.partial(rebuilt_kernel, head_size, len(rebuilt)),
        in_specs=[smem] + [vmem] * (7 + len(rebuilt)),
        out_specs=[vmem] * 4,
        out_shape=[jax.ShapeDtypeStruct((tokens, cols + 128), jnp.bfloat16)] * 4,
        scratch_shapes=[pltpu.VMEM(s.shape, s.dtype) for s in state_shapes] + scratch(half),
        compiler_params=VMEM,
        name="attend_rebuilt",
    )(plan, state[0], first_all, stop_all, *state[1:], order, *rebuilt)
    arrived = [partial_out[0]] + [send_seq(partial_out[dy], y=dy) for dy in (1, 2, 3)]
    context = pl.pallas_call(
        functools.partial(merge_kernel, head_size),
        in_specs=[vmem] * 4,
        out_specs=vmem,
        out_shape=jax.ShapeDtypeStruct((tokens, cols), jnp.bfloat16),
        compiler_params=VMEM,
        name="merge",
    )(*arrived)

    near, far = gather_chips(context)
    target = head_at(head_x + part_index % 2, head_z + part_index // 2)
    offset = 2 * ((target // 2 - y) % 4) + (target % 2 - x) % 2
    source = jnp.zeros(8, jnp.int32)
    for at, place in enumerate((0, 1, 2, 6, 4, 7, 3, 5)):
        source = jnp.where(offset == place, at, source)
    parts = project_parts(
        (near, far, send_seq(near, core=1), send_seq(far, core=1)),
        out_weight,
        source.astype(jnp.int32),
        core.reshape(1).astype(jnp.int32),
    )
    summed_out = sum(term.astype(jnp.float32) for term in sum_over_head(parts))
    return (hidden.astype(jnp.float32) + jnp.tanh(cross_gate[0]) * summed_out).astype(jnp.bfloat16)


def solution(mesh):
    placed = (
        P("head", "seq"),
        P("seq", "head"),
        P("seq", None, "head"),
        P("seq", None, "head"),
        P("head", None),
        P(),
        P("head", "seq"),
        P(),
        P(),
        P(),
        P(),
    )
    return jax.shard_map(
        on_device, mesh=mesh, in_specs=placed, out_specs=P("head", "seq"), check_vma=False
    )
```

```python
import functools
import math

import jax
import jax.numpy as jnp
from jax import lax
from jax.experimental import pallas as pl
from jax.experimental.pallas import tpu as pltpu
from jax.sharding import PartitionSpec as P

MASKED_SCORE = -1e30
CHUNK = 32
COUNT_ROW = 18
ID_ROW = 19
PLAN_ROWS = 24
VMEM = pltpu.CompilerParams(vmem_limit_bytes=20 * 1024 * 1024)


def seq_at(y, x, core):
    return (y % 4) * 4 + (x % 2) * 2 + core % 2


def head_at(x, z):
    return (x % 2) * 4 + z % 4


def send_seq(array, y=0, x=0, core=0):
    pairs = [
        (seq_at(a, b, c), seq_at(a + y, b + x, c + core)) for a in range(4) for b in range(2) for c in range(2)
    ]
    return lax.ppermute(array, "seq", pairs)


def send_head(array, x=0, z=0):
    return lax.ppermute(array, "head", [(head_at(a, b), head_at(a + x, b + z)) for a in range(2) for b in range(4)])


def add(*terms):
    return sum(term.astype(jnp.float32) for term in terms).astype(jnp.bfloat16)


def add_kernel(*refs):
    *terms, _, out_ref = refs
    out_ref[...] = sum(term[...].astype(jnp.float32) for term in terms).astype(out_ref.dtype)


def add_after(after, *terms):
    vmem = pl.BlockSpec(memory_space=pltpu.VMEM)
    return pl.pallas_call(
        add_kernel,
        in_specs=[vmem] * len(terms) + [pl.BlockSpec(memory_space=pl.ANY)],
        out_specs=vmem,
        out_shape=jax.ShapeDtypeStruct(terms[0].shape, terms[0].dtype),
        compiler_params=VMEM,
        name="add_after",
    )(*terms, after)


def sum_over_head(parts):
    p00, p01, p10, p11, p20, p21, p30, p31 = parts
    via_x = send_head(p21, x=1)
    down = send_head(p31, z=-1)
    across = send_head(p11, x=1)
    last = send_head(p30, z=-1)
    p20 = add(p20, via_x)
    p01 = add(p01, down)
    up = send_head(p20, z=1)
    side = send_head(p01, x=1)
    p10 = add(p10, across, up)
    ahead = send_head(p10, z=1)
    return p00, last, side, ahead


def sum_beside(parts, work, kv_of):
    p00, p01, p10, p11, p20, p21, p30, p31 = parts
    up = send_head(p20, z=1)
    down = send_head(p21, z=-1)
    across = send_head(p11, z=1)
    last = send_head(p30, z=-1)
    kv = kv_of(p30)
    state = work[0]()
    p10 = add_after(state[-1], p10, up)
    p31 = add_after(state[-1], p31, down)
    ahead = send_head(p10, z=1)
    behind = send_head(p31, z=-1)
    state = work[1](state, *kv[:2])
    p01 = add_after(state[-1], p01, across, behind)
    side = send_head(p01, x=1)
    state = work[2](state, kv[2])
    return (p00, last, ahead, side), state


def gather_chips(block):
    r30 = send_seq(block, y=1)
    r01 = send_seq(block, x=1)
    r10 = send_seq(block, y=-1)
    r20 = send_seq(r30, y=1)
    r31 = send_seq(r30, x=1)
    r11 = send_seq(r01, y=-1)
    r21 = send_seq(r20, x=1)
    return jnp.stack([block, r01, r10, r30]), jnp.stack([r20, r31, r11, r21])


def rebuild_kernel(order_ref, pick_ref, own_ref, peer_ref, proj0_ref, proj1_ref, *refs):
    *out_refs, rows_ref = refs[-9:]
    step = pl.program_id(0)

    @pl.when(step == 0)
    def _():
        rows_ref[...] = jnp.where(pick_ref[0] > 0, own_ref[0], peer_ref[...])

    products = [
        jnp.dot(rows_ref[...], proj_ref[...], preferred_element_type=jnp.float32).astype(jnp.bfloat16)
        for proj_ref in (proj0_ref, proj1_ref)
    ]
    for at in range(4):

        @pl.when(step == at)
        def _():
            out_refs[2 * at][...] = products[0]
            out_refs[2 * at + 1][...] = products[1]


def rebuild_parts(features, peer_part, proj, order, pick, after):
    count, depth = peer_part.shape
    cols = proj.shape[1] // 8
    return pl.pallas_call(
        rebuild_kernel,
        grid_spec=pltpu.PrefetchScalarGridSpec(
            num_scalar_prefetch=2,
            grid=(4,),
            in_specs=[
                pl.BlockSpec((1, count, depth), lambda i, order, pick: (0, pick[1], 0)),
                pl.BlockSpec((count, depth), lambda i, order, pick: (0, 0)),
                pl.BlockSpec((depth, cols), lambda i, order, pick: (0, order[2 * i])),
                pl.BlockSpec((depth, cols), lambda i, order, pick: (0, order[2 * i + 1])),
            ]
            + [pl.BlockSpec(memory_space=pl.ANY)] * len(after),
            out_specs=[pl.BlockSpec((count, cols), lambda i, order, pick: (0, 0))] * 8,
            scratch_shapes=[pltpu.VMEM((count, depth), jnp.bfloat16)],
        ),
        out_shape=[jax.ShapeDtypeStruct((count, cols), jnp.bfloat16)] * 8,
        compiler_params=VMEM,
        name="rebuild_parts",
    )(order, pick, features, peer_part, proj, proj, *after)


def project_kernel(order_ref, core_ref, own0_ref, own1_ref, other0_ref, other1_ref, weight_ref, *out_refs):
    step = pl.program_id(0)
    even = core_ref[0] == 0
    tokens = own0_ref.shape[1]

    def block(first_ref, second_ref, at):
        return jnp.where(at < 4, first_ref[jnp.minimum(at, 3)], second_ref[jnp.maximum(at - 4, 0)])

    rows = []
    for part in range(2):
        at = order_ref[2 * step + part]
        own, other = block(own0_ref, own1_ref, at), block(other0_ref, other1_ref, at)
        rows += [jnp.where(even, own, other), jnp.where(even, other, own)]
    product = jnp.dot(
        jnp.concatenate(rows, axis=0), weight_ref[...], preferred_element_type=jnp.float32
    ).astype(jnp.bfloat16)
    for at in range(4):

        @pl.when(step == at)
        def _():
            out_refs[2 * at][...] = product[: 2 * tokens]
            out_refs[2 * at + 1][...] = product[2 * tokens :]


def project_parts(blocks, weight, order, core):
    _, tokens, depth = blocks[0].shape
    cols = weight.shape[1]
    return pl.pallas_call(
        project_kernel,
        grid_spec=pltpu.PrefetchScalarGridSpec(
            num_scalar_prefetch=2,
            grid=(4,),
            in_specs=[pl.BlockSpec((4, tokens, depth), lambda i, order, core: (0, 0, 0))] * 4
            + [pl.BlockSpec((depth, cols), lambda i, order, core: (0, 0))],
            out_specs=[pl.BlockSpec((2 * tokens, cols), lambda i, order, core: (0, 0))] * 8,
        ),
        out_shape=[jax.ShapeDtypeStruct((2 * tokens, cols), jnp.bfloat16)] * 8,
        compiler_params=VMEM,
        name="project_parts",
    )(order, core, *blocks, weight)


def plan_kernel(pos_ref, placement_ref, evicted_ref, spans_ref, order_ref, first_ref, stop_ref, plan_ref):
    seq_pos = pos_ref[0]
    y, x, core = seq_pos // 4, (seq_pos // 2) % 2, seq_pos % 2
    tokens = spans_ref.shape[2]
    chips = (seq_pos // 2, seq_at(y, x + 1, 0) // 2)

    def stale(slot):
        image = placement_ref[slot]
        return (image == evicted_ref[0]) | (image == evicted_ref[1])

    entries = []
    for chip in chips:
        for slot in (2 * chip + core, 2 * chip + 1 - core):
            entries.append((placement_ref[slot], ~stale(slot)))
    once, twice = [], []
    for chip in chips:
        low, high = stale(2 * chip), stale(2 * chip + 1)
        once.append((jnp.where(low, placement_ref[2 * chip], placement_ref[2 * chip + 1]), low | high))
        twice.append((placement_ref[2 * chip + 1], low & high))
    entries += once + twice
    slot_lane = lax.broadcasted_iota(jnp.int32, (CHUNK, 128), 1)
    ids = jnp.full((CHUNK, 128), -1, jnp.int32)
    for at, (image, live) in enumerate(entries):
        ids = jnp.where(slot_lane == at, jnp.where(live, image, -1), ids)

    up = lax.broadcasted_iota(jnp.int32, (tokens, tokens), 0)
    along = lax.broadcasted_iota(jnp.int32, (tokens, tokens), 1)
    wanted = []
    for dy in range(4):
        block = seq_at(y + dy, x, core)
        first = jnp.broadcast_to(spans_ref[0, pl.ds(block, 1), :].astype(jnp.float32), (tokens, tokens))
        stop = jnp.broadcast_to(spans_ref[1, pl.ds(block, 1), :].astype(jnp.float32), (tokens, tokens))
        down = jnp.sum(jnp.where(up == along, first, 0.0), axis=1, keepdims=True)
        earlier = (down < first) | ((down == first) & (up < along))
        rank = jnp.sum(jnp.where(earlier, 1.0, 0.0), axis=0, keepdims=True).astype(jnp.int32)
        order = jnp.where(up == rank, 1.0, 0.0)
        order_ref[dy] = order.astype(jnp.bfloat16)
        first = jnp.broadcast_to(jnp.sum(order * first, axis=1, keepdims=True), (tokens, 128)).astype(jnp.int32)
        stop = jnp.broadcast_to(jnp.sum(order * stop, axis=1, keepdims=True), (tokens, 128)).astype(jnp.int32)
        first_ref[dy * tokens : (dy + 1) * tokens, :] = first
        stop_ref[dy * tokens : (dy + 1) * tokens, :] = stop
        for part in range(tokens // CHUNK):
            rows = slice(part * CHUNK, (part + 1) * CHUNK)
            seen = (first[rows] <= ids) & (ids < stop[rows])
            wanted.append(jnp.max(jnp.where(seen, 1, 0), axis=0, keepdims=True))
    places, total = [], jnp.zeros((1, 128), jnp.int32)
    for want in wanted:
        places.append(total)
        total = total + want
    for place in range(COUNT_ROW):
        row = jnp.zeros((1, 128), jnp.int32)
        for chunk, (want, at) in enumerate(zip(wanted, places)):
            row = jnp.where((want > 0) & (at == place), chunk, row)
        plan_ref[place : place + 1, :] = row
    plan_ref[COUNT_ROW : COUNT_ROW + 1, :] = total
    plan_ref[ID_ROW : ID_ROW + 1, :] = ids[:1]
    plan_ref[ID_ROW + 1 :, :] = jnp.zeros((PLAN_ROWS - ID_ROW - 1, 128), jnp.int32)


def sweep(head_size, plan_ref, low, q_ref, first_ref, stop_ref, kv_parts, state, even, odd, keys, wide):
    factor = math.log2(math.e) * head_size ** (-0.5)
    heads = q_ref.shape[1] // CHUNK
    m_ref, l_ref, acc_ref = state

    for slot, part in enumerate(kv_parts, low):
        count = plan_ref[COUNT_ROW, slot]

        def score(place, into):
            into[...] = lax.dot_general(
                q_ref[plan_ref[place, slot]],
                keys[...],
                (((1,), (1,)), ((), ())),
                preferred_element_type=jnp.float32,
            )

        def take(place, scores_ref):
            chunk = plan_ref[place, slot]
            image = jnp.where(place < count, plan_ref[ID_ROW, slot], -1)
            scores = scores_ref[...]
            here = jnp.broadcast_to(jnp.max(scores, axis=1, keepdims=True), (scores.shape[0], head_size))
            weights = jnp.exp2((scores - here[:, :1]) * factor)
            both = jnp.dot(weights.astype(jnp.bfloat16), wide[...], preferred_element_type=jnp.float32)
            mixed, total = both[:, :head_size], both[:, head_size:]
            tokens = pl.ds(pl.multiple_of(chunk * CHUNK, CHUNK), CHUNK)
            seen = (first_ref[tokens, :] <= image) & (image < stop_ref[tokens, :])
            seen = jnp.concatenate([seen.astype(jnp.int32)] * heads, axis=0) > 0
            before = m_ref[chunk]
            after = jnp.where(seen, jnp.maximum(before, here), before)
            keep = jnp.exp2((before - after) * factor)
            gain = jnp.where(seen, jnp.exp2((here - after) * factor), 0.0)
            m_ref[chunk] = after
            l_ref[chunk] = l_ref[chunk] * keep + gain * total
            acc_ref[chunk] = acc_ref[chunk] * keep + gain * mixed

        @pl.when(count > 0)
        def _():
            at = 0
            for rows_of in part:
                block = rows_of()
                rows = slice(at, at + block.shape[0])
                keys[rows, :] = block[:, :head_size]
                wide[rows, :head_size] = block[:, head_size:]
                at += block.shape[0]
            wide[:, head_size:] = jnp.ones_like(wide[:, head_size:])
            score(0, even)

            def body(at, carry):
                place = 2 * at
                score(place + 1, odd)
                take(place, even)
                score(place + 2, even)
                take(place + 1, odd)
                return carry

            lax.fori_loop(0, (count + 1) // 2, body, 0)


def copy_kernel(array_ref, after_ref, out_ref):
    out_ref[...] = array_ref[...]


def copy_after(array, after):
    vmem = pl.BlockSpec(memory_space=pltpu.VMEM)
    return pl.pallas_call(
        copy_kernel,
        in_specs=[vmem, pl.BlockSpec(memory_space=pl.ANY)],
        out_specs=vmem,
        out_shape=jax.ShapeDtypeStruct(array.shape, array.dtype),
        compiler_params=VMEM,
        name="copy_after",
    )(array, after)


def begin_kernel(head_size, plan, q0, q1, q2, q3, order, first, stop, a, qs, m, l, acc, *work):
    heads = q0.shape[1] // head_size
    per_block = q0.shape[0] // CHUNK
    for block, q_ref in enumerate((q0, q1, q2, q3)):
        ordered = jnp.dot(order[block], q_ref[...], preferred_element_type=jnp.float32).astype(jnp.bfloat16)
        for part in range(per_block):
            for head in range(heads):
                qs[block * per_block + part, head * CHUNK : (head + 1) * CHUNK, :] = ordered[
                    part * CHUNK : (part + 1) * CHUNK, head * head_size : (head + 1) * head_size
                ]
    m[...] = jnp.full_like(m, MASKED_SCORE)
    l[...] = jnp.zeros_like(l)
    acc[...] = jnp.zeros_like(acc)
    sweep(head_size, plan, 0, qs, first, stop, [[lambda: a[...]]], (m, l, acc), *work)


def go_on_kernel(head_size, parts, low, plan, qs, first, stop, m_in, l_in, acc_in, *refs):
    kv, (m, l, acc, *work) = refs[:parts], refs[parts:]
    m[...] = m_in[...]
    l[...] = l_in[...]
    acc[...] = acc_in[...]
    sweep(head_size, plan, low, qs, first, stop, [[lambda r=r: r[...]] for r in kv], (m, l, acc), *work)


def rebuilt_kernel(head_size, plan, qs, first, stop, m_in, l_in, acc_in, order, *refs):
    *once, twice, o0, o1, o2, o3, m, l, acc, even, odd, keys, wide = refs
    factor = math.log2(math.e) * head_size ** (-0.5)
    tokens = o0.shape[0]
    heads = qs.shape[1] // CHUNK
    per_block = tokens // CHUNK
    m[...] = m_in[...]
    l[...] = l_in[...]
    acc[...] = acc_in[...]
    kv_parts = [[lambda r=once[i]: r[...], lambda r=once[i + 2]: r[...]] for i in range(2)]
    kv_parts += [[lambda i=i: twice[i], lambda i=i: twice[i + 2]] for i in range(2)]
    sweep(head_size, plan, 4, qs, first, stop, kv_parts, (m, l, acc), even, odd, keys, wide)
    lanes = lax.broadcasted_iota(jnp.int32, (tokens, 128), 1)
    for block, out in enumerate((o0, o1, o2, o3)):
        extra = jnp.zeros((tokens, 128), jnp.float32)
        for head in range(heads):
            rows = slice(head * CHUNK, (head + 1) * CHUNK)
            chunks = range(block * per_block, (block + 1) * per_block)
            high = jnp.concatenate([m[chunk, rows, :] for chunk in chunks], axis=0)
            total = jnp.concatenate([l[chunk, rows, :] for chunk in chunks], axis=0)
            mixed = jnp.concatenate([acc[chunk, rows, :] for chunk in chunks], axis=0)
            some = total > 0.0
            safe = jnp.where(some, total, 1.0)
            level = jnp.where(some, high * factor + jnp.log2(safe), MASKED_SCORE)
            ordered = (mixed / safe).astype(jnp.bfloat16)
            out[:, head * head_size : (head + 1) * head_size] = lax.dot_general(
                order[block], ordered, (((0,), (0,)), ((), ())), preferred_element_type=jnp.float32
            ).astype(jnp.bfloat16)
            for piece in range(3):
                rounded = level.astype(jnp.bfloat16).astype(jnp.float32)
                extra = jnp.where(lanes == piece * heads + head, rounded, extra)
                level = level - rounded
        out[:, heads * head_size :] = lax.dot_general(
            order[block], extra.astype(jnp.bfloat16), (((0,), (0,)), ((), ())), preferred_element_type=jnp.float32
        ).astype(jnp.bfloat16)


def merge_kernel(head_size, a, b, c, d, out):
    heads = out.shape[1] // head_size
    parts = (a, b, c, d)
    extras = [part[:, heads * head_size :].astype(jnp.float32) for part in parts]
    for head in range(heads):
        cols = slice(head * head_size, (head + 1) * head_size)
        levels = [sum(e[:, p * heads + head : p * heads + head + 1] for p in range(3)) for e in extras]
        top = functools.reduce(jnp.maximum, levels)
        shares = [jnp.exp2(level - top) for level in levels]
        mixed = sum(share * part[:, cols].astype(jnp.float32) for share, part in zip(shares, parts))
        out[:, cols] = (mixed / sum(shares)).astype(jnp.bfloat16)


def normalize_kernel(gain_ref, after_ref, a, b, c, d, out):
    head_size = gain_ref.shape[1]
    keys, values = (
        sum(part[:, low : low + head_size].astype(jnp.float32) for part in (a, b, c, d)) for low in (0, head_size)
    )
    inverse = lax.rsqrt(jnp.mean(keys * keys, axis=-1, keepdims=True) + 1e-05)
    out[:, :head_size] = (keys * inverse * gain_ref[...]).astype(out.dtype)
    out[:, head_size:] = values.astype(out.dtype)


def normalize(terms, key_gain, after):
    vmem = pl.BlockSpec(memory_space=pltpu.VMEM)
    return pl.pallas_call(
        normalize_kernel,
        in_specs=[vmem, pl.BlockSpec(memory_space=pl.ANY)] + [vmem] * 4,
        out_specs=vmem,
        out_shape=jax.ShapeDtypeStruct(terms[0].shape, jnp.bfloat16),
        compiler_params=VMEM,
        name="normalize",
    )(key_gain[None], after, *terms)


def on_device(
    hidden,
    cross_query,
    image_cache,
    features,
    image_proj,
    key_gain,
    out_weight,
    cross_gate,
    image_spans,
    evicted,
    placement,
):
    head_size = key_gain.shape[0]
    tokens, cols = cross_query.shape
    heads = cols // head_size
    patches = features.shape[1]
    half = patches // 2
    seq_pos = lax.axis_index("seq")
    head_pos = lax.axis_index("head")
    y, x, core = seq_pos // 4, (seq_pos // 2) % 2, seq_pos % 2
    head_x, head_z = head_pos // 4, head_pos % 4
    chunks = 4 * tokens // CHUNK
    rows = heads * CHUNK

    sent_part = lax.dynamic_slice_in_dim(features[0], (1 - core) * half, half)
    peer_part = send_seq(sent_part, core=1)
    stale = jnp.any(placement[:, None] == evicted, axis=1).reshape(8, 2)
    both = jnp.any(stale[:, 0] & stale[:, 1])
    use_own = lax.dynamic_index_in_dim(stale, seq_pos // 2, 0, keepdims=False)[0] == (core == 0)
    part_index = jnp.arange(8, dtype=jnp.int32)
    home = head_at(head_x + part_index % 2, head_z + part_index // 2).astype(jnp.int32)

    held = image_cache[0]
    q_blocks = [cross_query] + [send_seq(cross_query, y=-dy) for dy in (1, 2, 3)]
    held_x = send_seq(held, x=1)

    def rebuild(own_first, after=(), work=None, kv_of=None):
        pick = jnp.where(jnp.arange(2) == 0, own_first.astype(jnp.int32), core).astype(jnp.int32)
        parts = rebuild_parts(features, peer_part, image_proj, home, pick, after)
        if work is None:
            terms, state = sum_over_head(parts), (peer_part,)
        else:
            terms, state = sum_beside(parts, work, kv_of)
        mine = normalize(terms, key_gain, state[-1])
        other = send_seq(mine, x=1)
        pieces = (mine, other, send_seq(mine, core=1), send_seq(other, core=1))
        return pieces if work is None else (pieces, state)

    smem = pl.BlockSpec(memory_space=pltpu.SMEM)
    vmem = pl.BlockSpec(memory_space=pltpu.VMEM)
    order, first_all, stop_all, plan = pl.pallas_call(
        plan_kernel,
        in_specs=[smem] * 3 + [vmem],
        out_specs=[vmem] * 4,
        out_shape=[
            jax.ShapeDtypeStruct((4, tokens, tokens), jnp.bfloat16),
            jax.ShapeDtypeStruct((4 * tokens, head_size), jnp.int32),
            jax.ShapeDtypeStruct((4 * tokens, head_size), jnp.int32),
            jax.ShapeDtypeStruct((PLAN_ROWS, 128), jnp.int32),
        ],
        compiler_params=VMEM,
        name="plan",
    )(seq_pos.reshape(1).astype(jnp.int32), placement, evicted, image_spans.T.reshape(2, 16, tokens))
    state_shapes = [jax.ShapeDtypeStruct((chunks, rows, head_size), jnp.float32)] * 3

    def scratch(keys):
        return [pltpu.VMEM((rows, keys), jnp.float32)] * 2 + [
            pltpu.VMEM((keys, head_size), jnp.bfloat16),
            pltpu.VMEM((keys, 2 * head_size), jnp.bfloat16),
        ]

    def attend_first():
        return pl.pallas_call(
            functools.partial(begin_kernel, head_size),
            in_specs=[smem] + [vmem] * 8,
            out_specs=[vmem] * 4,
            out_shape=[jax.ShapeDtypeStruct((chunks, rows, head_size), jnp.bfloat16)] + state_shapes,
            scratch_shapes=scratch(patches),
            compiler_params=VMEM,
            name="attend_first",
        )(plan, *q_blocks, order, first_all, stop_all, held)

    def attend_more(state, low, *kv):
        return state[:1] + pl.pallas_call(
            functools.partial(go_on_kernel, head_size, len(kv), low),
            in_specs=[smem] + [vmem] * (6 + len(kv)),
            out_specs=[vmem] * 3,
            out_shape=state_shapes,
            scratch_shapes=scratch(patches),
            input_output_aliases={4: 0, 5: 1, 6: 2},
            compiler_params=VMEM,
            name="attend_more",
        )(plan, state[0], first_all, stop_all, *state[1:], *kv)

    work = (
        attend_first,
        lambda state, *kv: attend_more(state, 1, *kv),
        lambda state, *kv: attend_more(state, 3, *kv),
    )

    def kv_of(after):
        return send_seq(copy_after(held, after), core=1), held_x, send_seq(held_x, core=1)

    twice = lax.cond(
        both,
        lambda: jnp.stack(rebuild(~use_own, q_blocks[1:])),
        lambda: jnp.zeros((4, half, 2 * head_size), jnp.bfloat16),
    )
    once, state = rebuild(use_own, (twice,), work, kv_of)
    partial_out = pl.pallas_call(
        functools.partial(rebuilt_kernel, head_size),
        in_specs=[smem] + [vmem] * 12,
        out_specs=[vmem] * 4,
        out_shape=[jax.ShapeDtypeStruct((tokens, cols + 128), jnp.bfloat16)] * 4,
        scratch_shapes=[pltpu.VMEM(s.shape, s.dtype) for s in state_shapes] + scratch(patches),
        compiler_params=VMEM,
        name="attend_rebuilt",
    )(plan, state[0], first_all, stop_all, *state[1:], order, *once, twice)
    arrived = [partial_out[0]] + [send_seq(partial_out[dy], y=dy) for dy in (1, 2, 3)]
    context = pl.pallas_call(
        functools.partial(merge_kernel, head_size),
        in_specs=[vmem] * 4,
        out_specs=vmem,
        out_shape=jax.ShapeDtypeStruct((tokens, cols), jnp.bfloat16),
        compiler_params=VMEM,
        name="merge",
    )(*arrived)

    near, far = gather_chips(context)
    target = head_at(head_x + part_index % 2, head_z + part_index // 2)
    offset = 2 * ((target // 2 - y) % 4) + (target % 2 - x) % 2
    source = jnp.zeros(8, jnp.int32)
    for at, place in enumerate((0, 1, 2, 6, 4, 7, 3, 5)):
        source = jnp.where(offset == place, at, source)
    parts = project_parts(
        (near, far, send_seq(near, core=1), send_seq(far, core=1)),
        out_weight,
        source.astype(jnp.int32),
        core.reshape(1).astype(jnp.int32),
    )
    summed_out = sum(term.astype(jnp.float32) for term in sum_over_head(parts))
    return (hidden.astype(jnp.float32) + jnp.tanh(cross_gate[0]) * summed_out).astype(jnp.bfloat16)


def solution(mesh):
    placed = (
        P("head", "seq"),
        P("seq", "head"),
        P("seq", None, "head"),
        P("seq", None, "head"),
        P("head", None),
        P(),
        P("head", "seq"),
        P(),
        P(),
        P(),
        P(),
    )
    return jax.shard_map(
        on_device, mesh=mesh, in_specs=placed, out_specs=P("head", "seq"), check_vma=False
    )
```

```python
import functools
import math

import jax
import jax.numpy as jnp
from jax import lax
from jax.experimental import pallas as pl
from jax.experimental.pallas import tpu as pltpu
from jax.sharding import PartitionSpec as P

MASKED_SCORE = -1e30
CHUNK = 32
COUNT_ROW = 18
ID_ROW = 19
THIRD_ROW = 20
TWO_THIRDS_ROW = 21
ZERO_ROW = 22
PLAN_ROWS = 24
VMEM = pltpu.CompilerParams(vmem_limit_bytes=20 * 1024 * 1024)


def seq_at(y, x, core):
    return (y % 4) * 4 + (x % 2) * 2 + core % 2


def head_at(x, z):
    return (x % 2) * 4 + z % 4


def send_seq(array, y=0, x=0, core=0):
    pairs = [
        (seq_at(a, b, c), seq_at(a + y, b + x, c + core)) for a in range(4) for b in range(2) for c in range(2)
    ]
    return lax.ppermute(array, "seq", pairs)


def send_head(array, x=0, z=0):
    return lax.ppermute(array, "head", [(head_at(a, b), head_at(a + x, b + z)) for a in range(2) for b in range(4)])


def add(*terms):
    return sum(term.astype(jnp.float32) for term in terms).astype(jnp.bfloat16)


def add_kernel(*refs):
    *terms, _, out_ref = refs
    out_ref[...] = sum(term[...].astype(jnp.float32) for term in terms).astype(out_ref.dtype)


def add_after(after, *terms):
    vmem = pl.BlockSpec(memory_space=pltpu.VMEM)
    return pl.pallas_call(
        add_kernel,
        in_specs=[vmem] * len(terms) + [pl.BlockSpec(memory_space=pl.ANY)],
        out_specs=vmem,
        out_shape=jax.ShapeDtypeStruct(terms[0].shape, terms[0].dtype),
        compiler_params=VMEM,
        name="add_after",
    )(*terms, after)


def sum_over_head(parts):
    p00, p01, p10, p11, p20, p21, p30, p31 = parts
    via_x = send_head(p21, x=1)
    down = send_head(p31, z=-1)
    across = send_head(p11, x=1)
    last = send_head(p30, z=-1)
    p20 = add(p20, via_x)
    p01 = add(p01, down)
    up = send_head(p20, z=1)
    side = send_head(p01, x=1)
    p10 = add(p10, across, up)
    ahead = send_head(p10, z=1)
    return p00, last, side, ahead


def sum_beside(parts, work, kv_of):
    p00, p01, p10, p11, p20, p21, p30, p31 = parts
    up = send_head(p20, z=1)
    down = send_head(p21, z=-1)
    across = send_head(p11, z=1)
    last = send_head(p30, z=-1)
    kv = kv_of(p30)
    state = work[0](*kv[:2])
    p10 = add_after(state[-1], p10, up)
    p31 = add_after(state[-1], p31, down)
    held_x, p10, p31 = lax.optimization_barrier((kv[2], p10, p31))
    kv = kv[:2] + (held_x, send_seq(held_x, core=1))
    ahead = send_head(p10, z=1)
    behind = send_head(p31, z=-1)
    state = work[1](state, *kv)
    p01 = add_after(state[-1], p01, across, behind)
    side = send_head(p01, x=1)
    state = work[2](state, *kv)
    return (p00, last, ahead, side), state


def gather_chips(block):
    r30 = send_seq(block, y=1)
    r01 = send_seq(block, x=1)
    r10 = send_seq(block, y=-1)
    r30, r01, r10 = lax.optimization_barrier((r30, r01, r10))
    r20 = send_seq(r30, y=1)
    r31 = send_seq(r30, x=1)
    r11 = send_seq(r01, y=-1)
    r21 = send_seq(r20, x=1)
    return jnp.stack([block, r01, r30, r10]), jnp.stack([r20, r31, r11, r21])


def rebuild_kernel(order_ref, pick_ref, own_ref, peer_ref, proj0_ref, proj1_ref, *refs):
    *out_refs, rows_ref = refs[-9:]
    step = pl.program_id(0)

    @pl.when(step == 0)
    def _():
        rows_ref[...] = jnp.where(pick_ref[0] > 0, own_ref[0], peer_ref[...])

    products = [
        jnp.dot(rows_ref[...], proj_ref[...], preferred_element_type=jnp.float32).astype(jnp.bfloat16)
        for proj_ref in (proj0_ref, proj1_ref)
    ]
    for at in range(4):

        @pl.when(step == at)
        def _():
            out_refs[2 * at][...] = products[0]
            out_refs[2 * at + 1][...] = products[1]


def rebuild_parts(features, peer_part, proj, order, pick, after):
    count, depth = peer_part.shape
    cols = proj.shape[1] // 8
    return pl.pallas_call(
        rebuild_kernel,
        grid_spec=pltpu.PrefetchScalarGridSpec(
            num_scalar_prefetch=2,
            grid=(4,),
            in_specs=[
                pl.BlockSpec((1, count, depth), lambda i, order, pick: (0, pick[1], 0)),
                pl.BlockSpec((count, depth), lambda i, order, pick: (0, 0)),
                pl.BlockSpec((depth, cols), lambda i, order, pick: (0, order[2 * i])),
                pl.BlockSpec((depth, cols), lambda i, order, pick: (0, order[2 * i + 1])),
            ]
            + [pl.BlockSpec(memory_space=pl.ANY)] * len(after),
            out_specs=[pl.BlockSpec((count, cols), lambda i, order, pick: (0, 0))] * 8,
            scratch_shapes=[pltpu.VMEM((count, depth), jnp.bfloat16)],
        ),
        out_shape=[jax.ShapeDtypeStruct((count, cols), jnp.bfloat16)] * 8,
        compiler_params=VMEM,
        name="rebuild_parts",
    )(order, pick, features, peer_part, proj, proj, *after)


def project_kernel(order_ref, core_ref, own0_ref, own1_ref, other0_ref, other1_ref, weight_ref, *out_refs):
    step = pl.program_id(0)
    even = core_ref[0] == 0
    tokens = own0_ref.shape[1]

    def block(first_ref, second_ref, at):
        return jnp.where(at < 4, first_ref[jnp.minimum(at, 3)], second_ref[jnp.maximum(at - 4, 0)])

    rows = []
    for part in range(2):
        at = order_ref[2 * step + part]
        own, other = block(own0_ref, own1_ref, at), block(other0_ref, other1_ref, at)
        rows += [jnp.where(even, own, other), jnp.where(even, other, own)]
    product = jnp.dot(
        jnp.concatenate(rows, axis=0), weight_ref[...], preferred_element_type=jnp.float32
    ).astype(jnp.bfloat16)
    for at in range(4):

        @pl.when(step == at)
        def _():
            out_refs[2 * at][...] = product[: 2 * tokens]
            out_refs[2 * at + 1][...] = product[2 * tokens :]


def project_parts(blocks, weight, order, core):
    _, tokens, depth = blocks[0].shape
    cols = weight.shape[1]
    return pl.pallas_call(
        project_kernel,
        grid_spec=pltpu.PrefetchScalarGridSpec(
            num_scalar_prefetch=2,
            grid=(4,),
            in_specs=[pl.BlockSpec((4, tokens, depth), lambda i, order, core: (0, 0, 0))] * 4
            + [pl.BlockSpec((depth, cols), lambda i, order, core: (0, 0))],
            out_specs=[pl.BlockSpec((2 * tokens, cols), lambda i, order, core: (0, 0))] * 8,
        ),
        out_shape=[jax.ShapeDtypeStruct((2 * tokens, cols), jnp.bfloat16)] * 8,
        compiler_params=VMEM,
        name="project_parts",
    )(order, core, *blocks, weight)


def plan_kernel(pos_ref, placement_ref, evicted_ref, spans_ref, order_ref, first_ref, stop_ref, plan_ref):
    seq_pos = pos_ref[0]
    y, x, core = seq_pos // 4, (seq_pos // 2) % 2, seq_pos % 2
    tokens = spans_ref.shape[2]
    chips = (seq_pos // 2, seq_at(y, x + 1, 0) // 2)

    def stale(slot):
        image = placement_ref[slot]
        return (image == evicted_ref[0]) | (image == evicted_ref[1])

    entries = []
    for chip in chips:
        for slot in (2 * chip + core, 2 * chip + 1 - core):
            entries.append((placement_ref[slot], ~stale(slot)))
    once, twice = [], []
    for chip in chips:
        low, high = stale(2 * chip), stale(2 * chip + 1)
        once.append((jnp.where(low, placement_ref[2 * chip], placement_ref[2 * chip + 1]), low | high))
        twice.append((placement_ref[2 * chip + 1], low & high))
    entries += once + twice
    slot_lane = lax.broadcasted_iota(jnp.int32, (CHUNK, 128), 1)
    ids = jnp.full((CHUNK, 128), -1, jnp.int32)
    for at, (image, live) in enumerate(entries):
        ids = jnp.where(slot_lane == at, jnp.where(live, image, -1), ids)

    up = lax.broadcasted_iota(jnp.int32, (tokens, tokens), 0)
    along = lax.broadcasted_iota(jnp.int32, (tokens, tokens), 1)
    wanted = []
    for dy in range(4):
        block = seq_at(y + dy, x, core)
        first = jnp.broadcast_to(spans_ref[0, pl.ds(block, 1), :].astype(jnp.float32), (tokens, tokens))
        stop = jnp.broadcast_to(spans_ref[1, pl.ds(block, 1), :].astype(jnp.float32), (tokens, tokens))
        down = jnp.sum(jnp.where(up == along, first, 0.0), axis=1, keepdims=True)
        earlier = (down < first) | ((down == first) & (up < along))
        rank = jnp.sum(jnp.where(earlier, 1.0, 0.0), axis=0, keepdims=True).astype(jnp.int32)
        order = jnp.where(up == rank, 1.0, 0.0)
        order_ref[dy] = order.astype(jnp.bfloat16)
        first = jnp.broadcast_to(jnp.sum(order * first, axis=1, keepdims=True), (tokens, 128)).astype(jnp.int32)
        stop = jnp.broadcast_to(jnp.sum(order * stop, axis=1, keepdims=True), (tokens, 128)).astype(jnp.int32)
        first_ref[dy * tokens : (dy + 1) * tokens, :] = first
        stop_ref[dy * tokens : (dy + 1) * tokens, :] = stop
        for part in range(tokens // CHUNK):
            rows = slice(part * CHUNK, (part + 1) * CHUNK)
            seen = (first[rows] <= ids) & (ids < stop[rows])
            wanted.append(jnp.max(jnp.where(seen, 1, 0), axis=0, keepdims=True))
    places, total = [], jnp.zeros((1, 128), jnp.int32)
    for want in wanted:
        places.append(total)
        total = total + want
    for place in range(COUNT_ROW):
        row = jnp.zeros((1, 128), jnp.int32)
        for chunk, (want, at) in enumerate(zip(wanted, places)):
            row = jnp.where((want > 0) & (at == place), chunk, row)
        plan_ref[place : place + 1, :] = row
    plan_ref[COUNT_ROW : COUNT_ROW + 1, :] = total
    plan_ref[ID_ROW : ID_ROW + 1, :] = ids[:1]
    plan_ref[ZERO_ROW:, :] = jnp.zeros((PLAN_ROWS - ZERO_ROW, 128), jnp.int32)
    lane = slot_lane[:1]
    counts = [jnp.sum(jnp.where(lane == at, total, 0), axis=1, keepdims=True) for at in range(4)]
    share = ((sum(counts) + 2) * 21846) >> 16
    third, two_thirds = jnp.zeros((1, 128), jnp.int32), jnp.zeros((1, 128), jnp.int32)
    before = jnp.zeros((1, 1), jnp.int32)
    for at, count in enumerate(counts):
        if at < 2:
            third = jnp.where(lane == at, jnp.clip(share - before, 0, count), third)
        two_thirds = jnp.where(lane == at, jnp.clip(2 * share - before, 0, count), two_thirds)
        before = before + count
    plan_ref[THIRD_ROW : THIRD_ROW + 1, :] = third
    plan_ref[TWO_THIRDS_ROW : TWO_THIRDS_ROW + 1, :] = two_thirds


def sweep(head_size, plan_ref, low, limits, q_ref, first_ref, stop_ref, kv_parts, state, even, odd, keys, wide):
    factor = math.log2(math.e) * head_size ** (-0.5)
    heads = q_ref.shape[1] // CHUNK
    m_ref, l_ref, acc_ref = state

    for slot, part in enumerate(kv_parts, low):
        begin, end = (plan_ref[row, slot] for row in limits)

        def score(place, into):
            into[...] = lax.dot_general(
                q_ref[plan_ref[place, slot]],
                keys[...],
                (((1,), (1,)), ((), ())),
                preferred_element_type=jnp.float32,
            )

        def take(place, scores_ref):
            chunk = plan_ref[place, slot]
            image = jnp.where(place < end, plan_ref[ID_ROW, slot], -1)
            scores = scores_ref[...]
            here = jnp.broadcast_to(jnp.max(scores, axis=1, keepdims=True), (scores.shape[0], head_size))
            weights = jnp.exp2((scores - here[:, :1]) * factor)
            both = jnp.dot(weights.astype(jnp.bfloat16), wide[...], preferred_element_type=jnp.float32)
            mixed, total = both[:, :head_size], both[:, head_size:]
            tokens = pl.ds(pl.multiple_of(chunk * CHUNK, CHUNK), CHUNK)
            seen = (first_ref[tokens, :] <= image) & (image < stop_ref[tokens, :])
            seen = jnp.concatenate([seen.astype(jnp.int32)] * heads, axis=0) > 0
            before = m_ref[chunk]
            after = jnp.where(seen, jnp.maximum(before, here), before)
            keep = jnp.exp2((before - after) * factor)
            gain = jnp.where(seen, jnp.exp2((here - after) * factor), 0.0)
            m_ref[chunk] = after
            l_ref[chunk] = l_ref[chunk] * keep + gain * total
            acc_ref[chunk] = acc_ref[chunk] * keep + gain * mixed

        @pl.when(end > begin)
        def _():
            at = 0
            for rows_of in part:
                block = rows_of()
                rows = slice(at, at + block.shape[0])
                keys[rows, :] = block[:, :head_size]
                wide[rows, :head_size] = block[:, head_size:]
                at += block.shape[0]
            wide[:, head_size:] = jnp.ones_like(wide[:, head_size:])
            score(begin, even)

            def body(at, carry):
                place = begin + 2 * at
                score(place + 1, odd)
                take(place, even)
                score(place + 2, even)
                take(place + 1, odd)
                return carry

            lax.fori_loop(0, (end - begin + 1) // 2, body, 0)


def copy_kernel(array_ref, after_ref, out_ref):
    out_ref[...] = array_ref[...]


def copy_after(array, after):
    vmem = pl.BlockSpec(memory_space=pltpu.VMEM)
    return pl.pallas_call(
        copy_kernel,
        in_specs=[vmem, pl.BlockSpec(memory_space=pl.ANY)],
        out_specs=vmem,
        out_shape=jax.ShapeDtypeStruct(array.shape, array.dtype),
        compiler_params=VMEM,
        name="copy_after",
    )(array, after)


def begin_kernel(head_size, plan, q0, q1, q2, q3, order, first, stop, a, b, qs, m, l, acc, *work):
    heads = q0.shape[1] // head_size
    per_block = q0.shape[0] // CHUNK
    for block, q_ref in enumerate((q0, q1, q2, q3)):
        ordered = jnp.dot(order[block], q_ref[...], preferred_element_type=jnp.float32).astype(jnp.bfloat16)
        for part in range(per_block):
            for head in range(heads):
                qs[block * per_block + part, head * CHUNK : (head + 1) * CHUNK, :] = ordered[
                    part * CHUNK : (part + 1) * CHUNK, head * head_size : (head + 1) * head_size
                ]
    m[...] = jnp.full_like(m, MASKED_SCORE)
    l[...] = jnp.zeros_like(l)
    acc[...] = jnp.zeros_like(acc)
    kv_parts = [[lambda r=r: r[...]] for r in (a, b)]
    sweep(head_size, plan, 0, (ZERO_ROW, THIRD_ROW), qs, first, stop, kv_parts, (m, l, acc), *work)


def go_on_kernel(head_size, parts, limits, plan, qs, first, stop, m_in, l_in, acc_in, *refs):
    kv, (m, l, acc, *work) = refs[:parts], refs[parts:]
    m[...] = m_in[...]
    l[...] = l_in[...]
    acc[...] = acc_in[...]
    sweep(head_size, plan, 0, limits, qs, first, stop, [[lambda r=r: r[...]] for r in kv], (m, l, acc), *work)


def rebuilt_kernel(head_size, plan, qs, first, stop, m_in, l_in, acc_in, order, *refs):
    *once, twice, o0, o1, o2, o3, m, l, acc, even, odd, keys, wide = refs
    factor = math.log2(math.e) * head_size ** (-0.5)
    tokens = o0.shape[0]
    heads = qs.shape[1] // CHUNK
    per_block = tokens // CHUNK
    m[...] = m_in[...]
    l[...] = l_in[...]
    acc[...] = acc_in[...]
    kv_parts = [[lambda r=once[i]: r[...], lambda r=once[i + 2]: r[...]] for i in range(2)]
    kv_parts += [[lambda i=i: twice[i], lambda i=i: twice[i + 2]] for i in range(2)]
    sweep(head_size, plan, 4, (ZERO_ROW, COUNT_ROW), qs, first, stop, kv_parts, (m, l, acc), even, odd, keys, wide)
    lanes = lax.broadcasted_iota(jnp.int32, (tokens, 128), 1)
    for block, out in enumerate((o0, o1, o2, o3)):
        extra = jnp.zeros((tokens, 128), jnp.float32)
        for head in range(heads):
            rows = slice(head * CHUNK, (head + 1) * CHUNK)
            chunks = range(block * per_block, (block + 1) * per_block)
            high = jnp.concatenate([m[chunk, rows, :] for chunk in chunks], axis=0)
            total = jnp.concatenate([l[chunk, rows, :] for chunk in chunks], axis=0)
            mixed = jnp.concatenate([acc[chunk, rows, :] for chunk in chunks], axis=0)
            some = total > 0.0
            safe = jnp.where(some, total, 1.0)
            level = jnp.where(some, high * factor + jnp.log2(safe), MASKED_SCORE)
            ordered = (mixed / safe).astype(jnp.bfloat16)
            out[:, head * head_size : (head + 1) * head_size] = lax.dot_general(
                order[block], ordered, (((0,), (0,)), ((), ())), preferred_element_type=jnp.float32
            ).astype(jnp.bfloat16)
            for piece in range(3):
                rounded = level.astype(jnp.bfloat16).astype(jnp.float32)
                extra = jnp.where(lanes == piece * heads + head, rounded, extra)
                level = level - rounded
        out[:, heads * head_size :] = lax.dot_general(
            order[block], extra.astype(jnp.bfloat16), (((0,), (0,)), ((), ())), preferred_element_type=jnp.float32
        ).astype(jnp.bfloat16)


def merge_kernel(head_size, a, b, c, d, out):
    heads = out.shape[1] // head_size
    parts = (a, b, c, d)
    extras = [part[:, heads * head_size :].astype(jnp.float32) for part in parts]
    for head in range(heads):
        cols = slice(head * head_size, (head + 1) * head_size)
        levels = [sum(e[:, p * heads + head : p * heads + head + 1] for p in range(3)) for e in extras]
        top = functools.reduce(jnp.maximum, levels)
        shares = [jnp.exp2(level - top) for level in levels]
        mixed = sum(share * part[:, cols].astype(jnp.float32) for share, part in zip(shares, parts))
        out[:, cols] = (mixed / sum(shares)).astype(jnp.bfloat16)


def normalize_kernel(gain_ref, after_ref, a, b, c, d, out):
    head_size = gain_ref.shape[1]
    keys, values = (
        sum(part[:, low : low + head_size].astype(jnp.float32) for part in (a, b, c, d)) for low in (0, head_size)
    )
    inverse = lax.rsqrt(jnp.mean(keys * keys, axis=-1, keepdims=True) + 1e-05)
    out[:, :head_size] = (keys * inverse * gain_ref[...]).astype(out.dtype)
    out[:, head_size:] = values.astype(out.dtype)


def normalize(terms, key_gain, after):
    vmem = pl.BlockSpec(memory_space=pltpu.VMEM)
    return pl.pallas_call(
        normalize_kernel,
        in_specs=[vmem, pl.BlockSpec(memory_space=pl.ANY)] + [vmem] * 4,
        out_specs=vmem,
        out_shape=jax.ShapeDtypeStruct(terms[0].shape, jnp.bfloat16),
        compiler_params=VMEM,
        name="normalize",
    )(key_gain[None], after, *terms)


def on_device(
    hidden,
    cross_query,
    image_cache,
    features,
    image_proj,
    key_gain,
    out_weight,
    cross_gate,
    image_spans,
    evicted,
    placement,
):
    head_size = key_gain.shape[0]
    tokens, cols = cross_query.shape
    heads = cols // head_size
    patches = features.shape[1]
    half = patches // 2
    seq_pos = lax.axis_index("seq")
    head_pos = lax.axis_index("head")
    y, x, core = seq_pos // 4, (seq_pos // 2) % 2, seq_pos % 2
    head_x, head_z = head_pos // 4, head_pos % 4
    chunks = 4 * tokens // CHUNK
    rows = heads * CHUNK

    sent_part = lax.dynamic_slice_in_dim(features[0], (1 - core) * half, half)
    peer_part = send_seq(sent_part, core=1)
    stale = jnp.any(placement[:, None] == evicted, axis=1).reshape(8, 2)
    both = jnp.any(stale[:, 0] & stale[:, 1])
    use_own = lax.dynamic_index_in_dim(stale, seq_pos // 2, 0, keepdims=False)[0] == (core == 0)
    part_index = jnp.arange(8, dtype=jnp.int32)
    home = head_at(head_x + part_index % 2, head_z + part_index // 2).astype(jnp.int32)

    held = image_cache[0]
    q_blocks = [cross_query] + [send_seq(cross_query, y=-dy) for dy in (1, 2, 3)]
    held_x = send_seq(held, x=1)

    def rebuild(own_first, after=(), work=None, kv_of=None):
        pick = jnp.where(jnp.arange(2) == 0, own_first.astype(jnp.int32), core).astype(jnp.int32)
        parts = rebuild_parts(features, peer_part, image_proj, home, pick, after)
        if work is None:
            terms, state = sum_over_head(parts), (peer_part,)
        else:
            terms, state = sum_beside(parts, work, kv_of)
        mine = normalize(terms, key_gain, state[-1])
        other = send_seq(mine, x=1)
        pieces = (mine, other, send_seq(mine, core=1), send_seq(other, core=1))
        return pieces if work is None else (pieces, state)

    smem = pl.BlockSpec(memory_space=pltpu.SMEM)
    vmem = pl.BlockSpec(memory_space=pltpu.VMEM)
    order, first_all, stop_all, plan = pl.pallas_call(
        plan_kernel,
        in_specs=[smem] * 3 + [vmem],
        out_specs=[vmem] * 4,
        out_shape=[
            jax.ShapeDtypeStruct((4, tokens, tokens), jnp.bfloat16),
            jax.ShapeDtypeStruct((4 * tokens, head_size), jnp.int32),
            jax.ShapeDtypeStruct((4 * tokens, head_size), jnp.int32),
            jax.ShapeDtypeStruct((PLAN_ROWS, 128), jnp.int32),
        ],
        compiler_params=VMEM,
        name="plan",
    )(seq_pos.reshape(1).astype(jnp.int32), placement, evicted, image_spans.T.reshape(2, 16, tokens))
    state_shapes = [jax.ShapeDtypeStruct((chunks, rows, head_size), jnp.float32)] * 3

    def scratch(keys):
        return [pltpu.VMEM((rows, keys), jnp.float32)] * 2 + [
            pltpu.VMEM((keys, head_size), jnp.bfloat16),
            pltpu.VMEM((keys, 2 * head_size), jnp.bfloat16),
        ]

    def attend_first(*kv):
        return pl.pallas_call(
            functools.partial(begin_kernel, head_size),
            in_specs=[smem] + [vmem] * 9,
            out_specs=[vmem] * 4,
            out_shape=[jax.ShapeDtypeStruct((chunks, rows, head_size), jnp.bfloat16)] + state_shapes,
            scratch_shapes=scratch(patches),
            compiler_params=VMEM,
            name="attend_first",
        )(plan, *q_blocks, order, first_all, stop_all, *kv)

    def attend_more(state, limits, *kv):
        return state[:1] + pl.pallas_call(
            functools.partial(go_on_kernel, head_size, len(kv), limits),
            in_specs=[smem] + [vmem] * (6 + len(kv)),
            out_specs=[vmem] * 3,
            out_shape=state_shapes,
            scratch_shapes=scratch(patches),
            input_output_aliases={4: 0, 5: 1, 6: 2},
            compiler_params=VMEM,
            name="attend_more",
        )(plan, state[0], first_all, stop_all, *state[1:], *kv)

    work = (
        attend_first,
        lambda state, *kv: attend_more(state, (THIRD_ROW, TWO_THIRDS_ROW), *kv),
        lambda state, *kv: attend_more(state, (TWO_THIRDS_ROW, COUNT_ROW), *kv),
    )

    def kv_of(after):
        return held, send_seq(copy_after(held, after), core=1), held_x

    twice = lax.cond(
        both,
        lambda: jnp.stack(rebuild(~use_own, (q_blocks[1], q_blocks[3]))),
        lambda: jnp.zeros((4, half, 2 * head_size), jnp.bfloat16),
    )
    once, state = rebuild(use_own, (twice,), work, kv_of)
    partial_out = pl.pallas_call(
        functools.partial(rebuilt_kernel, head_size),
        in_specs=[smem] + [vmem] * 12,
        out_specs=[vmem] * 4,
        out_shape=[jax.ShapeDtypeStruct((tokens, cols + 128), jnp.bfloat16)] * 4,
        scratch_shapes=[pltpu.VMEM(s.shape, s.dtype) for s in state_shapes] + scratch(patches),
        compiler_params=VMEM,
        name="attend_rebuilt",
    )(plan, state[0], first_all, stop_all, *state[1:], order, *once, twice)
    arrived = [partial_out[0]] + [send_seq(partial_out[dy], y=dy) for dy in (1, 2, 3)]
    context = pl.pallas_call(
        functools.partial(merge_kernel, head_size),
        in_specs=[vmem] * 4,
        out_specs=vmem,
        out_shape=jax.ShapeDtypeStruct((tokens, cols), jnp.bfloat16),
        compiler_params=VMEM,
        name="merge",
    )(*arrived)

    near, far = gather_chips(context)
    target = head_at(head_x + part_index % 2, head_z + part_index // 2)
    offset = 2 * ((target // 2 - y) % 4) + (target % 2 - x) % 2
    source = jnp.zeros(8, jnp.int32)
    for at, place in enumerate((0, 1, 6, 2, 4, 7, 3, 5)):
        source = jnp.where(offset == place, at, source)
    parts = project_parts(
        (near, far, send_seq(near, core=1), send_seq(far, core=1)),
        out_weight,
        source.astype(jnp.int32),
        core.reshape(1).astype(jnp.int32),
    )
    summed_out = sum(term.astype(jnp.float32) for term in sum_over_head(parts))
    return (hidden.astype(jnp.float32) + jnp.tanh(cross_gate[0]) * summed_out).astype(jnp.bfloat16)


def solution(mesh):
    placed = (
        P("head", "seq"),
        P("seq", "head"),
        P("seq", None, "head"),
        P("seq", None, "head"),
        P("head", None),
        P(),
        P("head", "seq"),
        P(),
        P(),
        P(),
        P(),
    )
    return jax.shard_map(
        on_device, mesh=mesh, in_specs=placed, out_specs=P("head", "seq"), check_vma=False
    )
```

```python
import functools
import math

import jax
import jax.numpy as jnp
from jax import lax
from jax.experimental import pallas as pl
from jax.experimental.pallas import tpu as pltpu
from jax.sharding import PartitionSpec as P

MASKED_SCORE = -1e30
CHUNK = 32
COUNT_ROW = 18
ID_ROW = 19
THIRD_ROW = 20
TWO_THIRDS_ROW = 21
ZERO_ROW = 22
PLAN_ROWS = 24
VMEM = pltpu.CompilerParams(vmem_limit_bytes=20 * 1024 * 1024)


def seq_at(y, x, core):
    return (y % 4) * 4 + (x % 2) * 2 + core % 2


def head_at(x, z):
    return (x % 2) * 4 + z % 4


def send_seq(array, y=0, x=0, core=0):
    pairs = [
        (seq_at(a, b, c), seq_at(a + y, b + x, c + core)) for a in range(4) for b in range(2) for c in range(2)
    ]
    return lax.ppermute(array, "seq", pairs)


def send_head(array, x=0, z=0):
    return lax.ppermute(array, "head", [(head_at(a, b), head_at(a + x, b + z)) for a in range(2) for b in range(4)])


def add(*terms):
    return sum(term.astype(jnp.float32) for term in terms).astype(jnp.bfloat16)


def add_kernel(*refs):
    *terms, _, out_ref = refs
    out_ref[...] = sum(term[...].astype(jnp.float32) for term in terms).astype(out_ref.dtype)


def add_after(after, *terms):
    vmem = pl.BlockSpec(memory_space=pltpu.VMEM)
    return pl.pallas_call(
        add_kernel,
        in_specs=[vmem] * len(terms) + [pl.BlockSpec(memory_space=pl.ANY)],
        out_specs=vmem,
        out_shape=jax.ShapeDtypeStruct(terms[0].shape, terms[0].dtype),
        compiler_params=VMEM,
        name="add_after",
    )(*terms, after)


def sum_over_head(parts):
    p00, p01, p10, p11, p20, p21, p30, p31 = parts
    via_x = send_head(p21, x=1)
    down = send_head(p31, z=-1)
    across = send_head(p11, z=1)
    via_x, down, across = lax.optimization_barrier((via_x, down, across))
    p20 = add(p20, via_x)
    p01 = add(p01, down, across)
    up = send_head(p20, z=1)
    side = send_head(p01, x=1)
    last = send_head(p30, z=-1)
    p10 = add(p10, up)
    ahead = send_head(p10, z=1)
    return p00, last, side, ahead


def sum_beside(parts, work, kv_of):
    p00, p01, p10, p11, p20, p21, p30, p31 = parts
    up = send_head(p20, z=1)
    down = send_head(p21, z=-1)
    across = send_head(p11, z=1)
    last = send_head(p30, z=-1)
    kv = kv_of(p30)
    state = work[0](*kv[:2])
    p10 = add_after(state[-1], p10, up)
    p31 = add_after(state[-1], p31, down)
    held_x, p10, p31 = lax.optimization_barrier((kv[2], p10, p31))
    kv = kv[:2] + (held_x, send_seq(held_x, core=1))
    ahead = send_head(p10, z=1)
    behind = send_head(p31, z=-1)
    state = work[1](state, *kv)
    p01 = add_after(state[-1], p01, across, behind)
    side = send_head(p01, x=1)
    state = work[2](state, *kv)
    return (p00, last, ahead, side), state


def gather_chips(block):
    r30 = send_seq(block, y=1)
    r01 = send_seq(block, x=1)
    r10 = send_seq(block, y=-1)
    r30, r01, r10 = lax.optimization_barrier((r30, r01, r10))
    r20 = send_seq(r30, y=1)
    r31 = send_seq(r30, x=1)
    r11 = send_seq(r01, y=-1)
    r21 = send_seq(r20, x=1)
    return jnp.stack([block, r01, r30, r10]), jnp.stack([r20, r31, r11, r21])


def rebuild_kernel(pairs, order_ref, pick_ref, own_ref, peer_ref, proj0_ref, proj1_ref, *refs):
    *out_refs, rows_ref = refs[-2 * pairs - 1 :]
    step = pl.program_id(0)

    @pl.when(step == 0)
    def _():
        rows_ref[...] = jnp.where(pick_ref[0] > 0, own_ref[0], peer_ref[...])

    products = [
        jnp.dot(rows_ref[...], proj_ref[...], preferred_element_type=jnp.float32).astype(jnp.bfloat16)
        for proj_ref in (proj0_ref, proj1_ref)
    ]
    for at in range(pairs):

        @pl.when(step == at)
        def _():
            out_refs[2 * at][...] = products[0]
            out_refs[2 * at + 1][...] = products[1]


def rebuild_parts(features, peer_part, proj, order, pick, after):
    count, depth = peer_part.shape
    cols = proj.shape[1] // 8
    pairs = order.shape[0] // 2
    return pl.pallas_call(
        functools.partial(rebuild_kernel, pairs),
        grid_spec=pltpu.PrefetchScalarGridSpec(
            num_scalar_prefetch=2,
            grid=(pairs,),
            in_specs=[
                pl.BlockSpec((1, count, depth), lambda i, order, pick: (0, pick[1], 0)),
                pl.BlockSpec((count, depth), lambda i, order, pick: (0, 0)),
                pl.BlockSpec((depth, cols), lambda i, order, pick: (0, order[2 * i])),
                pl.BlockSpec((depth, cols), lambda i, order, pick: (0, order[2 * i + 1])),
            ]
            + [pl.BlockSpec(memory_space=pl.ANY)] * len(after),
            out_specs=[pl.BlockSpec((count, cols), lambda i, order, pick: (0, 0))] * (2 * pairs),
            scratch_shapes=[pltpu.VMEM((count, depth), jnp.bfloat16)],
        ),
        out_shape=[jax.ShapeDtypeStruct((count, cols), jnp.bfloat16)] * (2 * pairs),
        compiler_params=VMEM,
        name="rebuild_parts",
    )(order, pick, features, peer_part, proj, proj, *after)


def project_kernel(order_ref, core_ref, own0_ref, own1_ref, other0_ref, other1_ref, weight_ref, *out_refs):
    step = pl.program_id(0)
    even = core_ref[0] == 0
    tokens = own0_ref.shape[1]

    def block(first_ref, second_ref, at):
        return jnp.where(at < 4, first_ref[jnp.minimum(at, 3)], second_ref[jnp.maximum(at - 4, 0)])

    rows = []
    for part in range(2):
        at = order_ref[2 * step + part]
        own, other = block(own0_ref, own1_ref, at), block(other0_ref, other1_ref, at)
        rows += [jnp.where(even, own, other), jnp.where(even, other, own)]
    product = jnp.dot(
        jnp.concatenate(rows, axis=0), weight_ref[...], preferred_element_type=jnp.float32
    ).astype(jnp.bfloat16)
    for at in range(4):

        @pl.when(step == at)
        def _():
            out_refs[2 * at][...] = product[: 2 * tokens]
            out_refs[2 * at + 1][...] = product[2 * tokens :]


def project_parts(blocks, weight, order, core):
    _, tokens, depth = blocks[0].shape
    cols = weight.shape[1]
    return pl.pallas_call(
        project_kernel,
        grid_spec=pltpu.PrefetchScalarGridSpec(
            num_scalar_prefetch=2,
            grid=(4,),
            in_specs=[pl.BlockSpec((4, tokens, depth), lambda i, order, core: (0, 0, 0))] * 4
            + [pl.BlockSpec((depth, cols), lambda i, order, core: (0, 0))],
            out_specs=[pl.BlockSpec((2 * tokens, cols), lambda i, order, core: (0, 0))] * 8,
        ),
        out_shape=[jax.ShapeDtypeStruct((2 * tokens, cols), jnp.bfloat16)] * 8,
        compiler_params=VMEM,
        name="project_parts",
    )(order, core, *blocks, weight)


def plan_kernel(pos_ref, placement_ref, evicted_ref, spans_ref, order_ref, first_ref, stop_ref, plan_ref):
    seq_pos = pos_ref[0]
    y, x, core = seq_pos // 4, (seq_pos // 2) % 2, seq_pos % 2
    tokens = spans_ref.shape[2]
    chips = (seq_pos // 2, seq_at(y, x + 1, 0) // 2)

    def stale(slot):
        image = placement_ref[slot]
        return (image == evicted_ref[0]) | (image == evicted_ref[1])

    entries = []
    for chip in chips:
        for slot in (2 * chip + core, 2 * chip + 1 - core):
            entries.append((placement_ref[slot], ~stale(slot)))
    once, twice = [], []
    for chip in chips:
        low, high = stale(2 * chip), stale(2 * chip + 1)
        once.append((jnp.where(low, placement_ref[2 * chip], placement_ref[2 * chip + 1]), low | high))
        twice.append((placement_ref[2 * chip + 1], low & high))
    entries += once + twice
    slot_lane = lax.broadcasted_iota(jnp.int32, (CHUNK, 128), 1)
    ids = jnp.full((CHUNK, 128), -1, jnp.int32)
    for at, (image, live) in enumerate(entries):
        ids = jnp.where(slot_lane == at, jnp.where(live, image, -1), ids)

    up = lax.broadcasted_iota(jnp.int32, (tokens, tokens), 0)
    along = lax.broadcasted_iota(jnp.int32, (tokens, tokens), 1)
    wanted = []
    for dy in range(4):
        block = seq_at(y + dy, x, core)
        first = jnp.broadcast_to(spans_ref[0, pl.ds(block, 1), :].astype(jnp.float32), (tokens, tokens))
        stop = jnp.broadcast_to(spans_ref[1, pl.ds(block, 1), :].astype(jnp.float32), (tokens, tokens))
        down = jnp.sum(jnp.where(up == along, first, 0.0), axis=1, keepdims=True)
        earlier = (down < first) | ((down == first) & (up < along))
        rank = jnp.sum(jnp.where(earlier, 1.0, 0.0), axis=0, keepdims=True).astype(jnp.int32)
        order = jnp.where(up == rank, 1.0, 0.0)
        order_ref[dy] = order.astype(jnp.bfloat16)
        first = jnp.broadcast_to(jnp.sum(order * first, axis=1, keepdims=True), (tokens, 128)).astype(jnp.int32)
        stop = jnp.broadcast_to(jnp.sum(order * stop, axis=1, keepdims=True), (tokens, 128)).astype(jnp.int32)
        first_ref[dy * tokens : (dy + 1) * tokens, :] = first
        stop_ref[dy * tokens : (dy + 1) * tokens, :] = stop
        for part in range(tokens // CHUNK):
            rows = slice(part * CHUNK, (part + 1) * CHUNK)
            seen = (first[rows] <= ids) & (ids < stop[rows])
            wanted.append(jnp.max(jnp.where(seen, 1, 0), axis=0, keepdims=True))
    places, total = [], jnp.zeros((1, 128), jnp.int32)
    for want in wanted:
        places.append(total)
        total = total + want
    for place in range(COUNT_ROW):
        row = jnp.zeros((1, 128), jnp.int32)
        for chunk, (want, at) in enumerate(zip(wanted, places)):
            row = jnp.where((want > 0) & (at == place), chunk, row)
        plan_ref[place : place + 1, :] = row
    plan_ref[COUNT_ROW : COUNT_ROW + 1, :] = total
    plan_ref[ID_ROW : ID_ROW + 1, :] = ids[:1]
    plan_ref[ZERO_ROW:, :] = jnp.zeros((PLAN_ROWS - ZERO_ROW, 128), jnp.int32)
    lane = slot_lane[:1]
    counts = [jnp.sum(jnp.where(lane == at, total, 0), axis=1, keepdims=True) for at in range(4)]
    share = ((sum(counts) + 2) * 21846) >> 16
    third, two_thirds = jnp.zeros((1, 128), jnp.int32), jnp.zeros((1, 128), jnp.int32)
    before = jnp.zeros((1, 1), jnp.int32)
    for at, count in enumerate(counts):
        if at < 2:
            third = jnp.where(lane == at, jnp.clip(share - before, 0, count), third)
        two_thirds = jnp.where(lane == at, jnp.clip(2 * share - before, 0, count), two_thirds)
        before = before + count
    plan_ref[THIRD_ROW : THIRD_ROW + 1, :] = third
    plan_ref[TWO_THIRDS_ROW : TWO_THIRDS_ROW + 1, :] = two_thirds


def sweep(head_size, plan_ref, low, limits, q_ref, first_ref, stop_ref, kv_parts, state, even, odd, keys, wide):
    factor = math.log2(math.e) * head_size ** (-0.5)
    heads = q_ref.shape[1] // CHUNK
    m_ref, l_ref, acc_ref = state

    for slot, part in enumerate(kv_parts, low):
        begin, end = (plan_ref[row, slot] for row in limits)

        def score(place, into):
            into[...] = lax.dot_general(
                q_ref[plan_ref[place, slot]],
                keys[...],
                (((1,), (1,)), ((), ())),
                preferred_element_type=jnp.float32,
            )

        def take(place, scores_ref):
            chunk = plan_ref[place, slot]
            image = jnp.where(place < end, plan_ref[ID_ROW, slot], -1)
            scores = scores_ref[...]
            here = jnp.broadcast_to(jnp.max(scores, axis=1, keepdims=True), (scores.shape[0], head_size))
            weights = jnp.exp2((scores - here[:, :1]) * factor)
            both = jnp.dot(weights.astype(jnp.bfloat16), wide[...], preferred_element_type=jnp.float32)
            mixed, total = both[:, :head_size], both[:, head_size:]
            tokens = pl.ds(pl.multiple_of(chunk * CHUNK, CHUNK), CHUNK)
            seen = (first_ref[tokens, :] <= image) & (image < stop_ref[tokens, :])
            seen = jnp.concatenate([seen.astype(jnp.int32)] * heads, axis=0) > 0
            before = m_ref[chunk]
            after = jnp.where(seen, jnp.maximum(before, here), before)
            keep = jnp.exp2((before - after) * factor)
            gain = jnp.where(seen, jnp.exp2((here - after) * factor), 0.0)
            m_ref[chunk] = after
            l_ref[chunk] = l_ref[chunk] * keep + gain * total
            acc_ref[chunk] = acc_ref[chunk] * keep + gain * mixed

        @pl.when(end > begin)
        def _():
            at = 0
            for rows_of in part:
                block = rows_of()
                rows = slice(at, at + block.shape[0])
                keys[rows, :] = block[:, :head_size]
                wide[rows, :head_size] = block[:, head_size:]
                at += block.shape[0]
            wide[:, head_size:] = jnp.ones_like(wide[:, head_size:])
            score(begin, even)

            def body(at, carry):
                place = begin + 2 * at
                score(place + 1, odd)
                take(place, even)
                score(place + 2, even)
                take(place + 1, odd)
                return carry

            lax.fori_loop(0, (end - begin + 1) // 2, body, 0)


def copy_kernel(array_ref, after_ref, out_ref):
    out_ref[...] = array_ref[...]


def copy_after(array, after):
    vmem = pl.BlockSpec(memory_space=pltpu.VMEM)
    return pl.pallas_call(
        copy_kernel,
        in_specs=[vmem, pl.BlockSpec(memory_space=pl.ANY)],
        out_specs=vmem,
        out_shape=jax.ShapeDtypeStruct(array.shape, array.dtype),
        compiler_params=VMEM,
        name="copy_after",
    )(array, after)


def begin_kernel(head_size, plan, q0, q1, q2, q3, order, first, stop, a, b, qs, m, l, acc, *work):
    heads = q0.shape[1] // head_size
    per_block = q0.shape[0] // CHUNK
    for block, q_ref in enumerate((q0, q1, q2, q3)):
        ordered = jnp.dot(order[block], q_ref[...], preferred_element_type=jnp.float32).astype(jnp.bfloat16)
        for part in range(per_block):
            for head in range(heads):
                qs[block * per_block + part, head * CHUNK : (head + 1) * CHUNK, :] = ordered[
                    part * CHUNK : (part + 1) * CHUNK, head * head_size : (head + 1) * head_size
                ]
    m[...] = jnp.full_like(m, MASKED_SCORE)
    l[...] = jnp.zeros_like(l)
    acc[...] = jnp.zeros_like(acc)
    kv_parts = [[lambda r=r: r[...]] for r in (a, b)]
    sweep(head_size, plan, 0, (ZERO_ROW, THIRD_ROW), qs, first, stop, kv_parts, (m, l, acc), *work)


def go_on_kernel(head_size, parts, limits, plan, qs, first, stop, m_in, l_in, acc_in, *refs):
    kv, (m, l, acc, *work) = refs[:parts], refs[parts:]
    m[...] = m_in[...]
    l[...] = l_in[...]
    acc[...] = acc_in[...]
    sweep(head_size, plan, 0, limits, qs, first, stop, [[lambda r=r: r[...]] for r in kv], (m, l, acc), *work)


def rebuilt_kernel(head_size, plan, qs, first, stop, m_in, l_in, acc_in, order, *refs):
    *once, twice, o0, o1, o2, o3, m, l, acc, even, odd, keys, wide = refs
    factor = math.log2(math.e) * head_size ** (-0.5)
    tokens = o0.shape[0]
    heads = qs.shape[1] // CHUNK
    per_block = tokens // CHUNK
    m[...] = m_in[...]
    l[...] = l_in[...]
    acc[...] = acc_in[...]
    kv_parts = [[lambda r=once[i]: r[...], lambda r=once[i + 2]: r[...]] for i in range(2)]
    kv_parts += [[lambda i=i: twice[i], lambda i=i: twice[i + 2]] for i in range(2)]
    sweep(head_size, plan, 4, (ZERO_ROW, COUNT_ROW), qs, first, stop, kv_parts, (m, l, acc), even, odd, keys, wide)
    lanes = lax.broadcasted_iota(jnp.int32, (tokens, 128), 1)
    for block, out in enumerate((o0, o1, o2, o3)):
        extra = jnp.zeros((tokens, 128), jnp.float32)
        for head in range(heads):
            rows = slice(head * CHUNK, (head + 1) * CHUNK)
            chunks = range(block * per_block, (block + 1) * per_block)
            high = jnp.concatenate([m[chunk, rows, :] for chunk in chunks], axis=0)
            total = jnp.concatenate([l[chunk, rows, :] for chunk in chunks], axis=0)
            mixed = jnp.concatenate([acc[chunk, rows, :] for chunk in chunks], axis=0)
            some = total > 0.0
            safe = jnp.where(some, total, 1.0)
            level = jnp.where(some, high * factor + jnp.log2(safe), MASKED_SCORE)
            ordered = (mixed / safe).astype(jnp.bfloat16)
            out[:, head * head_size : (head + 1) * head_size] = lax.dot_general(
                order[block], ordered, (((0,), (0,)), ((), ())), preferred_element_type=jnp.float32
            ).astype(jnp.bfloat16)
            for piece in range(3):
                rounded = level.astype(jnp.bfloat16).astype(jnp.float32)
                extra = jnp.where(lanes == piece * heads + head, rounded, extra)
                level = level - rounded
        out[:, heads * head_size :] = lax.dot_general(
            order[block], extra.astype(jnp.bfloat16), (((0,), (0,)), ((), ())), preferred_element_type=jnp.float32
        ).astype(jnp.bfloat16)


def merge_kernel(head_size, a, b, c, d, out):
    heads = out.shape[1] // head_size
    parts = (a, b, c, d)
    extras = [part[:, heads * head_size :].astype(jnp.float32) for part in parts]
    for head in range(heads):
        cols = slice(head * head_size, (head + 1) * head_size)
        levels = [sum(e[:, p * heads + head : p * heads + head + 1] for p in range(3)) for e in extras]
        top = functools.reduce(jnp.maximum, levels)
        shares = [jnp.exp2(level - top) for level in levels]
        mixed = sum(share * part[:, cols].astype(jnp.float32) for share, part in zip(shares, parts))
        out[:, cols] = (mixed / sum(shares)).astype(jnp.bfloat16)


def normalize_kernel(gain_ref, after_ref, a, b, c, d, out):
    head_size = gain_ref.shape[1]
    keys, values = (
        sum(part[:, low : low + head_size].astype(jnp.float32) for part in (a, b, c, d)) for low in (0, head_size)
    )
    inverse = lax.rsqrt(jnp.mean(keys * keys, axis=-1, keepdims=True) + 1e-05)
    out[:, :head_size] = (keys * inverse * gain_ref[...]).astype(out.dtype)
    out[:, head_size:] = values.astype(out.dtype)


def normalize(terms, key_gain, after):
    vmem = pl.BlockSpec(memory_space=pltpu.VMEM)
    return pl.pallas_call(
        normalize_kernel,
        in_specs=[vmem, pl.BlockSpec(memory_space=pl.ANY)] + [vmem] * 4,
        out_specs=vmem,
        out_shape=jax.ShapeDtypeStruct(terms[0].shape, jnp.bfloat16),
        compiler_params=VMEM,
        name="normalize",
    )(key_gain[None], after, *terms)


def on_device(
    hidden,
    cross_query,
    image_cache,
    features,
    image_proj,
    key_gain,
    out_weight,
    cross_gate,
    image_spans,
    evicted,
    placement,
):
    head_size = key_gain.shape[0]
    tokens, cols = cross_query.shape
    heads = cols // head_size
    patches = features.shape[1]
    half = patches // 2
    seq_pos = lax.axis_index("seq")
    head_pos = lax.axis_index("head")
    y, x, core = seq_pos // 4, (seq_pos // 2) % 2, seq_pos % 2
    head_x, head_z = head_pos // 4, head_pos % 4
    chunks = 4 * tokens // CHUNK
    rows = heads * CHUNK

    sent_part = lax.dynamic_slice_in_dim(features[0], (1 - core) * half, half)
    peer_part = send_seq(sent_part, core=1)
    stale = jnp.any(placement[:, None] == evicted, axis=1).reshape(8, 2)
    both = jnp.any(stale[:, 0] & stale[:, 1])
    use_own = lax.dynamic_index_in_dim(stale, seq_pos // 2, 0, keepdims=False)[0] == (core == 0)
    part_index = jnp.arange(8, dtype=jnp.int32)
    far_index = part_index[:2] + 4
    near_index = jnp.where(part_index[:6] < 4, part_index[:6], part_index[:6] + 2)
    far_home, near_home = (
        head_at(head_x + index % 2, head_z + index // 2).astype(jnp.int32) for index in (far_index, near_index)
    )

    held = image_cache[0]
    q_blocks = [cross_query] + [send_seq(cross_query, y=-dy) for dy in (1, 2, 3)]
    held_x = send_seq(held, x=1)

    def rebuild(own_first, after=(), work=None, kv_of=None):
        pick = jnp.where(jnp.arange(2) == 0, own_first.astype(jnp.int32), core).astype(jnp.int32)
        p20, p21 = rebuild_parts(features, peer_part, image_proj, far_home, pick, after)
        parts = rebuild_parts(features, peer_part, image_proj, near_home, pick, (p20,) if work is None else (p20, q_blocks[2]))
        parts = [*parts[:4], p20, p21, *parts[4:]]
        if work is None:
            terms, state = sum_over_head(parts), (peer_part,)
        else:
            terms, state = sum_beside(parts, work, kv_of)
        mine = normalize(terms, key_gain, state[-1])
        other = send_seq(mine, x=1)
        pieces = (mine, other, send_seq(mine, core=1), send_seq(other, core=1))
        return pieces if work is None else (pieces, state)

    smem = pl.BlockSpec(memory_space=pltpu.SMEM)
    vmem = pl.BlockSpec(memory_space=pltpu.VMEM)
    order, first_all, stop_all, plan = pl.pallas_call(
        plan_kernel,
        in_specs=[smem] * 3 + [vmem],
        out_specs=[vmem] * 4,
        out_shape=[
            jax.ShapeDtypeStruct((4, tokens, tokens), jnp.bfloat16),
            jax.ShapeDtypeStruct((4 * tokens, head_size), jnp.int32),
            jax.ShapeDtypeStruct((4 * tokens, head_size), jnp.int32),
            jax.ShapeDtypeStruct((PLAN_ROWS, 128), jnp.int32),
        ],
        compiler_params=VMEM,
        name="plan",
    )(seq_pos.reshape(1).astype(jnp.int32), placement, evicted, image_spans.T.reshape(2, 16, tokens))
    state_shapes = [jax.ShapeDtypeStruct((chunks, rows, head_size), jnp.float32)] * 3

    def scratch(keys):
        return [pltpu.VMEM((rows, keys), jnp.float32)] * 2 + [
            pltpu.VMEM((keys, head_size), jnp.bfloat16),
            pltpu.VMEM((keys, 2 * head_size), jnp.bfloat16),
        ]

    def attend_first(*kv):
        return pl.pallas_call(
            functools.partial(begin_kernel, head_size),
            in_specs=[smem] + [vmem] * 9,
            out_specs=[vmem] * 4,
            out_shape=[jax.ShapeDtypeStruct((chunks, rows, head_size), jnp.bfloat16)] + state_shapes,
            scratch_shapes=scratch(patches),
            compiler_params=VMEM,
            name="attend_first",
        )(plan, *q_blocks, order, first_all, stop_all, *kv)

    def attend_more(state, limits, *kv):
        return state[:1] + pl.pallas_call(
            functools.partial(go_on_kernel, head_size, len(kv), limits),
            in_specs=[smem] + [vmem] * (6 + len(kv)),
            out_specs=[vmem] * 3,
            out_shape=state_shapes,
            scratch_shapes=scratch(patches),
            input_output_aliases={4: 0, 5: 1, 6: 2},
            compiler_params=VMEM,
            name="attend_more",
        )(plan, state[0], first_all, stop_all, *state[1:], *kv)

    work = (
        attend_first,
        lambda state, *kv: attend_more(state, (THIRD_ROW, TWO_THIRDS_ROW), *kv),
        lambda state, *kv: attend_more(state, (TWO_THIRDS_ROW, COUNT_ROW), *kv),
    )

    def kv_of(after):
        return held, send_seq(copy_after(held, after), core=1), held_x

    twice = lax.cond(
        both,
        lambda: jnp.stack(rebuild(~use_own, (q_blocks[1], q_blocks[3], order))),
        lambda: jnp.zeros((4, half, 2 * head_size), jnp.bfloat16),
    )
    once, state = rebuild(use_own, (twice,), work, kv_of)
    partial_out = pl.pallas_call(
        functools.partial(rebuilt_kernel, head_size),
        in_specs=[smem] + [vmem] * 12,
        out_specs=[vmem] * 4,
        out_shape=[jax.ShapeDtypeStruct((tokens, cols + 128), jnp.bfloat16)] * 4,
        scratch_shapes=[pltpu.VMEM(s.shape, s.dtype) for s in state_shapes] + scratch(patches),
        compiler_params=VMEM,
        name="attend_rebuilt",
    )(plan, state[0], first_all, stop_all, *state[1:], order, *once, twice)
    arrived = [partial_out[0]] + [send_seq(partial_out[dy], y=dy) for dy in (1, 2, 3)]
    context = pl.pallas_call(
        functools.partial(merge_kernel, head_size),
        in_specs=[vmem] * 4,
        out_specs=vmem,
        out_shape=jax.ShapeDtypeStruct((tokens, cols), jnp.bfloat16),
        compiler_params=VMEM,
        name="merge",
    )(*arrived)

    near, far = gather_chips(context)
    target = head_at(head_x + part_index % 2, head_z + part_index // 2)
    offset = 2 * ((target // 2 - y) % 4) + (target % 2 - x) % 2
    source = jnp.zeros(8, jnp.int32)
    for at, place in enumerate((0, 1, 6, 2, 4, 7, 3, 5)):
        source = jnp.where(offset == place, at, source)
    parts = project_parts(
        (near, far, send_seq(near, core=1), send_seq(far, core=1)),
        out_weight,
        source.astype(jnp.int32),
        core.reshape(1).astype(jnp.int32),
    )
    summed_out = sum(term.astype(jnp.float32) for term in sum_over_head(parts))
    return (hidden.astype(jnp.float32) + jnp.tanh(cross_gate[0]) * summed_out).astype(jnp.bfloat16)


def solution(mesh):
    placed = (
        P("head", "seq"),
        P("seq", "head"),
        P("seq", None, "head"),
        P("seq", None, "head"),
        P("head", None),
        P(),
        P("head", "seq"),
        P(),
        P(),
        P(),
        P(),
    )
    return jax.shard_map(
        on_device, mesh=mesh, in_specs=placed, out_specs=P("head", "seq"), check_vma=False
    )
```

```python
import functools
import math

import jax
import jax.numpy as jnp
from jax import lax
from jax.experimental import pallas as pl
from jax.experimental.pallas import tpu as pltpu
from jax.sharding import PartitionSpec as P

MASKED_SCORE = -1e30
CHUNK = 32
COUNT_ROW = 18
ID_ROW = 19
THIRD_ROW = 20
TWO_THIRDS_ROW = 21
ZERO_ROW = 22
PLAN_ROWS = 24
VMEM = pltpu.CompilerParams(vmem_limit_bytes=20 * 1024 * 1024)


def seq_at(y, x, core):
    return (y % 4) * 4 + (x % 2) * 2 + core % 2


def head_at(x, z):
    return (x % 2) * 4 + z % 4


def send_seq(array, y=0, x=0, core=0):
    pairs = [
        (seq_at(a, b, c), seq_at(a + y, b + x, c + core)) for a in range(4) for b in range(2) for c in range(2)
    ]
    return lax.ppermute(array, "seq", pairs)


def send_head(array, x=0, z=0):
    return lax.ppermute(array, "head", [(head_at(a, b), head_at(a + x, b + z)) for a in range(2) for b in range(4)])


def add(*terms):
    return sum(term.astype(jnp.float32) for term in terms).astype(jnp.bfloat16)


def add_kernel(*refs):
    *terms, _, out_ref = refs
    out_ref[...] = sum(term[...].astype(jnp.float32) for term in terms).astype(out_ref.dtype)


def add_after(after, *terms):
    vmem = pl.BlockSpec(memory_space=pltpu.VMEM)
    return pl.pallas_call(
        add_kernel,
        in_specs=[vmem] * len(terms) + [pl.BlockSpec(memory_space=pl.ANY)],
        out_specs=vmem,
        out_shape=jax.ShapeDtypeStruct(terms[0].shape, terms[0].dtype),
        compiler_params=VMEM,
        name="add_after",
    )(*terms, after)


def sum_over_head(parts):
    p00, p01, p10, p11, p20, p21, p30, p31 = parts
    via_x = send_head(p21, x=1)
    down = send_head(p31, z=-1)
    across = send_head(p11, x=1)
    last = send_head(p30, z=-1)
    p20 = add(p20, via_x)
    p01 = add(p01, down)
    up = send_head(p20, z=1)
    side = send_head(p01, x=1)
    p10 = add(p10, across, up)
    ahead = send_head(p10, z=1)
    return p00, last, side, ahead


def sum_beside(parts, work, kv_of):
    p00, p01, p10, p11, p20, p21, p30, p31 = parts
    up = send_head(p20, z=1)
    down = send_head(p21, z=-1)
    across = send_head(p11, z=1)
    last = send_head(p30, z=-1)
    kv = kv_of(p30)
    state = work[0](*kv[:2])
    p10 = add_after(state[-1], p10, up)
    p31 = add_after(state[-1], p31, down)
    held_x, p10, p31 = lax.optimization_barrier((kv[2], p10, p31))
    kv = kv[:2] + (held_x, send_seq(held_x, core=1))
    ahead = send_head(p10, z=1)
    behind = send_head(p31, z=-1)
    state = work[1](state, *kv)
    p01 = add_after(state[-1], p01, across, behind)
    side = send_head(p01, x=1)
    state = work[2](state, *kv)
    return (p00, last, ahead, side), state


def gather_chips(block):
    r30 = send_seq(block, y=1)
    r01 = send_seq(block, x=1)
    r10 = send_seq(block, y=-1)
    r30, r01, r10 = lax.optimization_barrier((r30, r01, r10))
    r20 = send_seq(r30, y=1)
    r31 = send_seq(r30, x=1)
    r11 = send_seq(r01, y=-1)
    r21 = send_seq(r20, x=1)
    return jnp.stack([block, r01, r30, r10]), jnp.stack([r20, r31, r11, r21])


def rebuild_kernel(order_ref, pick_ref, own_ref, peer_ref, proj0_ref, proj1_ref, *refs):
    *out_refs, rows_ref = refs[-9:]
    step = pl.program_id(0)

    @pl.when(step == 0)
    def _():
        rows_ref[...] = jnp.where(pick_ref[0] > 0, own_ref[0], peer_ref[...])

    products = [
        jnp.dot(rows_ref[...], proj_ref[...], preferred_element_type=jnp.float32).astype(jnp.bfloat16)
        for proj_ref in (proj0_ref, proj1_ref)
    ]
    for at in range(4):

        @pl.when(step == at)
        def _():
            out_refs[2 * at][...] = products[0]
            out_refs[2 * at + 1][...] = products[1]


def rebuild_parts(features, peer_part, proj, order, pick, after):
    count, depth = peer_part.shape
    cols = proj.shape[1] // 8
    return pl.pallas_call(
        rebuild_kernel,
        grid_spec=pltpu.PrefetchScalarGridSpec(
            num_scalar_prefetch=2,
            grid=(4,),
            in_specs=[
                pl.BlockSpec((1, count, depth), lambda i, order, pick: (0, pick[1], 0)),
                pl.BlockSpec((count, depth), lambda i, order, pick: (0, 0)),
                pl.BlockSpec((depth, cols), lambda i, order, pick: (0, order[2 * i])),
                pl.BlockSpec((depth, cols), lambda i, order, pick: (0, order[2 * i + 1])),
            ]
            + [pl.BlockSpec(memory_space=pl.ANY)] * len(after),
            out_specs=[pl.BlockSpec((count, cols), lambda i, order, pick: (0, 0))] * 8,
            scratch_shapes=[pltpu.VMEM((count, depth), jnp.bfloat16)],
        ),
        out_shape=[jax.ShapeDtypeStruct((count, cols), jnp.bfloat16)] * 8,
        compiler_params=VMEM,
        name="rebuild_parts",
    )(order, pick, features, peer_part, proj, proj, *after)


def project_kernel(order_ref, core_ref, own0_ref, own1_ref, other0_ref, other1_ref, weight_ref, *out_refs):
    step = pl.program_id(0)
    even = core_ref[0] == 0
    tokens = own0_ref.shape[1]

    def block(first_ref, second_ref, at):
        return jnp.where(at < 4, first_ref[jnp.minimum(at, 3)], second_ref[jnp.maximum(at - 4, 0)])

    rows = []
    for part in range(2):
        at = order_ref[2 * step + part]
        own, other = block(own0_ref, own1_ref, at), block(other0_ref, other1_ref, at)
        rows += [jnp.where(even, own, other), jnp.where(even, other, own)]
    product = jnp.dot(
        jnp.concatenate(rows, axis=0), weight_ref[...], preferred_element_type=jnp.float32
    ).astype(jnp.bfloat16)
    for at in range(4):

        @pl.when(step == at)
        def _():
            out_refs[2 * at][...] = product[: 2 * tokens]
            out_refs[2 * at + 1][...] = product[2 * tokens :]


def project_parts(blocks, weight, order, core):
    _, tokens, depth = blocks[0].shape
    cols = weight.shape[1]
    return pl.pallas_call(
        project_kernel,
        grid_spec=pltpu.PrefetchScalarGridSpec(
            num_scalar_prefetch=2,
            grid=(4,),
            in_specs=[pl.BlockSpec((4, tokens, depth), lambda i, order, core: (0, 0, 0))] * 4
            + [pl.BlockSpec((depth, cols), lambda i, order, core: (0, 0))],
            out_specs=[pl.BlockSpec((2 * tokens, cols), lambda i, order, core: (0, 0))] * 8,
        ),
        out_shape=[jax.ShapeDtypeStruct((2 * tokens, cols), jnp.bfloat16)] * 8,
        compiler_params=VMEM,
        name="project_parts",
    )(order, core, *blocks, weight)


def plan_kernel(pos_ref, placement_ref, evicted_ref, spans_ref, order_ref, first_ref, stop_ref, plan_ref):
    seq_pos = pos_ref[0]
    y, x, core = seq_pos // 4, (seq_pos // 2) % 2, seq_pos % 2
    tokens = spans_ref.shape[2]
    chips = (seq_pos // 2, seq_at(y, x + 1, 0) // 2)

    def stale(slot):
        image = placement_ref[slot]
        return (image == evicted_ref[0]) | (image == evicted_ref[1])

    entries = []
    for chip in chips:
        for slot in (2 * chip + core, 2 * chip + 1 - core):
            entries.append((placement_ref[slot], ~stale(slot)))
    once, twice = [], []
    for chip in chips:
        low, high = stale(2 * chip), stale(2 * chip + 1)
        once.append((jnp.where(low, placement_ref[2 * chip], placement_ref[2 * chip + 1]), low | high))
        twice.append((placement_ref[2 * chip + 1], low & high))
    entries += once + twice
    slot_lane = lax.broadcasted_iota(jnp.int32, (CHUNK, 128), 1)
    ids = jnp.full((CHUNK, 128), -1, jnp.int32)
    for at, (image, live) in enumerate(entries):
        ids = jnp.where(slot_lane == at, jnp.where(live, image, -1), ids)

    up = lax.broadcasted_iota(jnp.int32, (tokens, tokens), 0)
    along = lax.broadcasted_iota(jnp.int32, (tokens, tokens), 1)
    wanted = []
    for dy in range(4):
        block = seq_at(y + dy, x, core)
        first = jnp.broadcast_to(spans_ref[0, pl.ds(block, 1), :].astype(jnp.float32), (tokens, tokens))
        stop = jnp.broadcast_to(spans_ref[1, pl.ds(block, 1), :].astype(jnp.float32), (tokens, tokens))
        down = jnp.sum(jnp.where(up == along, first, 0.0), axis=1, keepdims=True)
        earlier = (down < first) | ((down == first) & (up < along))
        rank = jnp.sum(jnp.where(earlier, 1.0, 0.0), axis=0, keepdims=True).astype(jnp.int32)
        order = jnp.where(up == rank, 1.0, 0.0)
        order_ref[dy] = order.astype(jnp.bfloat16)
        first = jnp.broadcast_to(jnp.sum(order * first, axis=1, keepdims=True), (tokens, 128)).astype(jnp.int32)
        stop = jnp.broadcast_to(jnp.sum(order * stop, axis=1, keepdims=True), (tokens, 128)).astype(jnp.int32)
        first_ref[dy * tokens : (dy + 1) * tokens, :] = first
        stop_ref[dy * tokens : (dy + 1) * tokens, :] = stop
        for part in range(tokens // CHUNK):
            rows = slice(part * CHUNK, (part + 1) * CHUNK)
            seen = (first[rows] <= ids) & (ids < stop[rows])
            wanted.append(jnp.max(jnp.where(seen, 1, 0), axis=0, keepdims=True))
    places, total = [], jnp.zeros((1, 128), jnp.int32)
    for want in wanted:
        places.append(total)
        total = total + want
    for place in range(COUNT_ROW):
        row = jnp.zeros((1, 128), jnp.int32)
        for chunk, (want, at) in enumerate(zip(wanted, places)):
            row = jnp.where((want > 0) & (at == place), chunk, row)
        plan_ref[place : place + 1, :] = row
    plan_ref[COUNT_ROW : COUNT_ROW + 1, :] = total
    plan_ref[ID_ROW : ID_ROW + 1, :] = ids[:1]
    plan_ref[ZERO_ROW:, :] = jnp.zeros((PLAN_ROWS - ZERO_ROW, 128), jnp.int32)
    lane = slot_lane[:1]
    counts = [jnp.sum(jnp.where(lane == at, total, 0), axis=1, keepdims=True) for at in range(4)]
    share = ((sum(counts) + 2) * 21846) >> 16
    third, two_thirds = jnp.zeros((1, 128), jnp.int32), jnp.zeros((1, 128), jnp.int32)
    before = jnp.zeros((1, 1), jnp.int32)
    for at, count in enumerate(counts):
        if at < 2:
            third = jnp.where(lane == at, jnp.clip(share - before, 0, count), third)
        two_thirds = jnp.where(lane == at, jnp.clip(2 * share - before, 0, count), two_thirds)
        before = before + count
    plan_ref[THIRD_ROW : THIRD_ROW + 1, :] = third
    plan_ref[TWO_THIRDS_ROW : TWO_THIRDS_ROW + 1, :] = two_thirds


def sweep(head_size, plan_ref, low, limits, q_ref, first_ref, stop_ref, kv_parts, state, even, odd, keys, wide):
    factor = math.log2(math.e) * head_size ** (-0.5)
    heads = q_ref.shape[1] // CHUNK
    m_ref, l_ref, acc_ref = state

    for slot, part in enumerate(kv_parts, low):
        begin, end = (plan_ref[row, slot] for row in limits)

        def score(place, into):
            into[...] = lax.dot_general(
                q_ref[plan_ref[place, slot]],
                keys[...],
                (((1,), (1,)), ((), ())),
                preferred_element_type=jnp.float32,
            )

        def take(place, scores_ref):
            chunk = plan_ref[place, slot]
            image = jnp.where(place < end, plan_ref[ID_ROW, slot], -1)
            scores = scores_ref[...]
            here = jnp.broadcast_to(jnp.max(scores, axis=1, keepdims=True), (scores.shape[0], head_size))
            weights = jnp.exp2((scores - here[:, :1]) * factor)
            both = jnp.dot(weights.astype(jnp.bfloat16), wide[...], preferred_element_type=jnp.float32)
            mixed, total = both[:, :head_size], both[:, head_size:]
            tokens = pl.ds(pl.multiple_of(chunk * CHUNK, CHUNK), CHUNK)
            seen = (first_ref[tokens, :] <= image) & (image < stop_ref[tokens, :])
            seen = jnp.concatenate([seen.astype(jnp.int32)] * heads, axis=0) > 0
            before = m_ref[chunk]
            after = jnp.where(seen, jnp.maximum(before, here), before)
            keep = jnp.exp2((before - after) * factor)
            gain = jnp.where(seen, jnp.exp2((here - after) * factor), 0.0)
            m_ref[chunk] = after
            l_ref[chunk] = l_ref[chunk] * keep + gain * total
            acc_ref[chunk] = acc_ref[chunk] * keep + gain * mixed

        @pl.when(end > begin)
        def _():
            at = 0
            for rows_of in part:
                block = rows_of()
                rows = slice(at, at + block.shape[0])
                keys[rows, :] = block[:, :head_size]
                wide[rows, :head_size] = block[:, head_size:]
                at += block.shape[0]
            wide[:, head_size:] = jnp.ones_like(wide[:, head_size:])
            score(begin, even)

            def body(at, carry):
                place = begin + 2 * at
                score(place + 1, odd)
                take(place, even)
                score(place + 2, even)
                take(place + 1, odd)
                return carry

            lax.fori_loop(0, (end - begin + 1) // 2, body, 0)


def copy_kernel(array_ref, after_ref, out_ref):
    out_ref[...] = array_ref[...]


def copy_after(array, after):
    vmem = pl.BlockSpec(memory_space=pltpu.VMEM)
    return pl.pallas_call(
        copy_kernel,
        in_specs=[vmem, pl.BlockSpec(memory_space=pl.ANY)],
        out_specs=vmem,
        out_shape=jax.ShapeDtypeStruct(array.shape, array.dtype),
        compiler_params=VMEM,
        name="copy_after",
    )(array, after)


def begin_kernel(head_size, plan, q0, q1, q2, q3, order, first, stop, a, b, qs, m, l, acc, *work):
    heads = q0.shape[1] // head_size
    per_block = q0.shape[0] // CHUNK
    for block, q_ref in enumerate((q0, q1, q2, q3)):
        ordered = jnp.dot(order[block], q_ref[...], preferred_element_type=jnp.float32).astype(jnp.bfloat16)
        for part in range(per_block):
            for head in range(heads):
                qs[block * per_block + part, head * CHUNK : (head + 1) * CHUNK, :] = ordered[
                    part * CHUNK : (part + 1) * CHUNK, head * head_size : (head + 1) * head_size
                ]
    m[...] = jnp.full_like(m, MASKED_SCORE)
    l[...] = jnp.zeros_like(l)
    acc[...] = jnp.zeros_like(acc)
    kv_parts = [[lambda r=r: r[...]] for r in (a, b)]
    sweep(head_size, plan, 0, (ZERO_ROW, THIRD_ROW), qs, first, stop, kv_parts, (m, l, acc), *work)


def go_on_kernel(head_size, parts, limits, plan, qs, first, stop, m_in, l_in, acc_in, *refs):
    kv, (m, l, acc, *work) = refs[:parts], refs[parts:]
    m[...] = m_in[...]
    l[...] = l_in[...]
    acc[...] = acc_in[...]
    sweep(head_size, plan, 0, limits, qs, first, stop, [[lambda r=r: r[...]] for r in kv], (m, l, acc), *work)


def rebuilt_kernel(head_size, plan, qs, first, stop, m_in, l_in, acc_in, order, *refs):
    *once, twice, o0, o1, o2, o3, m, l, acc, even, odd, keys, wide = refs
    factor = math.log2(math.e) * head_size ** (-0.5)
    tokens = o0.shape[0]
    heads = qs.shape[1] // CHUNK
    per_block = tokens // CHUNK
    m[...] = m_in[...]
    l[...] = l_in[...]
    acc[...] = acc_in[...]
    kv_parts = [[lambda r=once[i]: r[...], lambda r=once[i + 2]: r[...]] for i in range(2)]
    kv_parts += [[lambda i=i: twice[i], lambda i=i: twice[i + 2]] for i in range(2)]
    sweep(head_size, plan, 4, (ZERO_ROW, COUNT_ROW), qs, first, stop, kv_parts, (m, l, acc), even, odd, keys, wide)
    lanes = lax.broadcasted_iota(jnp.int32, (tokens, 128), 1)
    for block, out in enumerate((o0, o1, o2, o3)):
        extra = jnp.zeros((tokens, 128), jnp.float32)
        for head in range(heads):
            rows = slice(head * CHUNK, (head + 1) * CHUNK)
            chunks = range(block * per_block, (block + 1) * per_block)
            high = jnp.concatenate([m[chunk, rows, :] for chunk in chunks], axis=0)
            total = jnp.concatenate([l[chunk, rows, :] for chunk in chunks], axis=0)
            mixed = jnp.concatenate([acc[chunk, rows, :] for chunk in chunks], axis=0)
            some = total > 0.0
            safe = jnp.where(some, total, 1.0)
            level = jnp.where(some, high * factor + jnp.log2(safe), MASKED_SCORE)
            ordered = (mixed / safe).astype(jnp.bfloat16)
            out[:, head * head_size : (head + 1) * head_size] = lax.dot_general(
                order[block], ordered, (((0,), (0,)), ((), ())), preferred_element_type=jnp.float32
            ).astype(jnp.bfloat16)
            for piece in range(3):
                rounded = level.astype(jnp.bfloat16).astype(jnp.float32)
                extra = jnp.where(lanes == piece * heads + head, rounded, extra)
                level = level - rounded
        out[:, heads * head_size :] = lax.dot_general(
            order[block], extra.astype(jnp.bfloat16), (((0,), (0,)), ((), ())), preferred_element_type=jnp.float32
        ).astype(jnp.bfloat16)


def merge_kernel(head_size, a, b, c, d, out):
    heads = out.shape[1] // head_size
    parts = (a, b, c, d)
    extras = [part[:, heads * head_size :].astype(jnp.float32) for part in parts]
    for head in range(heads):
        cols = slice(head * head_size, (head + 1) * head_size)
        levels = [sum(e[:, p * heads + head : p * heads + head + 1] for p in range(3)) for e in extras]
        top = functools.reduce(jnp.maximum, levels)
        shares = [jnp.exp2(level - top) for level in levels]
        mixed = sum(share * part[:, cols].astype(jnp.float32) for share, part in zip(shares, parts))
        out[:, cols] = (mixed / sum(shares)).astype(jnp.bfloat16)


def normalize_kernel(gain_ref, after_ref, a, b, c, d, out):
    head_size = gain_ref.shape[1]
    keys, values = (
        sum(part[:, low : low + head_size].astype(jnp.float32) for part in (a, b, c, d)) for low in (0, head_size)
    )
    inverse = lax.rsqrt(jnp.mean(keys * keys, axis=-1, keepdims=True) + 1e-05)
    out[:, :head_size] = (keys * inverse * gain_ref[...]).astype(out.dtype)
    out[:, head_size:] = values.astype(out.dtype)


def normalize(terms, key_gain, after):
    vmem = pl.BlockSpec(memory_space=pltpu.VMEM)
    return pl.pallas_call(
        normalize_kernel,
        in_specs=[vmem, pl.BlockSpec(memory_space=pl.ANY)] + [vmem] * 4,
        out_specs=vmem,
        out_shape=jax.ShapeDtypeStruct(terms[0].shape, jnp.bfloat16),
        compiler_params=VMEM,
        name="normalize",
    )(key_gain[None], after, *terms)


def on_device(
    hidden,
    cross_query,
    image_cache,
    features,
    image_proj,
    key_gain,
    out_weight,
    cross_gate,
    image_spans,
    evicted,
    placement,
):
    head_size = key_gain.shape[0]
    tokens, cols = cross_query.shape
    heads = cols // head_size
    patches = features.shape[1]
    half = patches // 2
    seq_pos = lax.axis_index("seq")
    head_pos = lax.axis_index("head")
    y, x, core = seq_pos // 4, (seq_pos // 2) % 2, seq_pos % 2
    head_x, head_z = head_pos // 4, head_pos % 4
    chunks = 4 * tokens // CHUNK
    rows = heads * CHUNK

    sent_part = lax.dynamic_slice_in_dim(features[0], (1 - core) * half, half)
    peer_part = send_seq(sent_part, core=1)
    stale = jnp.any(placement[:, None] == evicted, axis=1).reshape(8, 2)
    both = jnp.any(stale[:, 0] & stale[:, 1])
    use_own = lax.dynamic_index_in_dim(stale, seq_pos // 2, 0, keepdims=False)[0] == (core == 0)
    part_index = jnp.arange(8, dtype=jnp.int32)
    home = head_at(head_x + part_index % 2, head_z + part_index // 2).astype(jnp.int32)

    held = image_cache[0]
    after_one = send_seq(cross_query, y=-1)
    q_blocks = [cross_query, after_one, send_seq(after_one, y=-1), send_seq(cross_query, y=1)]
    held_x = send_seq(held, x=1)

    def rebuild(own_first, after=(), work=None, kv_of=None):
        pick = jnp.where(jnp.arange(2) == 0, own_first.astype(jnp.int32), core).astype(jnp.int32)
        parts = rebuild_parts(features, peer_part, image_proj, home, pick, after)
        if work is None:
            terms, state = sum_over_head(parts), (peer_part,)
        else:
            terms, state = sum_beside(parts, work, kv_of)
        mine = normalize(terms, key_gain, state[-1])
        other = send_seq(mine, x=1)
        pieces = (mine, other, send_seq(mine, core=1), send_seq(other, core=1))
        return pieces if work is None else (pieces, state)

    smem = pl.BlockSpec(memory_space=pltpu.SMEM)
    vmem = pl.BlockSpec(memory_space=pltpu.VMEM)
    order, first_all, stop_all, plan = pl.pallas_call(
        plan_kernel,
        in_specs=[smem] * 3 + [vmem],
        out_specs=[vmem] * 4,
        out_shape=[
            jax.ShapeDtypeStruct((4, tokens, tokens), jnp.bfloat16),
            jax.ShapeDtypeStruct((4 * tokens, head_size), jnp.int32),
            jax.ShapeDtypeStruct((4 * tokens, head_size), jnp.int32),
            jax.ShapeDtypeStruct((PLAN_ROWS, 128), jnp.int32),
        ],
        compiler_params=VMEM,
        name="plan",
    )(seq_pos.reshape(1).astype(jnp.int32), placement, evicted, image_spans.T.reshape(2, 16, tokens))
    state_shapes = [jax.ShapeDtypeStruct((chunks, rows, head_size), jnp.float32)] * 3

    def scratch(keys):
        return [pltpu.VMEM((rows, keys), jnp.float32)] * 2 + [
            pltpu.VMEM((keys, head_size), jnp.bfloat16),
            pltpu.VMEM((keys, 2 * head_size), jnp.bfloat16),
        ]

    def attend_first(*kv):
        return pl.pallas_call(
            functools.partial(begin_kernel, head_size),
            in_specs=[smem] + [vmem] * 9,
            out_specs=[vmem] * 4,
            out_shape=[jax.ShapeDtypeStruct((chunks, rows, head_size), jnp.bfloat16)] + state_shapes,
            scratch_shapes=scratch(patches),
            compiler_params=VMEM,
            name="attend_first",
        )(plan, *q_blocks, order, first_all, stop_all, *kv)

    def attend_more(state, limits, *kv):
        return state[:1] + pl.pallas_call(
            functools.partial(go_on_kernel, head_size, len(kv), limits),
            in_specs=[smem] + [vmem] * (6 + len(kv)),
            out_specs=[vmem] * 3,
            out_shape=state_shapes,
            scratch_shapes=scratch(patches),
            input_output_aliases={4: 0, 5: 1, 6: 2},
            compiler_params=VMEM,
            name="attend_more",
        )(plan, state[0], first_all, stop_all, *state[1:], *kv)

    work = (
        attend_first,
        lambda state, *kv: attend_more(state, (THIRD_ROW, TWO_THIRDS_ROW), *kv),
        lambda state, *kv: attend_more(state, (TWO_THIRDS_ROW, COUNT_ROW), *kv),
    )

    def kv_of(after):
        return held, send_seq(copy_after(held, after), core=1), held_x

    twice = lax.cond(
        both,
        lambda: jnp.stack(rebuild(~use_own, (q_blocks[1], q_blocks[3]))),
        lambda: jnp.zeros((4, half, 2 * head_size), jnp.bfloat16),
    )
    once, state = rebuild(use_own, (twice,), work, kv_of)
    partial_out = pl.pallas_call(
        functools.partial(rebuilt_kernel, head_size),
        in_specs=[smem] + [vmem] * 12,
        out_specs=[vmem] * 4,
        out_shape=[jax.ShapeDtypeStruct((tokens, cols + 128), jnp.bfloat16)] * 4,
        scratch_shapes=[pltpu.VMEM(s.shape, s.dtype) for s in state_shapes] + scratch(patches),
        compiler_params=VMEM,
        name="attend_rebuilt",
    )(plan, state[0], first_all, stop_all, *state[1:], order, *once, twice)
    arrived = [partial_out[0]] + [send_seq(partial_out[dy], y=dy) for dy in (1, 2, 3)]
    context = pl.pallas_call(
        functools.partial(merge_kernel, head_size),
        in_specs=[vmem] * 4,
        out_specs=vmem,
        out_shape=jax.ShapeDtypeStruct((tokens, cols), jnp.bfloat16),
        compiler_params=VMEM,
        name="merge",
    )(*arrived)

    near, far = gather_chips(context)
    target = head_at(head_x + part_index % 2, head_z + part_index // 2)
    offset = 2 * ((target // 2 - y) % 4) + (target % 2 - x) % 2
    source = jnp.zeros(8, jnp.int32)
    for at, place in enumerate((0, 1, 6, 2, 4, 7, 3, 5)):
        source = jnp.where(offset == place, at, source)
    parts = project_parts(
        (near, far, send_seq(near, core=1), send_seq(far, core=1)),
        out_weight,
        source.astype(jnp.int32),
        core.reshape(1).astype(jnp.int32),
    )
    summed_out = sum(term.astype(jnp.float32) for term in sum_over_head(parts))
    return (hidden.astype(jnp.float32) + jnp.tanh(cross_gate[0]) * summed_out).astype(jnp.bfloat16)


def solution(mesh):
    placed = (
        P("head", "seq"),
        P("seq", "head"),
        P("seq", None, "head"),
        P("seq", None, "head"),
        P("head", None),
        P(),
        P("head", "seq"),
        P(),
        P(),
        P(),
        P(),
    )
    return jax.shard_map(
        on_device, mesh=mesh, in_specs=placed, out_specs=P("head", "seq"), check_vma=False
    )
```

```python
import functools
import math

import jax
import jax.numpy as jnp
from jax import lax
from jax.experimental import pallas as pl
from jax.experimental.pallas import tpu as pltpu
from jax.sharding import PartitionSpec as P

MASKED_SCORE = -1e30
CHUNK = 32
COUNT_ROW = 18
ID_ROW = 19
THIRD_ROW = 20
TWO_THIRDS_ROW = 21
ZERO_ROW = 22
PLAN_ROWS = 24
VMEM = pltpu.CompilerParams(vmem_limit_bytes=20 * 1024 * 1024)


def seq_at(y, x, core):
    return (y % 4) * 4 + (x % 2) * 2 + core % 2


def head_at(x, z):
    return (x % 2) * 4 + z % 4


def send_seq(array, y=0, x=0, core=0):
    pairs = [
        (seq_at(a, b, c), seq_at(a + y, b + x, c + core)) for a in range(4) for b in range(2) for c in range(2)
    ]
    return lax.ppermute(array, "seq", pairs)


def send_head(array, x=0, z=0):
    return lax.ppermute(array, "head", [(head_at(a, b), head_at(a + x, b + z)) for a in range(2) for b in range(4)])


def add(*terms):
    return sum(term.astype(jnp.float32) for term in terms).astype(jnp.bfloat16)


def add_kernel(*refs):
    *terms, _, out_ref = refs
    out_ref[...] = sum(term[...].astype(jnp.float32) for term in terms).astype(out_ref.dtype)


def add_after(after, *terms):
    vmem = pl.BlockSpec(memory_space=pltpu.VMEM)
    return pl.pallas_call(
        add_kernel,
        in_specs=[vmem] * len(terms) + [pl.BlockSpec(memory_space=pl.ANY)],
        out_specs=vmem,
        out_shape=jax.ShapeDtypeStruct(terms[0].shape, terms[0].dtype),
        compiler_params=VMEM,
        name="add_after",
    )(*terms, after)


def sum_over_head(parts):
    p00, p01, p10, p11, p20, p21, p30, p31 = parts
    via_x = send_head(p21, x=1)
    down = send_head(p31, z=-1)
    across = send_head(p11, x=1)
    last = send_head(p30, z=-1)
    p20 = add(p20, via_x)
    p01 = add(p01, down)
    up = send_head(p20, z=1)
    side = send_head(p01, x=1)
    p10 = add(p10, across, up)
    ahead = send_head(p10, z=1)
    return p00, last, side, ahead


def sum_beside(parts, work, kv_of):
    p00, p01, p10, p11, p20, p21, p30, p31 = parts
    up = send_head(p20, z=1)
    down = send_head(p21, z=-1)
    across = send_head(p11, z=1)
    last = send_head(p30, z=-1)
    kv = kv_of(p30)
    state = work[0](*kv[:2])
    p10 = add_after(state[-1], p10, up)
    p31 = add_after(state[-1], p31, down)
    held_x, p10, p31 = lax.optimization_barrier((kv[2], p10, p31))
    kv = kv[:2] + (held_x, send_seq(held_x, core=1))
    ahead = send_head(p10, z=1)
    behind = send_head(p31, z=-1)
    state = work[1](state, *kv)
    p01 = add_after(state[-1], p01, across, behind)
    side = send_head(p01, x=1)
    state = work[2](state, *kv)
    return (p00, last, ahead, side), state


def gather_chips(block):
    r30 = send_seq(block, y=1)
    r01 = send_seq(block, x=1)
    r10 = send_seq(block, y=-1)
    r30, r01, r10 = lax.optimization_barrier((r30, r01, r10))
    r20 = send_seq(r30, y=1)
    r31 = send_seq(r30, x=1)
    r11 = send_seq(r01, y=-1)
    r21 = send_seq(r11, y=-1)
    return jnp.stack([block, r01, r30, r10]), jnp.stack([r20, r31, r11, r21])


def rebuild_kernel(order_ref, pick_ref, own_ref, peer_ref, proj0_ref, proj1_ref, *refs):
    *out_refs, rows_ref = refs[-9:]
    step = pl.program_id(0)

    @pl.when(step == 0)
    def _():
        rows_ref[...] = jnp.where(pick_ref[0] > 0, own_ref[0], peer_ref[...])

    products = [
        jnp.dot(rows_ref[...], proj_ref[...], preferred_element_type=jnp.float32).astype(jnp.bfloat16)
        for proj_ref in (proj0_ref, proj1_ref)
    ]
    for at in range(4):

        @pl.when(step == at)
        def _():
            out_refs[2 * at][...] = products[0]
            out_refs[2 * at + 1][...] = products[1]


def rebuild_parts(features, peer_part, proj, order, pick, after):
    count, depth = peer_part.shape
    cols = proj.shape[1] // 8
    return pl.pallas_call(
        rebuild_kernel,
        grid_spec=pltpu.PrefetchScalarGridSpec(
            num_scalar_prefetch=2,
            grid=(4,),
            in_specs=[
                pl.BlockSpec((1, count, depth), lambda i, order, pick: (0, pick[1], 0)),
                pl.BlockSpec((count, depth), lambda i, order, pick: (0, 0)),
                pl.BlockSpec((depth, cols), lambda i, order, pick: (0, order[2 * i])),
                pl.BlockSpec((depth, cols), lambda i, order, pick: (0, order[2 * i + 1])),
            ]
            + [pl.BlockSpec(memory_space=pl.ANY)] * len(after),
            out_specs=[pl.BlockSpec((count, cols), lambda i, order, pick: (0, 0))] * 8,
            scratch_shapes=[pltpu.VMEM((count, depth), jnp.bfloat16)],
        ),
        out_shape=[jax.ShapeDtypeStruct((count, cols), jnp.bfloat16)] * 8,
        compiler_params=VMEM,
        name="rebuild_parts",
    )(order, pick, features, peer_part, proj, proj, *after)


def project_kernel(order_ref, core_ref, own0_ref, own1_ref, other0_ref, other1_ref, weight_ref, *out_refs):
    step = pl.program_id(0)
    even = core_ref[0] == 0
    tokens = own0_ref.shape[1]

    def block(first_ref, second_ref, at):
        return jnp.where(at < 4, first_ref[jnp.minimum(at, 3)], second_ref[jnp.maximum(at - 4, 0)])

    rows = []
    for part in range(2):
        at = order_ref[2 * step + part]
        own, other = block(own0_ref, own1_ref, at), block(other0_ref, other1_ref, at)
        rows += [jnp.where(even, own, other), jnp.where(even, other, own)]
    product = jnp.dot(
        jnp.concatenate(rows, axis=0), weight_ref[...], preferred_element_type=jnp.float32
    ).astype(jnp.bfloat16)
    for at in range(4):

        @pl.when(step == at)
        def _():
            out_refs[2 * at][...] = product[: 2 * tokens]
            out_refs[2 * at + 1][...] = product[2 * tokens :]


def project_parts(blocks, weight, order, core):
    _, tokens, depth = blocks[0].shape
    cols = weight.shape[1]
    return pl.pallas_call(
        project_kernel,
        grid_spec=pltpu.PrefetchScalarGridSpec(
            num_scalar_prefetch=2,
            grid=(4,),
            in_specs=[pl.BlockSpec((4, tokens, depth), lambda i, order, core: (0, 0, 0))] * 4
            + [pl.BlockSpec((depth, cols), lambda i, order, core: (0, 0))],
            out_specs=[pl.BlockSpec((2 * tokens, cols), lambda i, order, core: (0, 0))] * 8,
        ),
        out_shape=[jax.ShapeDtypeStruct((2 * tokens, cols), jnp.bfloat16)] * 8,
        compiler_params=VMEM,
        name="project_parts",
    )(order, core, *blocks, weight)


def plan_kernel(pos_ref, placement_ref, evicted_ref, spans_ref, order_ref, first_ref, stop_ref, plan_ref):
    seq_pos = pos_ref[0]
    y, x, core = seq_pos // 4, (seq_pos // 2) % 2, seq_pos % 2
    tokens = spans_ref.shape[2]
    chips = (seq_pos // 2, seq_at(y, x + 1, 0) // 2)

    def stale(slot):
        image = placement_ref[slot]
        return (image == evicted_ref[0]) | (image == evicted_ref[1])

    entries = []
    for chip in chips:
        for slot in (2 * chip + core, 2 * chip + 1 - core):
            entries.append((placement_ref[slot], ~stale(slot)))
    once, twice = [], []
    for chip in chips:
        low, high = stale(2 * chip), stale(2 * chip + 1)
        once.append((jnp.where(low, placement_ref[2 * chip], placement_ref[2 * chip + 1]), low | high))
        twice.append((placement_ref[2 * chip + 1], low & high))
    entries += once + twice
    slot_lane = lax.broadcasted_iota(jnp.int32, (CHUNK, 128), 1)
    ids = jnp.full((CHUNK, 128), -1, jnp.int32)
    for at, (image, live) in enumerate(entries):
        ids = jnp.where(slot_lane == at, jnp.where(live, image, -1), ids)

    up = lax.broadcasted_iota(jnp.int32, (tokens, tokens), 0)
    along = lax.broadcasted_iota(jnp.int32, (tokens, tokens), 1)
    wanted = []
    for dy in range(4):
        block = seq_at(y + dy, x, core)
        first = jnp.broadcast_to(spans_ref[0, pl.ds(block, 1), :].astype(jnp.float32), (tokens, tokens))
        stop = jnp.broadcast_to(spans_ref[1, pl.ds(block, 1), :].astype(jnp.float32), (tokens, tokens))
        down = jnp.sum(jnp.where(up == along, first, 0.0), axis=1, keepdims=True)
        earlier = (down < first) | ((down == first) & (up < along))
        rank = jnp.sum(jnp.where(earlier, 1.0, 0.0), axis=0, keepdims=True).astype(jnp.int32)
        order = jnp.where(up == rank, 1.0, 0.0)
        order_ref[dy] = order.astype(jnp.bfloat16)
        first = jnp.broadcast_to(jnp.sum(order * first, axis=1, keepdims=True), (tokens, 128)).astype(jnp.int32)
        stop = jnp.broadcast_to(jnp.sum(order * stop, axis=1, keepdims=True), (tokens, 128)).astype(jnp.int32)
        first_ref[dy * tokens : (dy + 1) * tokens, :] = first
        stop_ref[dy * tokens : (dy + 1) * tokens, :] = stop
        for part in range(tokens // CHUNK):
            rows = slice(part * CHUNK, (part + 1) * CHUNK)
            seen = (first[rows] <= ids) & (ids < stop[rows])
            wanted.append(jnp.max(jnp.where(seen, 1, 0), axis=0, keepdims=True))
    places, total = [], jnp.zeros((1, 128), jnp.int32)
    for want in wanted:
        places.append(total)
        total = total + want
    for place in range(COUNT_ROW):
        row = jnp.zeros((1, 128), jnp.int32)
        for chunk, (want, at) in enumerate(zip(wanted, places)):
            row = jnp.where((want > 0) & (at == place), chunk, row)
        plan_ref[place : place + 1, :] = row
    plan_ref[COUNT_ROW : COUNT_ROW + 1, :] = total
    plan_ref[ID_ROW : ID_ROW + 1, :] = ids[:1]
    plan_ref[ZERO_ROW:, :] = jnp.zeros((PLAN_ROWS - ZERO_ROW, 128), jnp.int32)
    lane = slot_lane[:1]
    counts = [jnp.sum(jnp.where(lane == at, total, 0), axis=1, keepdims=True) for at in range(4)]
    share = ((sum(counts) + 2) * 21846) >> 16
    third, two_thirds = jnp.zeros((1, 128), jnp.int32), jnp.zeros((1, 128), jnp.int32)
    before = jnp.zeros((1, 1), jnp.int32)
    for at, count in enumerate(counts):
        if at < 2:
            third = jnp.where(lane == at, jnp.clip(share - before, 0, count), third)
        two_thirds = jnp.where(lane == at, jnp.clip(2 * share - before, 0, count), two_thirds)
        before = before + count
    plan_ref[THIRD_ROW : THIRD_ROW + 1, :] = third
    plan_ref[TWO_THIRDS_ROW : TWO_THIRDS_ROW + 1, :] = two_thirds


def sweep(head_size, plan_ref, low, limits, q_ref, first_ref, stop_ref, kv_parts, state, even, odd, keys, wide):
    factor = math.log2(math.e) * head_size ** (-0.5)
    heads = q_ref.shape[1] // CHUNK
    m_ref, l_ref, acc_ref = state

    for slot, part in enumerate(kv_parts, low):
        begin, end = (plan_ref[row, slot] for row in limits)

        def score(place, into):
            into[...] = lax.dot_general(
                q_ref[plan_ref[place, slot]],
                keys[...],
                (((1,), (1,)), ((), ())),
                preferred_element_type=jnp.float32,
            )

        def take(place, scores_ref):
            chunk = plan_ref[place, slot]
            image = jnp.where(place < end, plan_ref[ID_ROW, slot], -1)
            scores = scores_ref[...]
            here = jnp.broadcast_to(jnp.max(scores, axis=1, keepdims=True), (scores.shape[0], head_size))
            weights = jnp.exp2((scores - here[:, :1]) * factor)
            both = jnp.dot(weights.astype(jnp.bfloat16), wide[...], preferred_element_type=jnp.float32)
            mixed, total = both[:, :head_size], both[:, head_size:]
            tokens = pl.ds(pl.multiple_of(chunk * CHUNK, CHUNK), CHUNK)
            seen = (first_ref[tokens, :] <= image) & (image < stop_ref[tokens, :])
            seen = jnp.concatenate([seen.astype(jnp.int32)] * heads, axis=0) > 0
            before = m_ref[chunk]
            after = jnp.where(seen, jnp.maximum(before, here), before)
            keep = jnp.exp2((before - after) * factor)
            gain = jnp.where(seen, jnp.exp2((here - after) * factor), 0.0)
            m_ref[chunk] = after
            l_ref[chunk] = l_ref[chunk] * keep + gain * total
            acc_ref[chunk] = acc_ref[chunk] * keep + gain * mixed

        @pl.when(end > begin)
        def _():
            at = 0
            for rows_of in part:
                block = rows_of()
                rows = slice(at, at + block.shape[0])
                keys[rows, :] = block[:, :head_size]
                wide[rows, :head_size] = block[:, head_size:]
                at += block.shape[0]
            wide[:, head_size:] = jnp.ones_like(wide[:, head_size:])
            score(begin, even)

            def body(at, carry):
                place = begin + 2 * at
                score(place + 1, odd)
                take(place, even)
                score(place + 2, even)
                take(place + 1, odd)
                return carry

            lax.fori_loop(0, (end - begin + 1) // 2, body, 0)


def copy_kernel(array_ref, after_ref, out_ref):
    out_ref[...] = array_ref[...]


def copy_after(array, after):
    vmem = pl.BlockSpec(memory_space=pltpu.VMEM)
    return pl.pallas_call(
        copy_kernel,
        in_specs=[vmem, pl.BlockSpec(memory_space=pl.ANY)],
        out_specs=vmem,
        out_shape=jax.ShapeDtypeStruct(array.shape, array.dtype),
        compiler_params=VMEM,
        name="copy_after",
    )(array, after)


def begin_kernel(head_size, plan, q0, q1, q2, q3, order, first, stop, a, b, qs, m, l, acc, *work):
    heads = q0.shape[1] // head_size
    per_block = q0.shape[0] // CHUNK
    for block, q_ref in enumerate((q0, q1, q2, q3)):
        ordered = jnp.dot(order[block], q_ref[...], preferred_element_type=jnp.float32).astype(jnp.bfloat16)
        for part in range(per_block):
            for head in range(heads):
                qs[block * per_block + part, head * CHUNK : (head + 1) * CHUNK, :] = ordered[
                    part * CHUNK : (part + 1) * CHUNK, head * head_size : (head + 1) * head_size
                ]
    m[...] = jnp.full_like(m, MASKED_SCORE)
    l[...] = jnp.zeros_like(l)
    acc[...] = jnp.zeros_like(acc)
    kv_parts = [[lambda r=r: r[...]] for r in (a, b)]
    sweep(head_size, plan, 0, (ZERO_ROW, THIRD_ROW), qs, first, stop, kv_parts, (m, l, acc), *work)


def go_on_kernel(head_size, parts, limits, plan, qs, first, stop, m_in, l_in, acc_in, *refs):
    kv, (m, l, acc, *work) = refs[:parts], refs[parts:]
    m[...] = m_in[...]
    l[...] = l_in[...]
    acc[...] = acc_in[...]
    sweep(head_size, plan, 0, limits, qs, first, stop, [[lambda r=r: r[...]] for r in kv], (m, l, acc), *work)


def rebuilt_kernel(head_size, plan, qs, first, stop, m_in, l_in, acc_in, order, *refs):
    *once, twice, o0, o1, o2, o3, m, l, acc, even, odd, keys, wide = refs
    factor = math.log2(math.e) * head_size ** (-0.5)
    tokens = o0.shape[0]
    heads = qs.shape[1] // CHUNK
    per_block = tokens // CHUNK
    m[...] = m_in[...]
    l[...] = l_in[...]
    acc[...] = acc_in[...]
    kv_parts = [[lambda r=once[i]: r[...], lambda r=once[i + 2]: r[...]] for i in range(2)]
    kv_parts += [[lambda i=i: twice[i], lambda i=i: twice[i + 2]] for i in range(2)]
    sweep(head_size, plan, 4, (ZERO_ROW, COUNT_ROW), qs, first, stop, kv_parts, (m, l, acc), even, odd, keys, wide)
    lanes = lax.broadcasted_iota(jnp.int32, (tokens, 128), 1)
    for block, out in enumerate((o0, o1, o2, o3)):
        extra = jnp.zeros((tokens, 128), jnp.float32)
        for head in range(heads):
            rows = slice(head * CHUNK, (head + 1) * CHUNK)
            chunks = range(block * per_block, (block + 1) * per_block)
            high = jnp.concatenate([m[chunk, rows, :] for chunk in chunks], axis=0)
            total = jnp.concatenate([l[chunk, rows, :] for chunk in chunks], axis=0)
            mixed = jnp.concatenate([acc[chunk, rows, :] for chunk in chunks], axis=0)
            some = total > 0.0
            safe = jnp.where(some, total, 1.0)
            level = jnp.where(some, high * factor + jnp.log2(safe), MASKED_SCORE)
            ordered = (mixed / safe).astype(jnp.bfloat16)
            out[:, head * head_size : (head + 1) * head_size] = lax.dot_general(
                order[block], ordered, (((0,), (0,)), ((), ())), preferred_element_type=jnp.float32
            ).astype(jnp.bfloat16)
            for piece in range(3):
                rounded = level.astype(jnp.bfloat16).astype(jnp.float32)
                extra = jnp.where(lanes == piece * heads + head, rounded, extra)
                level = level - rounded
        out[:, heads * head_size :] = lax.dot_general(
            order[block], extra.astype(jnp.bfloat16), (((0,), (0,)), ((), ())), preferred_element_type=jnp.float32
        ).astype(jnp.bfloat16)


def merge_kernel(head_size, a, b, c, d, out):
    heads = out.shape[1] // head_size
    parts = (a, b, c, d)
    extras = [part[:, heads * head_size :].astype(jnp.float32) for part in parts]
    for head in range(heads):
        cols = slice(head * head_size, (head + 1) * head_size)
        levels = [sum(e[:, p * heads + head : p * heads + head + 1] for p in range(3)) for e in extras]
        top = functools.reduce(jnp.maximum, levels)
        shares = [jnp.exp2(level - top) for level in levels]
        mixed = sum(share * part[:, cols].astype(jnp.float32) for share, part in zip(shares, parts))
        out[:, cols] = (mixed / sum(shares)).astype(jnp.bfloat16)


def normalize_kernel(gain_ref, after_ref, a, b, c, d, out):
    head_size = gain_ref.shape[1]
    keys, values = (
        sum(part[:, low : low + head_size].astype(jnp.float32) for part in (a, b, c, d)) for low in (0, head_size)
    )
    inverse = lax.rsqrt(jnp.mean(keys * keys, axis=-1, keepdims=True) + 1e-05)
    out[:, :head_size] = (keys * inverse * gain_ref[...]).astype(out.dtype)
    out[:, head_size:] = values.astype(out.dtype)


def normalize(terms, key_gain, after):
    vmem = pl.BlockSpec(memory_space=pltpu.VMEM)
    return pl.pallas_call(
        normalize_kernel,
        in_specs=[vmem, pl.BlockSpec(memory_space=pl.ANY)] + [vmem] * 4,
        out_specs=vmem,
        out_shape=jax.ShapeDtypeStruct(terms[0].shape, jnp.bfloat16),
        compiler_params=VMEM,
        name="normalize",
    )(key_gain[None], after, *terms)


def on_device(
    hidden,
    cross_query,
    image_cache,
    features,
    image_proj,
    key_gain,
    out_weight,
    cross_gate,
    image_spans,
    evicted,
    placement,
):
    head_size = key_gain.shape[0]
    tokens, cols = cross_query.shape
    heads = cols // head_size
    patches = features.shape[1]
    half = patches // 2
    seq_pos = lax.axis_index("seq")
    head_pos = lax.axis_index("head")
    y, x, core = seq_pos // 4, (seq_pos // 2) % 2, seq_pos % 2
    head_x, head_z = head_pos // 4, head_pos % 4
    chunks = 4 * tokens // CHUNK
    rows = heads * CHUNK

    sent_part = lax.dynamic_slice_in_dim(features[0], (1 - core) * half, half)
    peer_part = send_seq(sent_part, core=1)
    stale = jnp.any(placement[:, None] == evicted, axis=1).reshape(8, 2)
    both = jnp.any(stale[:, 0] & stale[:, 1])
    use_own = lax.dynamic_index_in_dim(stale, seq_pos // 2, 0, keepdims=False)[0] == (core == 0)
    part_index = jnp.arange(8, dtype=jnp.int32)
    home = head_at(head_x + part_index % 2, head_z + part_index // 2).astype(jnp.int32)

    held = image_cache[0]
    after_one = send_seq(cross_query, y=-1)
    q_blocks = [cross_query, after_one, send_seq(after_one, y=-1), send_seq(cross_query, y=1)]
    held_x = send_seq(held, x=1)

    def rebuild(own_first, after=(), work=None, kv_of=None):
        pick = jnp.where(jnp.arange(2) == 0, own_first.astype(jnp.int32), core).astype(jnp.int32)
        parts = rebuild_parts(features, peer_part, image_proj, home, pick, after)
        if work is None:
            terms, state = sum_over_head(parts), (peer_part,)
        else:
            terms, state = sum_beside(parts, work, kv_of)
        mine = normalize(terms, key_gain, state[-1])
        other = send_seq(mine, x=1)
        pieces = (mine, other, send_seq(mine, core=1), send_seq(other, core=1))
        return pieces if work is None else (pieces, state)

    smem = pl.BlockSpec(memory_space=pltpu.SMEM)
    vmem = pl.BlockSpec(memory_space=pltpu.VMEM)
    order, first_all, stop_all, plan = pl.pallas_call(
        plan_kernel,
        in_specs=[smem] * 3 + [vmem],
        out_specs=[vmem] * 4,
        out_shape=[
            jax.ShapeDtypeStruct((4, tokens, tokens), jnp.bfloat16),
            jax.ShapeDtypeStruct((4 * tokens, head_size), jnp.int32),
            jax.ShapeDtypeStruct((4 * tokens, head_size), jnp.int32),
            jax.ShapeDtypeStruct((PLAN_ROWS, 128), jnp.int32),
        ],
        compiler_params=VMEM,
        name="plan",
    )(seq_pos.reshape(1).astype(jnp.int32), placement, evicted, image_spans.T.reshape(2, 16, tokens))
    state_shapes = [jax.ShapeDtypeStruct((chunks, rows, head_size), jnp.float32)] * 3

    def scratch(keys):
        return [pltpu.VMEM((rows, keys), jnp.float32)] * 2 + [
            pltpu.VMEM((keys, head_size), jnp.bfloat16),
            pltpu.VMEM((keys, 2 * head_size), jnp.bfloat16),
        ]

    def attend_first(*kv):
        return pl.pallas_call(
            functools.partial(begin_kernel, head_size),
            in_specs=[smem] + [vmem] * 9,
            out_specs=[vmem] * 4,
            out_shape=[jax.ShapeDtypeStruct((chunks, rows, head_size), jnp.bfloat16)] + state_shapes,
            scratch_shapes=scratch(patches),
            compiler_params=VMEM,
            name="attend_first",
        )(plan, *q_blocks, order, first_all, stop_all, *kv)

    def attend_more(state, limits, *kv):
        return state[:1] + pl.pallas_call(
            functools.partial(go_on_kernel, head_size, len(kv), limits),
            in_specs=[smem] + [vmem] * (6 + len(kv)),
            out_specs=[vmem] * 3,
            out_shape=state_shapes,
            scratch_shapes=scratch(patches),
            input_output_aliases={4: 0, 5: 1, 6: 2},
            compiler_params=VMEM,
            name="attend_more",
        )(plan, state[0], first_all, stop_all, *state[1:], *kv)

    work = (
        attend_first,
        lambda state, *kv: attend_more(state, (THIRD_ROW, TWO_THIRDS_ROW), *kv),
        lambda state, *kv: attend_more(state, (TWO_THIRDS_ROW, COUNT_ROW), *kv),
    )

    def kv_of(after):
        return held, send_seq(copy_after(held, after), core=1), held_x

    twice = lax.cond(
        both,
        lambda: jnp.stack(rebuild(~use_own, (q_blocks[1], q_blocks[3]))),
        lambda: jnp.zeros((4, half, 2 * head_size), jnp.bfloat16),
    )
    once, state = rebuild(use_own, (twice,), work, kv_of)
    partial_out = pl.pallas_call(
        functools.partial(rebuilt_kernel, head_size),
        in_specs=[smem] + [vmem] * 12,
        out_specs=[vmem] * 4,
        out_shape=[jax.ShapeDtypeStruct((tokens, cols + 128), jnp.bfloat16)] * 4,
        scratch_shapes=[pltpu.VMEM(s.shape, s.dtype) for s in state_shapes] + scratch(patches),
        compiler_params=VMEM,
        name="attend_rebuilt",
    )(plan, state[0], first_all, stop_all, *state[1:], order, *once, twice)
    arrived = [partial_out[0]] + [send_seq(partial_out[dy], y=dy) for dy in (1, 2, 3)]
    context = pl.pallas_call(
        functools.partial(merge_kernel, head_size),
        in_specs=[vmem] * 4,
        out_specs=vmem,
        out_shape=jax.ShapeDtypeStruct((tokens, cols), jnp.bfloat16),
        compiler_params=VMEM,
        name="merge",
    )(*arrived)

    near, far = gather_chips(context)
    target = head_at(head_x + part_index % 2, head_z + part_index // 2)
    offset = 2 * ((target // 2 - y) % 4) + (target % 2 - x) % 2
    source = jnp.zeros(8, jnp.int32)
    for at, place in enumerate((0, 1, 6, 2, 4, 7, 3, 5)):
        source = jnp.where(offset == place, at, source)
    parts = project_parts(
        (near, far, send_seq(near, core=1), send_seq(far, core=1)),
        out_weight,
        source.astype(jnp.int32),
        core.reshape(1).astype(jnp.int32),
    )
    summed_out = sum(term.astype(jnp.float32) for term in sum_over_head(parts))
    return (hidden.astype(jnp.float32) + jnp.tanh(cross_gate[0]) * summed_out).astype(jnp.bfloat16)


def solution(mesh):
    placed = (
        P("head", "seq"),
        P("seq", "head"),
        P("seq", None, "head"),
        P("seq", None, "head"),
        P("head", None),
        P(),
        P("head", "seq"),
        P(),
        P(),
        P(),
        P(),
    )
    return jax.shard_map(
        on_device, mesh=mesh, in_specs=placed, out_specs=P("head", "seq"), check_vma=False
    )
```
